256 devices in a mesh: seq: 16 (over x, y), tp: 8 (over z), rep: 2 (over core).
Axes of the slice: x: 4, y: 4, z: 8, core: 2. Of those that a mesh axis runs over, the one named last changes fastest.
Arguments:
- light_query: bfloat16 [32768, 8192], P(('seq', 'rep'), 'tp'), may hold values from -6 to 6
- light_key: bfloat16 [32768, 8192], P(('seq', 'rep'), 'tp'), may hold values from -6 to 6
- light_value: bfloat16 [32768, 8192], P(('seq', 'rep'), 'tp'), may hold values from -6 to 6
- log_decay: float32 [32768, 64], P(('seq', 'rep'), 'tp'), may hold values from -0.8 to 0
- prompt_pages: int32 [4], replicated, may hold values from 1 to 64, 128 in all
- norm_gain: float32 [8192], P('tp'), may hold values from 0.5 to 1.5
- cache_keys: bfloat16 [32768, 1024], P(('seq', 'rep'), 'tp'), may hold values from -6 to 6
- cache_values: bfloat16 [32768, 1024], P(('seq', 'rep'), 'tp'), may hold values from -6 to 6
- step_query: bfloat16 [2, 4, 4, 8192], P('rep', None, None, 'tp'), may hold values from -6 to 6
- step_key: bfloat16 [2, 4, 4, 8192], P('rep', None, None, 'tp'), may hold values from -6 to 6
- step_value: bfloat16 [2, 4, 4, 8192], P('rep', None, None, 'tp'), may hold values from -6 to 6
- step_decay: float32 [2, 4, 4, 64], P('rep', None, None, 'tp'), may hold values from -3 to -0.2
- soft_query: bfloat16 [2, 4, 4, 8192], P('rep', None, None, 'tp'), may hold values from -256 to 256
- soft_key: bfloat16 [2, 4, 4, 1024], P('rep', None, None, 'tp'), may hold values from -15 to 15
- soft_value: bfloat16 [2, 4, 4, 1024], P('rep', None, None, 'tp'), may hold values from -6 to 6
Outputs:
- light_out: bfloat16 [32768, 8192], P(('seq', 'rep'), 'tp')
- light_decode: bfloat16 [2, 4, 4, 64, 128], P('rep', None, None, 'tp', 'seq')
- soft_decode: bfloat16 [2, 4, 4, 8192], P('rep', None, None, 'tp')
The draws below stay inside these ranges and needn't reach their ends.
Inputs may be any that keep to these rules, and one draw needn't show every extreme that they name: `prompt_pages`: the prompts are laid end to end in order and fill all 128 pages; the longest has exactly 64 pages.
All inputs are finite; a program needn't handle non-finite values.
Results may differ from the reference program's by a relative error of at most 0.014.
Values may be sent and summed in bfloat16 or wider, within the bound.
A program may use at most 128 MiB of HBM per device.

```python
import math
import jax
import jax.numpy as jnp
import numpy as np
from jax import lax

QUERY_HEADS = 64
DH = 128
KVH = 8
PAGE = 256
BLK = 512
DOCS = 4
STEPS = 4
TOK_DEV = 1024
PROMPT_TOKENS = 32768
PAGES = 128
SAMPLES = 2


def draw_log_decay(key, part):
    key = jax.random.fold_in(key, 11)
    random_subkeys = jax.random.split(key, 7)
    fast_share = 0.5
    fast_heads = jax.random.uniform(random_subkeys[0], (QUERY_HEADS,)) < fast_share
    fast_rate = jnp.exp(jax.random.uniform(random_subkeys[1], (QUERY_HEADS,), minval=math.log(1.0 / 50.0), maxval=math.log(1.0 / 30.0)))
    slow_rate = jax.random.uniform(random_subkeys[2], (QUERY_HEADS,), minval=0.05, maxval=0.3) / PROMPT_TOKENS
    baseline_rate = jnp.where(fast_heads, fast_rate, slow_rate)
    processor_factor = jnp.exp(jax.random.uniform(random_subkeys[3], (PROMPT_TOKENS // TOK_DEV, 1), minval=-math.log(2.0), maxval=math.log(2.0)))
    processor_factor = jnp.repeat(processor_factor, TOK_DEV, axis=0)
    jaggedness = jax.random.uniform(random_subkeys[4], (PROMPT_TOKENS, QUERY_HEADS), minval=0.5, maxval=1.5)
    spike_rows = jax.random.randint(random_subkeys[5], (2,), 0, PROMPT_TOKENS)
    spike_mask = jnp.any(jnp.arange(PROMPT_TOKENS)[:, None] == spike_rows[None, :], axis=1)
    spike_loss = jax.random.uniform(random_subkeys[6], (PROMPT_TOKENS, QUERY_HEADS), minval=0.2, maxval=0.5)
    spike_term = jnp.where(spike_mask[:, None], jnp.log(1.0 - spike_loss), 0.0)
    return (spike_term - baseline_rate[None, :] * processor_factor * jaggedness).astype(jnp.float32)


def draw_soft_query(key, part):
    key = jax.random.fold_in(key, 12)
    first_key = jax.random.fold_in(key, 0)
    values = jnp.clip(jax.random.normal(first_key, (SAMPLES, DOCS, STEPS, QUERY_HEADS, DH)), -4.0, 4.0)
    return values.reshape(SAMPLES, DOCS, STEPS, QUERY_HEADS * DH).astype(jnp.bfloat16)


def block_scale(stream_key, shape, cuts, least, largest):
    gain = 1.0
    for position, blocks in cuts:
        steps = jax.random.uniform(jax.random.fold_in(jax.random.fold_in(stream_key, 6), position), (blocks,), jnp.float32, least / len(cuts), largest / len(cuts))
        gain = gain * jnp.repeat(jnp.exp(steps), shape[position] // blocks).reshape((-1,) + (1,) * (len(shape) - 1 - position))
    return gain


def profile(amount, total, most, slope):
    loads = [(1 << 20) // math.isqrt(grade ** slope) + 1 for grade in range(2, amount + 1)]
    rest, given = total - most - (amount - 1), [1] * (amount - 1)
    while rest > 0:
        movable = [i for i in range(amount - 1) if given[i] < most]
        pool, budget = sum([loads[i] for i in movable]), rest
        for i in movable:
            more = min(most - given[i], max(1, budget * loads[i] // pool), rest)
            given[i] = given[i] + more
            rest = rest - more
    return np.array([most] + given)


def ragged_sizes(own_key, count, total, limit, slope):
    if count == 2:
        one = jax.random.randint(own_key, (), max(1, total - limit), min(limit, total - 1) + 1)
        return jnp.stack([one, total - one])
    lengths = jnp.asarray(profile(count, total, limit, slope), jnp.int32)
    pairs = (count - 1) // 2
    giver, sink = lengths[1:1 + 2 * pairs:2], lengths[2:2 + 2 * pairs:2]
    room = jnp.minimum(giver - 1, limit - sink)
    moved = jax.random.randint(jax.random.fold_in(own_key, 1), (pairs,), 0, 1 << 20) % (room + 1)
    lengths = lengths.at[1:1 + 2 * pairs:2].set(giver - moved).at[2:2 + 2 * pairs:2].set(sink + moved)
    return lengths[jax.random.permutation(jax.random.fold_in(own_key, 2), count)]


def normal_values(stream_key, extent, scale, bound, pieces=(), held_as=jnp.bfloat16):
    loudness = block_scale(stream_key, extent, pieces, -0.22, 0.18) if pieces else 1.0
    array = jax.random.normal(stream_key, extent, jnp.float32) * scale * loudness
    return jnp.minimum(jnp.maximum(array, -bound), bound).astype(held_as)


def setup_inputs(seed: int = 0) -> dict:
    keys = jax.random.split(jax.random.key(seed), 16)
    return {
        "light_query": normal_values(keys[0], (PROMPT_TOKENS, QUERY_HEADS * DH), 1.0, 6.0, ((0, 32), (1, 8))),
        "light_key": normal_values(keys[1], (PROMPT_TOKENS, QUERY_HEADS * DH), 1.0, 6.0, ((0, 32), (1, 8))),
        "light_value": normal_values(keys[2], (PROMPT_TOKENS, QUERY_HEADS * DH), 1.0, 6.0, ((0, 32), (1, 8))),
        "log_decay": draw_log_decay(jax.random.fold_in(keys[15], 71), 0),
        "prompt_pages": ragged_sizes(keys[4], DOCS, PAGES, PAGES // 2, 2).astype(jnp.int32),
        "norm_gain": jnp.clip(1.0 + 0.1 * jax.random.normal(keys[5], (QUERY_HEADS * DH,), jnp.float32), 0.5, 1.5),
        "cache_keys": normal_values(keys[6], (PROMPT_TOKENS, KVH * DH), 1.0, 6.0, ((0, 32), (1, 8))),
        "cache_values": normal_values(keys[7], (PROMPT_TOKENS, KVH * DH), 1.0, 6.0, ((0, 32), (1, 8))),
        "step_query": normal_values(keys[8], (SAMPLES, DOCS, STEPS, QUERY_HEADS * DH), 1.0, 6.0, ((0, 2), (3, 8))),
        "step_key": normal_values(keys[9], (SAMPLES, DOCS, STEPS, QUERY_HEADS * DH), 1.0, 6.0, ((0, 2), (3, 8))),
        "step_value": normal_values(keys[10], (SAMPLES, DOCS, STEPS, QUERY_HEADS * DH), 1.0, 6.0, ((0, 2), (3, 8))),
        "step_decay": jnp.clip(-3.0 + 2.8 * jax.random.uniform(keys[11], (SAMPLES, DOCS, STEPS, QUERY_HEADS), jnp.float32) ** block_scale(keys[11], (SAMPLES, DOCS, STEPS, QUERY_HEADS), ((0, 2), (3, 8)), -0.2, 0.2), -3.0, -0.2),
        "soft_query": draw_soft_query(jax.random.fold_in(keys[15], 71), 0),
        "soft_key": normal_values(keys[13], (SAMPLES, DOCS, STEPS, KVH * DH), 2.5, 15.0, ((0, 2), (3, 8))),
        "soft_value": normal_values(keys[14], (SAMPLES, DOCS, STEPS, KVH * DH), 1.0, 6.0, ((0, 2), (3, 8))),
    }


norm_eps = 1e-06
mask_low = -1e+30
highest = lax.Precision.HIGHEST

def rounded(values):
    return lax.optimization_barrier(values.astype(jnp.bfloat16)).astype(jnp.float32)

def token_docs(prompt_pages, positions):
    page_ends = (PAGE * jnp.cumsum(prompt_pages)).astype(jnp.int32)
    return lax.optimization_barrier(jnp.sum((positions[:, None] >= page_ends[None, :]).astype(jnp.int32), axis=1)).astype(jnp.int32)

def reference(light_query, light_key, light_value, log_decay, prompt_pages, norm_gain, cache_keys, cache_values, step_query, step_key, step_value, step_decay, soft_query, soft_key, soft_value):
    page_ends = (PAGE * jnp.cumsum(prompt_pages)).astype(jnp.int32)
    positions = jnp.arange(PROMPT_TOKENS, dtype=jnp.int32)
    doc_ids = token_docs(prompt_pages, positions)
    block_count = PROMPT_TOKENS // BLK
    row_order = jnp.arange(BLK, dtype=jnp.int32)
    page_last = (jnp.arange(BLK // PAGE, dtype=jnp.int32) + 1) * PAGE - 1

    def block_step(carry, inputs):
        running, final_states = carry
        q_block, k_block, v_block, g_block, doc_block, previous, begin = inputs
        q_wide = q_block.astype(jnp.float32)
        k_wide = k_block.astype(jnp.float32)
        v_wide = v_block.astype(jnp.float32)
        cumulative = jnp.cumsum(g_block, axis=0)
        causal = (row_order[:, None] >= row_order[None, :]) & (doc_block[:, None] == doc_block[None, :])
        spread = cumulative.T[:, :, None] - cumulative.T[:, None, :]
        decay_grid = jnp.where(causal[None], jnp.exp(jnp.minimum(spread, 0.0)), 0.0)
        scores = jnp.einsum('thd,shd->hts', q_wide, k_wide, precision=highest)
        weights_grid = rounded(scores * decay_grid)
        intra_out = jnp.einsum('hts,shd->thd', weights_grid, v_wide, precision=highest)
        weight = jnp.exp(cumulative) * (doc_block == previous).astype(jnp.float32)[:, None]
        inter_out = jnp.einsum('thd,hde->the', q_wide * weight[:, :, None], running, precision=highest)
        cumulative_end = cumulative[PAGE - 1::PAGE]
        doc_end = doc_block[PAGE - 1::PAGE]
        weight_end = weight[PAGE - 1::PAGE]
        page_mask = (row_order[None, :] <= page_last[:, None]) & (doc_block[None, :] == doc_end[:, None])
        factor = jnp.where(page_mask[:, :, None], jnp.exp(jnp.minimum(cumulative_end[:, None, :] - cumulative[None, :, :], 0.0)), 0.0)
        decayed = rounded(k_wide[None] * factor[:, :, :, None])
        states = weight_end[:, :, None, None] * running[None] + jnp.einsum('eshd,shf->ehdf', decayed, v_wide, precision=highest)
        owner_map = (page_ends[:, None] == (begin + page_last + 1)[None, :]).astype(jnp.float32)
        final_states = final_states + jnp.einsum('pe,ehdf->phdf', owner_map, states, precision=highest)
        return ((states[-1], final_states), intra_out + inter_out)
    previous_docs = jnp.concatenate([doc_ids[:1], doc_ids[BLK - 1::BLK][:-1]])
    inputs = (light_query.reshape(block_count, BLK, QUERY_HEADS, DH), light_key.reshape(block_count, BLK, QUERY_HEADS, DH), light_value.reshape(block_count, BLK, QUERY_HEADS, DH), log_decay.reshape(block_count, BLK, QUERY_HEADS), doc_ids.reshape(block_count, BLK), previous_docs, jnp.arange(block_count, dtype=jnp.int32) * BLK)
    start_carry = (jnp.zeros((QUERY_HEADS, DH, DH), jnp.float32), jnp.zeros((DOCS, QUERY_HEADS, DH, DH), jnp.float32))
    (running, final_states), outputs = lax.scan(block_step, start_carry, inputs)
    mixed = outputs.reshape(PROMPT_TOKENS, QUERY_HEADS, DH)
    light_out = (mixed.reshape(PROMPT_TOKENS, QUERY_HEADS * DH) * lax.rsqrt(lax.optimization_barrier(jnp.mean(mixed * mixed, axis=(1, 2))) + norm_eps)[:, None] * norm_gain[None, :]).astype(jnp.bfloat16)
    running = jnp.broadcast_to(final_states[None], (SAMPLES, DOCS, QUERY_HEADS, DH, DH))
    step_q = step_query.reshape(SAMPLES, DOCS, STEPS, QUERY_HEADS, DH).astype(jnp.float32)
    step_k = step_key.reshape(SAMPLES, DOCS, STEPS, QUERY_HEADS, DH).astype(jnp.float32)
    step_v = step_value.reshape(SAMPLES, DOCS, STEPS, QUERY_HEADS, DH).astype(jnp.float32)
    results = []
    for step_id in range(STEPS):
        running = jnp.exp(step_decay[:, :, step_id, :])[..., None, None] * running + step_k[:, :, step_id, :, :, None] * step_v[:, :, step_id, :, None, :]
        results.append(jnp.einsum('rphd,rphdf->rphf', step_q[:, :, step_id], running, precision=highest))
    decoded = jnp.stack(results, axis=2)
    light_decode = (decoded * lax.rsqrt(lax.optimization_barrier(jnp.mean(decoded * decoded, axis=(3, 4))) + norm_eps)[..., None, None] * norm_gain.reshape(QUERY_HEADS, DH)).astype(jnp.bfloat16)
    group = QUERY_HEADS // KVH
    score_scale = DH ** (-0.5)
    queries_all = soft_query.reshape(SAMPLES, DOCS, STEPS, KVH, group, DH).astype(jnp.float32).transpose(3, 0, 1, 2, 4, 5)
    head_keys = cache_keys.reshape(PROMPT_TOKENS, KVH, DH).astype(jnp.float32).transpose(1, 0, 2)
    head_values = cache_values.reshape(PROMPT_TOKENS, KVH, DH).astype(jnp.float32).transpose(1, 0, 2)
    new_keys = soft_key.reshape(SAMPLES, DOCS, STEPS, KVH, DH).astype(jnp.float32).transpose(3, 0, 1, 2, 4)
    new_values = soft_value.reshape(SAMPLES, DOCS, STEPS, KVH, DH).astype(jnp.float32).transpose(3, 0, 1, 2, 4)
    doc_mask = (doc_ids[None, :] == jnp.arange(DOCS, dtype=jnp.int32)[:, None])[None, :, None, None, :]
    step_mask = (jnp.arange(STEPS)[:, None] >= jnp.arange(STEPS)[None, :])[None, None, :, None, :]

    def one_head(inputs):
        head_q, head_k, head_v, head_nk, head_nv = inputs
        scores = jnp.einsum('rpjgd,nd->rpjgn', head_q, head_k, precision=highest) * score_scale
        own = jnp.einsum('rpjgd,rpid->rpjgi', head_q, head_nk, precision=highest) * score_scale
        peak = jnp.maximum(lax.optimization_barrier(jnp.max(jnp.where(doc_mask, scores, mask_low), axis=-1)), lax.optimization_barrier(jnp.max(jnp.where(step_mask, own, mask_low), axis=-1)))
        cache_weights = jnp.where(doc_mask, jnp.exp(scores - peak[..., None]), 0.0)
        own_weights = jnp.where(step_mask, jnp.exp(own - peak[..., None]), 0.0)
        numer = jnp.einsum('rpjgn,nd->rpjgd', rounded(cache_weights), head_v, precision=highest) + jnp.einsum('rpjgi,rpid->rpjgd', rounded(own_weights), head_nv, precision=highest)
        denom = lax.optimization_barrier(jnp.sum(cache_weights, axis=-1)) + lax.optimization_barrier(jnp.sum(own_weights, axis=-1))
        return numer / denom[..., None]
    per_head = lax.map(one_head, (queries_all, head_keys, head_values, new_keys, new_values))
    soft_decode = per_head.transpose(1, 2, 3, 0, 4, 5).reshape(SAMPLES, DOCS, STEPS, QUERY_HEADS * DH).astype(jnp.bfloat16)
    return (light_out, light_decode, soft_decode)
```

```python
import math

import jax
import jax.numpy as jnp
from jax import lax
from jax.experimental import pallas as pl
from jax.experimental.pallas import tpu as pltpu
from jax.sharding import PartitionSpec as P

DH = 128
PAGE = 256
DOCS = 4
STEPS = 4
HEADS = 8
SEQ = 16
TP = 8
ROWS = 1024
PAGES_DEV = ROWS // PAGE
HALF = HEADS // 2 * 8

norm_eps = 1e-06
mask_low = -1e30
LOG2E = math.log2(math.e)
highest = lax.Precision.HIGHEST
f32 = jnp.float32
bf16 = jnp.bfloat16
MESH = pl.DeviceIdType.MESH

NN = (((1,), (0,)), ((), ()))
NT = (((1,), (1,)), ((), ()))
TN = (((0,), (0,)), ((), ()))

P_KEYS, P_VALUES, P_STATE, P_WEIGHT, P_SLOTS, P_CARRY, P_FINAL = range(7)
S_STATE, S_SLOTS, S_SOFT, S_BACK, S_GATHER = range(5)


def mm(a, b, dims, precision=None):
    return lax.dot_general(a, b, dims, precision=precision, preferred_element_type=f32)


def head_cols(h):
    return slice(h * DH, (h + 1) * DH)


def expand(rows):
    return jnp.concatenate(
        [jnp.broadcast_to(rows[i : i + 1], (8, DH)) for i in range(HEADS // 2)], axis=0
    )


def kernel(
    pages_ref, q_ref, k_ref, v_ref, g_ref, gain_ref, ck_ref, cv_ref,
    stq_ref, stk_ref, stv_ref, std_ref, sfq_ref, sfk_ref, sfv_ref,
    out_ref, dec_ref, soft_ref,
    mixed, ccol, crow, states, before, weights, stq, stk, stv, std, sfq, sfk, sfv,
    other_k, other_v,
    pair_state, pair_state_in, pair_weight, pair_weight_in, pair_slots, pair_slots_in,
    send_state, recv_state, send_slots, recv_slots, send_soft, recv_soft,
    carry, send_back, recv_back, pair_carry, pair_carry_in, carry_all,
    pair_final, pair_final_in, final_all, dec_own, send_gather, recv_gather, recv_tp,
    pair_send, pair_recv, seq_send, seq_recv, tp_send, tp_recv,
):
    me = lax.axis_index("seq")
    tp = lax.axis_index("tp")
    rep = lax.axis_index("rep")
    first_core = rep == 0
    own_rows = pl.ds(pl.multiple_of(rep * HALF, HALF), HALF)
    other_rows = pl.ds(pl.multiple_of((1 - rep) * HALF, HALF), HALF)

    def pair_copy(which, src, dst):
        return pltpu.make_async_remote_copy(
            src_ref=src, dst_ref=dst, send_sem=pair_send.at[which], recv_sem=pair_recv.at[which],
            device_id=(me, tp, 1 - rep), device_id_type=MESH,
        )

    def seq_copy(phase, src, dst, hop):
        target = lax.rem(me + hop, SEQ)
        return pltpu.make_async_remote_copy(
            src_ref=src(target), dst_ref=dst.at[me],
            send_sem=seq_send.at[phase, hop], recv_sem=seq_recv.at[phase, hop],
            device_id=(target, tp, rep), device_id_type=MESH,
        )

    def seq_start(phase, src, dst):
        def one(hop, _):
            seq_copy(phase, src, dst, hop).start()
            return 0

        lax.fori_loop(1, SEQ, one, 0)

    def seq_wait(phase, src, dst):
        def one(hop, _):
            source = lax.rem(me + SEQ - hop, SEQ)
            pltpu.make_async_remote_copy(
                src_ref=src(source), dst_ref=dst.at[source],
                send_sem=seq_send.at[phase, hop], recv_sem=seq_recv.at[phase, hop],
                device_id=(source, tp, rep), device_id_type=MESH,
            ).wait_recv()
            return 0

        lax.fori_loop(1, SEQ, one, 0)

    def seq_sent(phase, src, dst):
        def one(hop, _):
            seq_copy(phase, src, dst, hop).wait_send()
            return 0

        lax.fori_loop(1, SEQ, one, 0)

    src_state = lambda t: send_state.at[t]
    src_slots = lambda t: send_slots.at[t]
    src_soft = lambda t: send_soft.at[t]
    src_back = lambda t: send_back.at[t]
    src_gather = lambda t: send_gather

    def tp_copy(hop):
        return pltpu.make_async_remote_copy(
            src_ref=send_gather, dst_ref=recv_tp.at[tp],
            send_sem=tp_send.at[hop], recv_sem=tp_recv.at[hop],
            device_id=(me, lax.rem(tp + hop, TP), rep), device_id_type=MESH,
        )

    barrier = pltpu.get_barrier_semaphore()

    def greet_seq(hop, _):
        pl.semaphore_signal(
            barrier, inc=1, device_id=(lax.rem(me + hop, SEQ), tp, rep), device_id_type=MESH
        )
        return 0

    def greet_tp(hop, _):
        pl.semaphore_signal(
            barrier, inc=1, device_id=(me, lax.rem(tp + hop, TP), rep), device_id_type=MESH
        )
        return 0

    lax.fori_loop(1, SEQ, greet_seq, 0)
    lax.fori_loop(1, TP, greet_tp, 0)
    pl.semaphore_signal(barrier, inc=1, device_id=(me, tp, 1 - rep), device_id_type=MESH)

    ends = []
    for p in range(DOCS):
        ends.append(pages_ref[p] + (ends[-1] if ends else 0))
    chip_page = me * (2 * PAGES_DEV)
    dev_page = chip_page + rep * PAGES_DEV

    def flag(cond):
        return jnp.where(cond, 1, 0).astype(jnp.int32)

    def goes_on(page):
        hits = sum(flag(e == page) for e in ends)
        return jnp.where(hits == 0, 1.0, 0.0).astype(f32)

    def doc_of(page):
        return sum((e <= page).astype(jnp.int32) for e in ends)

    slot_page, slot_valid = [], []
    inside = [flag(jnp.logical_and(e > chip_page, e < chip_page + 2 * PAGES_DEV)) for e in ends]
    for s in range(2):
        place = 0
        for p in range(DOCS):
            rank = sum(inside[:p]) if p else 0
            place = place + inside[p] * flag(rank == s) * (ends[p] - chip_page)
        local = place - 1 - rep * PAGES_DEV
        ok = jnp.logical_and(
            place > 0, jnp.logical_and(local >= 0, local < PAGES_DEV)
        )
        slot_page.append(jnp.clip(local, 0, PAGES_DEV - 1))
        slot_valid.append(jnp.where(ok, 1.0, 0.0).astype(f32))

    rows_i = lax.broadcasted_iota(jnp.int32, (PAGE, PAGE), 0)
    cols_i = lax.broadcasted_iota(jnp.int32, (PAGE, PAGE), 1)
    states[0] = jnp.zeros((SEQ, 2 * HALF, DH), f32)

    def state_page(k, carried):
        rows = pl.ds(pl.multiple_of(k * PAGE, PAGE), PAGE)
        g = g_ref[rows, :] * LOG2E
        lower = (rows_i >= cols_i).astype(f32)
        upper = (rows_i <= cols_i).astype(f32)
        c = mm(lower, g, NN, highest)
        ccol[rows, :] = c
        crow[k] = mm(g, upper, TN, highest)
        decay = jnp.exp2(mm(g, jnp.ones((PAGE, DH), f32), TN, highest))
        cont = goes_on(dev_page + k)
        before[k] = carried * cont
        keep = decay * cont
        after = carried * keep
        weights[k] = after
        fade = jnp.exp2(c[PAGE - 1 : PAGE, :] - c)
        for h in range(HEADS):
            kd = (k_ref[rows, head_cols(h)].astype(f32) * fade[:, h : h + 1]).astype(bf16)
            add = mm(v_ref[rows, head_cols(h)], kd, TN)
            old = states[k, :, h * 8 : h * 8 + 8, :]
            states[k + 1, :, h * 8 : h * 8 + 8, :] = old * keep[h : h + 1, :][None] + add.reshape(
                SEQ, 8, DH
            )
        return after

    total = lax.fori_loop(0, PAGES_DEV, state_page, jnp.ones((HEADS, DH), f32))

    pl.semaphore_wait(barrier, SEQ - 1 + TP - 1 + 1)
    pair_state[...] = states[PAGES_DEV, :, other_rows, :].astype(bf16)
    pair_weight[0:8] = total
    for s in range(2):
        w = jnp.zeros((HEADS, DH), f32)
        for k in range(PAGES_DEV):
            pick = jnp.where(slot_page[s] == k, slot_valid[s], 0.0).astype(f32)
            w = w + pick * weights[k]
        pair_weight[8 + 8 * s : 16 + 8 * s] = w
    pair_copy(P_STATE, pair_state, pair_state_in).start()
    pair_copy(P_WEIGHT, pair_weight, pair_weight_in).start()
    for s in range(2):
        pair_slots[s] = (states[slot_page[s] + 1][:, 0:HALF, :] * slot_valid[s]).astype(bf16)
        pair_slots[2 + s] = (states[slot_page[s] + 1][:, HALF:, :] * slot_valid[s]).astype(bf16)
    pair_other = pair_slots.at[pl.ds((1 - rep) * 2, 2)]
    pair_copy(P_SLOTS, pair_other, pair_slots_in).start()
    pair_copy(P_KEYS, ck_ref, other_k).start()
    pair_copy(P_VALUES, cv_ref, other_v).start()

    causal = rows_i >= cols_i

    def inside_page(k):
        rows = pl.ds(pl.multiple_of(k * PAGE, PAGE), PAGE)
        c = ccol[rows, :]
        r = crow[k]
        for h in range(HEADS):
            scores = mm(q_ref[rows, head_cols(h)], k_ref[rows, head_cols(h)], NT)
            grid = jnp.exp2(c[:, h : h + 1] - r[h : h + 1, :])
            block = jnp.where(causal, scores * grid, 0.0).astype(bf16)
            mixed[rows, head_cols(h)] = mm(block, v_ref[rows, head_cols(h)], NN)

    def inside_loop(first, last):
        def one(k, _):
            inside_page(k)
            return 0

        lax.fori_loop(first, last, one, 0)

    inside_loop(0, 1)

    def half(x):
        return lax.select(first_core, x[0:4], x[4:8])

    pair_copy(P_STATE, pair_state, pair_state_in).wait_recv()
    pair_copy(P_WEIGHT, pair_weight, pair_weight_in).wait_recv()
    own_state = states[PAGES_DEV, :, own_rows, :]
    got_state = pair_state_in[...].astype(f32)
    state0 = lax.select(first_core, own_state, got_state)
    state1 = lax.select(first_core, got_state, own_state)
    own_w = [half(pair_weight[8 * n : 8 * n + 8]) for n in range(3)]
    got_w = [half(pair_weight_in[8 * n : 8 * n + 8]) for n in range(3)]
    w0 = [lax.select(first_core, a, b) for a, b in zip(own_w, got_w)]
    w1 = [lax.select(first_core, b, a) for a, b in zip(own_w, got_w)]
    chip_state = expand(w1[0])[None] * state0 + state1
    chip_w = jnp.concatenate([w1[0] * w0[0], w0[1] + w1[1] * w0[0]], axis=0)
    chip_hi = chip_w.astype(bf16).astype(f32)
    chip_rows = jnp.concatenate([chip_hi, chip_w - chip_hi], axis=0).astype(bf16)
    send_state[:, 0:HALF, :] = chip_state.astype(bf16)
    send_state[:, HALF:, :] = jnp.broadcast_to(chip_rows[None], (SEQ, 16, DH))
    seq_start(S_STATE, src_state, recv_state)
    recv_state[me] = send_state[me]

    pair_copy(P_SLOTS, pair_other, pair_slots_in).wait_recv()
    for s in range(2):
        own_slot = states[slot_page[s] + 1][:, 0:HALF, :]
        own_slot = lax.select(first_core, own_slot, states[slot_page[s] + 1][:, HALF:, :])
        slot = own_slot * slot_valid[s] + pair_slots_in[s].astype(f32)
        slot = slot + expand(w1[1 + s])[None] * state0
        send_slots[:, s] = slot.astype(bf16)
    seq_start(S_SLOTS, src_slots, recv_slots)
    recv_slots[me] = send_slots[me]

    for p in range(DOCS):
        part = slice(4 * p, 4 * p + 4)
        stq[part, :] = stq_ref[0, p].astype(f32)
        stk[part, :] = stk_ref[0, p].astype(f32)
        stv[part, :] = stv_ref[0, p].astype(f32)
        std[part, :] = std_ref[0, p]
        sfk[p] = sfk_ref[0, p].astype(f32)
        sfv[p] = sfv_ref[0, p].astype(f32)
        for h in range(HEADS):
            sfq[pl.ds(p * 32 + h, 4, stride=8), :] = sfq_ref[0, p, :, head_cols(h)].astype(f32)

    scale = DH**-0.5 * LOG2E
    pair_copy(P_KEYS, ck_ref, other_k).wait_recv()
    pair_copy(P_VALUES, cv_ref, other_v).wait_recv()
    queries = sfq[...].astype(bf16)
    query_doc = lax.broadcasted_iota(jnp.int32, (DH, ROWS), 0) // 32
    key_page = lax.broadcasted_iota(jnp.int32, (1, ROWS), 1) // PAGE
    score, here = [], []
    for base, key_block in ((dev_page, ck_ref), (chip_page + (1 - rep) * PAGES_DEV, other_k)):
        score.append(mm(queries, key_block[...], NT) * scale)
        here.append(query_doc == jnp.broadcast_to(doc_of(key_page + base), (DH, ROWS)))
    peak = jnp.maximum(
        *[
            jnp.max(jnp.where(m, s, mask_low), axis=1, keepdims=True)
            for m, s in zip(here, score)
        ]
    )
    chance = [jnp.where(m, jnp.exp2(s - peak), 0.0) for m, s in zip(here, score)]
    amount = sum(jnp.sum(x, axis=1, keepdims=True) for x in chance)
    numer = mm(chance[0].astype(bf16), cv_ref[...], NN) + mm(
        chance[1].astype(bf16), other_v[...], NN
    )
    lane = lax.broadcasted_iota(jnp.int32, (DH, DH), 1)
    both = jnp.where(lane < 64, jnp.broadcast_to(peak, (DH, DH)), jnp.broadcast_to(amount, (DH, DH)))
    send_soft[:, 0:8, :] = numer.reshape(SEQ, 8, DH)
    send_soft[:, 8:16, :] = both.reshape(SEQ, 8, DH)
    seq_start(S_SOFT, src_soft, recv_soft)
    recv_soft[me] = send_soft[me]

    seq_wait(S_STATE, src_state, recv_state)
    running = jnp.zeros((HALF, DH), f32)
    for j in range(SEQ):
        carry[j] = running
        send_back[j] = running.astype(bf16)
        rows = recv_state[j, HALF:, :].astype(f32)
        running = expand(rows[0:4] + rows[8:12]) * running + recv_state[j, 0:HALF, :].astype(f32)
    carry[SEQ] = running
    seq_start(S_BACK, src_back, recv_back)
    recv_back[me] = send_back[me]

    inside_loop(1, 3)

    seq_wait(S_SLOTS, src_slots, recv_slots)
    for p in range(DOCS):
        last_page = jnp.clip(ends[p] - 1, 0, 2 * PAGES_DEV * SEQ - 1)
        chip = lax.shift_right_logical(last_page, 3)
        chip_last = jnp.bitwise_and(last_page, 7) == 7
        rank = sum(
            [flag(lax.shift_right_logical(ends[o] - 1, 3) == chip) for o in range(p)],
            jnp.int32(0),
        )
        rows = recv_state[chip][HALF:, :].astype(f32)
        w = expand(rows[4:8] + rows[12:16]) * jnp.where(rank == 0, 1.0, 0.0).astype(f32)
        ended = recv_slots[chip, jnp.minimum(rank, 1)].astype(f32) + w * carry[chip]
        final = lax.select(chip_last, carry[chip + 1], ended)
        final_all[p, own_rows, :] = final
        pair_final[p] = final.astype(bf16)
    pair_copy(P_FINAL, pair_final, pair_final_in).start()

    inside_loop(3, 4)

    seq_wait(S_BACK, src_back, recv_back)
    carry0 = recv_back[...].astype(f32)
    carry1 = expand(w0[0])[None] * carry0 + state0
    carry_all[:, own_rows, :] = lax.select(first_core, carry0, carry1)
    pair_carry[...] = lax.select(first_core, carry1, carry0).astype(bf16)
    pair_copy(P_CARRY, pair_carry, pair_carry_in).start()

    seq_wait(S_SOFT, src_soft, recv_soft)
    doc = me // STEPS
    step = lax.rem(me, STEPS)
    own_q = sfq[pl.ds(pl.multiple_of(me * 8, 8), 8), :]
    own_k = sfk[doc]
    own_v = sfv[doc]
    peaks = [recv_soft[s, 8:16, 0:1] for s in range(SEQ)]
    amounts = [recv_soft[s, 8:16, 64:65] for s in range(SEQ)]
    numers = [recv_soft[s, 0:8, :] for s in range(SEQ)]
    top = peaks[0]
    for x in peaks[1:]:
        top = jnp.maximum(top, x)
    own = []
    for i in range(STEPS):
        s = jnp.sum(own_q * own_k[i : i + 1, :], axis=1, keepdims=True) * scale
        own.append(lax.select(step >= i, s, jnp.full((8, 1), mask_low, f32)))
        top = jnp.maximum(top, own[-1])
    numer = jnp.zeros((8, DH), f32)
    amount = jnp.zeros((8, 1), f32)
    for s in range(SEQ):
        shrink = jnp.exp2(peaks[s] - top)
        numer = numer + numers[s] * shrink
        amount = amount + amounts[s] * shrink
    for i in range(STEPS):
        e = lax.select(step >= i, jnp.exp2(own[i] - top), jnp.zeros((8, 1), f32))
        numer = numer + e.astype(bf16).astype(f32) * own_v[i : i + 1, :]
        amount = amount + e
    send_gather[0:8, :] = numer / amount

    pair_copy(P_FINAL, pair_final, pair_final_in).wait_recv()
    final_all[:, other_rows, :] = pair_final_in[...].astype(f32)
    t16 = lax.broadcasted_iota(jnp.int32, (16, 16), 0)
    s16 = lax.broadcasted_iota(jnp.int32, (16, 16), 1)
    chain = jnp.logical_and(t16 // STEPS == s16 // STEPS, t16 >= s16)
    chain_t = jnp.logical_and(t16 // STEPS == s16 // STEPS, t16 <= s16)
    fall = std[...] * LOG2E
    fall_col = mm(chain.astype(f32), fall, NN, highest)
    fall_row = mm(fall, chain_t.astype(f32), TN, highest)
    f128 = lax.broadcasted_iota(jnp.int32, (DH, 8), 0)
    c128 = lax.broadcasted_iota(jnp.int32, (DH, 8), 1)
    pick = (f128 == c128 + me * 8).astype(f32)
    r32 = lax.broadcasted_iota(jnp.int32, (32, 8), 0)
    c32 = lax.broadcasted_iota(jnp.int32, (32, 8), 1)
    fold = (jnp.bitwise_and(r32, 7) == c32).astype(f32)
    t32 = lax.broadcasted_iota(jnp.int32, (16, 32), 0)
    p32 = lax.broadcasted_iota(jnp.int32, (16, 32), 1)
    same = t32 // STEPS == p32 // 8
    squares = jnp.zeros((16, 8), f32)
    for h in range(HEADS):
        q = stq[:, head_cols(h)]
        k = stk[:, head_cols(h)]
        v = mm(stv[:, head_cols(h)], pick, NN, highest)
        spread = jnp.exp2(fall_col[:, h : h + 1] - fall_row[h : h + 1, :])
        grid = jnp.where(chain, mm(q, k, NT, highest) * spread, 0.0)
        final = final_all[:, h * 8 : h * 8 + 8, :].reshape(32, DH)
        read = jnp.where(same, mm(q, final, NT, highest), 0.0)
        value = mm(read, fold, NN, highest) * jnp.exp2(fall_col[:, h : h + 1])
        value = value + mm(grid, v, NN, highest)
        dec_own[h] = value
        squares = squares + value * value
    send_gather[8:24, :] = mm(squares, jnp.ones((8, DH), f32), NN, highest)
    seq_start(S_GATHER, src_gather, recv_gather)
    recv_gather[me] = send_gather[...]

    pair_copy(P_CARRY, pair_carry, pair_carry_in).wait_recv()
    carry_all[:, other_rows, :] = pair_carry_in[...].astype(f32)

    lines = []
    for k in range(PAGES_DEV):
        rows = slice(k * PAGE, (k + 1) * PAGE)
        rise = jnp.exp2(ccol[rows, :])
        cont = goes_on(dev_page + k)
        w = before[k]
        squares = jnp.zeros((PAGE, DH), f32)
        for h in range(HEADS):
            part = slice(h * 8, h * 8 + 8)
            state = states[k, :, part, :] * cont + carry_all[:, part, :] * w[h : h + 1, :][None]
            qd = (q_ref[rows, head_cols(h)].astype(f32) * rise[:, h : h + 1]).astype(bf16)
            value = mixed[rows, head_cols(h)] + mm(qd, state.reshape(DH, DH).astype(bf16), NT)
            mixed[rows, head_cols(h)] = value
            squares = squares + value * value
        lines.append(mm(jnp.ones((8, DH), f32), squares, NT, highest))

    seq_wait(S_GATHER, src_gather, recv_gather)
    seq_sent(S_GATHER, src_gather, recv_gather)
    decode_squares = jnp.zeros((16, DH), f32)
    for s in range(SEQ):
        soft_ref[s] = recv_gather[s, 0:8, :]
        decode_squares = decode_squares + recv_gather[s, 8:24, :]
    for k in range(PAGES_DEV):
        for n in range(PAGE // DH):
            send_gather[2 * k + n : 2 * k + n + 1, :] = lines[k][0:1, head_cols(n)]
    send_gather[8:24, :] = decode_squares

    def tp_start(hop, _):
        tp_copy(hop).start()
        return 0

    lax.fori_loop(1, TP, tp_start, 0)
    recv_tp[tp] = send_gather[...]

    def tp_wait(hop, _):
        source = lax.rem(tp + TP - hop, TP)
        pltpu.make_async_remote_copy(
            src_ref=send_gather, dst_ref=recv_tp.at[source],
            send_sem=tp_send.at[hop], recv_sem=tp_recv.at[hop],
            device_id=(me, source, rep), device_id_type=MESH,
        ).wait_recv()
        return 0

    lax.fori_loop(1, TP, tp_wait, 0)

    features = TP * HEADS * DH
    gain = gain_ref[...]
    total_squares = recv_tp[0, 8:24, :]
    for t in range(1, TP):
        total_squares = total_squares + recv_tp[t, 8:24, :]
    factor = lax.rsqrt(total_squares / features + norm_eps)[:, 0:8]
    gain_cols = mm(gain, pick, NN, highest)
    for h in range(HEADS):
        dec_ref[h] = dec_own[h] * factor * gain_cols[h : h + 1, :]
    ones = jnp.ones((TP, DH), f32)
    for b in range(ROWS // DH):
        total = mm(recv_tp[:, b, :], ones, TN, highest)
        factor = lax.rsqrt(total / features + norm_eps)
        rows = slice(b * DH, (b + 1) * DH)
        for h in range(HEADS):
            out_ref[rows, head_cols(h)] = (
                mixed[rows, head_cols(h)] * factor * gain[h : h + 1, :]
            ).astype(bf16)

    for which, src, dst in (
        (P_KEYS, ck_ref, other_k),
        (P_VALUES, cv_ref, other_v),
        (P_STATE, pair_state, pair_state_in),
        (P_WEIGHT, pair_weight, pair_weight_in),
        (P_SLOTS, pair_other, pair_slots_in),
        (P_CARRY, pair_carry, pair_carry_in),
        (P_FINAL, pair_final, pair_final_in),
    ):
        pair_copy(which, src, dst).wait_send()
    seq_sent(S_STATE, src_state, recv_state)
    seq_sent(S_SLOTS, src_slots, recv_slots)
    seq_sent(S_SOFT, src_soft, recv_soft)
    seq_sent(S_BACK, src_back, recv_back)

    def tp_sent(hop, _):
        tp_copy(hop).wait_send()
        return 0

    lax.fori_loop(1, TP, tp_sent, 0)


def per_device(
    light_query, light_key, light_value, log_decay, prompt_pages, norm_gain, cache_keys,
    cache_values, step_query, step_key, step_value, step_decay, soft_query, soft_key, soft_value,
):
    vm = pl.BlockSpec(memory_space=pltpu.VMEM)
    V = pltpu.VMEM
    D = pltpu.SemaphoreType.DMA
    out, dec, soft = pl.pallas_call(
        kernel,
        out_shape=(
            jax.ShapeDtypeStruct((ROWS, HEADS * DH), bf16),
            jax.ShapeDtypeStruct((HEADS, 16, 8), f32),
            jax.ShapeDtypeStruct((SEQ, 8, DH), f32),
        ),
        in_specs=[pl.BlockSpec(memory_space=pltpu.SMEM)] + [vm] * 14,
        out_specs=(vm, vm, vm),
        scratch_shapes=[
            V((ROWS, HEADS * DH), f32),
            V((ROWS, HEADS), f32),
            V((PAGES_DEV, HEADS, PAGE), f32),
            V((PAGES_DEV + 1, SEQ, 2 * HALF, DH), f32),
            V((PAGES_DEV, HEADS, DH), f32),
            V((PAGES_DEV, HEADS, DH), f32),
            V((16, HEADS * DH), f32),
            V((16, HEADS * DH), f32),
            V((16, HEADS * DH), f32),
            V((16, HEADS), f32),
            V((DH, DH), f32),
            V((DOCS, STEPS, DH), f32),
            V((DOCS, STEPS, DH), f32),
            V((ROWS, DH), bf16),
            V((ROWS, DH), bf16),
            V((SEQ, HALF, DH), bf16),
            V((SEQ, HALF, DH), bf16),
            V((24, DH), f32),
            V((24, DH), f32),
            V((4, SEQ, HALF, DH), bf16),
            V((2, SEQ, HALF, DH), bf16),
            V((SEQ, HALF + 16, DH), bf16),
            V((SEQ, HALF + 16, DH), bf16),
            V((SEQ, 2, HALF, DH), bf16),
            V((SEQ, 2, HALF, DH), bf16),
            V((SEQ, 16, DH), f32),
            V((SEQ, 16, DH), f32),
            V((SEQ + 1, HALF, DH), f32),
            V((SEQ, HALF, DH), bf16),
            V((SEQ, HALF, DH), bf16),
            V((SEQ, HALF, DH), bf16),
            V((SEQ, HALF, DH), bf16),
            V((SEQ, 2 * HALF, DH), f32),
            V((DOCS, HALF, DH), bf16),
            V((DOCS, HALF, DH), bf16),
            V((DOCS, 2 * HALF, DH), f32),
            V((HEADS, 16, 8), f32),
            V((24, DH), f32),
            V((SEQ, 24, DH), f32),
            V((TP, 24, DH), f32),
            D((7,)),
            D((7,)),
            D((5, SEQ)),
            D((5, SEQ)),
            D((TP,)),
            D((TP,)),
        ],
        compiler_params=pltpu.CompilerParams(
            collective_id=0, has_side_effects=True, vmem_limit_bytes=48 * 1024 * 1024
        ),
        name="attention_block",
    )(
        prompt_pages, light_query, light_key, light_value, log_decay,
        norm_gain.reshape(HEADS, DH), cache_keys, cache_values,
        step_query, step_key, step_value, step_decay, soft_query, soft_key, soft_value,
    )
    light_decode = dec.reshape(HEADS, DOCS, STEPS, 8).transpose(1, 2, 0, 3).astype(bf16)[None]
    soft_decode = soft.reshape(1, DOCS, STEPS, HEADS * DH).astype(bf16)
    return out, light_decode, soft_decode


def solution(mesh):
    prompt = P(("seq", "rep"), "tp")
    sample = P("rep", None, None, "tp")
    return jax.shard_map(
        per_device,
        mesh=mesh,
        in_specs=(prompt,) * 4 + (P(), P("tp")) + (prompt,) * 2 + (sample,) * 7,
        out_specs=(prompt, P("rep", None, None, "tp", "seq"), sample),
        check_vma=False,
    )
```

```python
import math

import jax
import jax.numpy as jnp
from jax import lax
from jax.experimental import pallas as pl
from jax.experimental.pallas import tpu as pltpu
from jax.sharding import PartitionSpec as P

DH = 128
PAGE = 256
DOCS = 4
STEPS = 4
HEADS = 8
SEQ = 16
TP = 8
ROWS = 1024
PAGES_DEV = ROWS // PAGE
HALF = HEADS // 2 * 8

norm_eps = 1e-06
mask_low = -1e30
LOG2E = math.log2(math.e)
highest = lax.Precision.HIGHEST
f32 = jnp.float32
bf16 = jnp.bfloat16
MESH = pl.DeviceIdType.MESH

NN = (((1,), (0,)), ((), ()))
NT = (((1,), (1,)), ((), ()))
TN = (((0,), (0,)), ((), ()))

P_KEYS, P_VALUES, P_STATE, P_WEIGHT, P_SLOTS, P_CARRY, P_FINAL = range(7)
S_STATE, S_SLOTS, S_SOFT, S_BACK, S_GATHER = range(5)


def mm(a, b, dims, precision=None):
    return lax.dot_general(a, b, dims, precision=precision, preferred_element_type=f32)


def head_cols(h):
    return slice(h * DH, (h + 1) * DH)


def expand(rows):
    return jnp.concatenate(
        [jnp.broadcast_to(rows[i : i + 1], (8, DH)) for i in range(HEADS // 2)], axis=0
    )


def kernel(
    pages_in, q_in, k_in, v_in, g_in, gain_in, ck_in, cv_in,
    stq_in, stk_in, stv_in, std_in, sfq_in, sfk_in, sfv_in,
    out_ref, dec_ref, soft_ref,
    pages_ref, q_ref, k_ref, v_ref, g_ref, gain_ref, ck_ref, cv_ref,
    stq_ref, stk_ref, stv_ref, std_ref, sfq_ref, sfk_ref, sfv_ref,
    mixed, ccol, crow, states, before, weights, stq, stk, stv, std, sfq, sfk, sfv,
    other_k, other_v,
    pair_state, pair_state_in, pair_weight, pair_weight_in, pair_slots, pair_slots_in,
    send_state, recv_state, send_slots, recv_slots, send_soft, recv_soft,
    carry, send_back, recv_back, pair_carry, pair_carry_in, carry_all,
    pair_final, pair_final_in, final_all, dec_own, send_gather, recv_gather, recv_tp,
    pair_send, pair_recv, seq_send, seq_recv, tp_send, tp_recv, in_sem,
):
    me = lax.axis_index("seq")
    tp = lax.axis_index("tp")
    rep = lax.axis_index("rep")
    first_core = rep == 0
    own_rows = pl.ds(pl.multiple_of(rep * HALF, HALF), HALF)
    other_rows = pl.ds(pl.multiple_of((1 - rep) * HALF, HALF), HALF)

    def page_rows(k):
        return pl.ds(k * PAGE, PAGE)

    inputs = {}

    def fetch(name, src, dst):
        inputs[name] = pltpu.make_async_copy(src, dst, in_sem.at[len(inputs)])
        inputs[name].start()

    fetch("pages", pages_in, pages_ref)
    fetch("g", g_in, g_ref)
    for k in range(PAGES_DEV):
        fetch(("k", k), k_in.at[page_rows(k)], k_ref.at[page_rows(k)])
        fetch(("v", k), v_in.at[page_rows(k)], v_ref.at[page_rows(k)])
    fetch("q", q_in, q_ref)
    fetch("ck", ck_in, ck_ref)
    fetch("cv", cv_in, cv_ref)
    small = (
        (stq_in, stq_ref), (stk_in, stk_ref), (stv_in, stv_ref), (std_in, std_ref),
        (sfq_in, sfq_ref), (sfk_in, sfk_ref), (sfv_in, sfv_ref),
    )
    for n, (src, dst) in enumerate(small):
        fetch(("small", n), src.at[0], dst)
    fetch("gain", gain_in, gain_ref)

    def pair_copy(which, src, dst):
        return pltpu.make_async_remote_copy(
            src_ref=src, dst_ref=dst, send_sem=pair_send.at[which], recv_sem=pair_recv.at[which],
            device_id=(me, tp, 1 - rep), device_id_type=MESH,
        )

    def seq_copy(phase, src, dst, hop):
        target = lax.rem(me + hop, SEQ)
        return pltpu.make_async_remote_copy(
            src_ref=src(target), dst_ref=dst.at[me],
            send_sem=seq_send.at[phase, hop], recv_sem=seq_recv.at[phase, hop],
            device_id=(target, tp, rep), device_id_type=MESH,
        )

    def seq_start(phase, src, dst):
        def one(hop, _):
            seq_copy(phase, src, dst, hop).start()
            return 0

        lax.fori_loop(1, SEQ, one, 0)

    def seq_wait(phase, src, dst):
        def one(hop, _):
            source = lax.rem(me + SEQ - hop, SEQ)
            pltpu.make_async_remote_copy(
                src_ref=src(source), dst_ref=dst.at[source],
                send_sem=seq_send.at[phase, hop], recv_sem=seq_recv.at[phase, hop],
                device_id=(source, tp, rep), device_id_type=MESH,
            ).wait_recv()
            return 0

        lax.fori_loop(1, SEQ, one, 0)

    def seq_sent(phase, src, dst):
        def one(hop, _):
            seq_copy(phase, src, dst, hop).wait_send()
            return 0

        lax.fori_loop(1, SEQ, one, 0)

    src_state = lambda t: send_state.at[t]
    src_slots = lambda t: send_slots.at[t]
    src_soft = lambda t: send_soft.at[t]
    src_back = lambda t: send_back.at[t]
    src_gather = lambda t: send_gather

    def tp_copy(hop):
        return pltpu.make_async_remote_copy(
            src_ref=send_gather, dst_ref=recv_tp.at[tp],
            send_sem=tp_send.at[hop], recv_sem=tp_recv.at[hop],
            device_id=(me, lax.rem(tp + hop, TP), rep), device_id_type=MESH,
        )

    barrier = pltpu.get_barrier_semaphore()

    def greet_seq(hop, _):
        pl.semaphore_signal(
            barrier, inc=1, device_id=(lax.rem(me + hop, SEQ), tp, rep), device_id_type=MESH
        )
        return 0

    def greet_tp(hop, _):
        pl.semaphore_signal(
            barrier, inc=1, device_id=(me, lax.rem(tp + hop, TP), rep), device_id_type=MESH
        )
        return 0

    lax.fori_loop(1, SEQ, greet_seq, 0)
    lax.fori_loop(1, TP, greet_tp, 0)
    pl.semaphore_signal(barrier, inc=1, device_id=(me, tp, 1 - rep), device_id_type=MESH)

    inputs["pages"].wait()
    ends = []
    for p in range(DOCS):
        ends.append(pages_ref[p] + (ends[-1] if ends else 0))
    chip_page = me * (2 * PAGES_DEV)
    dev_page = chip_page + rep * PAGES_DEV

    def flag(cond):
        return jnp.where(cond, 1, 0).astype(jnp.int32)

    def goes_on(page):
        hits = sum(flag(e == page) for e in ends)
        return jnp.where(hits == 0, 1.0, 0.0).astype(f32)

    def doc_of(page):
        return sum((e <= page).astype(jnp.int32) for e in ends)

    slot_page, slot_valid = [], []
    inside = [flag(jnp.logical_and(e > chip_page, e < chip_page + 2 * PAGES_DEV)) for e in ends]
    for s in range(2):
        place = 0
        for p in range(DOCS):
            rank = sum(inside[:p]) if p else 0
            place = place + inside[p] * flag(rank == s) * (ends[p] - chip_page)
        local = place - 1 - rep * PAGES_DEV
        ok = jnp.logical_and(
            place > 0, jnp.logical_and(local >= 0, local < PAGES_DEV)
        )
        slot_page.append(jnp.clip(local, 0, PAGES_DEV - 1))
        slot_valid.append(jnp.where(ok, 1.0, 0.0).astype(f32))

    rows_i = lax.broadcasted_iota(jnp.int32, (PAGE, PAGE), 0)
    cols_i = lax.broadcasted_iota(jnp.int32, (PAGE, PAGE), 1)
    states[0] = jnp.zeros((SEQ, 2 * HALF, DH), f32)

    inputs["g"].wait()

    def state_page(k, carried):
        rows = pl.ds(pl.multiple_of(k * PAGE, PAGE), PAGE)
        g = g_ref[:, rows] * LOG2E
        lower = (rows_i >= cols_i).astype(f32)
        upper = (rows_i <= cols_i).astype(f32)
        c = mm(lower, g, NT, highest)
        ccol[rows, :] = c
        crow[k] = mm(g, upper, NN, highest)
        decay = jnp.exp2(mm(g, jnp.ones((PAGE, DH), f32), NN, highest))
        cont = goes_on(dev_page + k)
        before[k] = carried * cont
        keep = decay * cont
        after = carried * keep
        weights[k] = after
        fade = jnp.exp2(c[PAGE - 1 : PAGE, :] - c)
        for h in range(HEADS):
            kd = (k_ref[rows, head_cols(h)].astype(f32) * fade[:, h : h + 1]).astype(bf16)
            add = mm(v_ref[rows, head_cols(h)], kd, TN)
            old = states[k, :, h * 8 : h * 8 + 8, :]
            states[k + 1, :, h * 8 : h * 8 + 8, :] = old * keep[h : h + 1, :][None] + add.reshape(
                SEQ, 8, DH
            )
        return after

    total = jnp.ones((HEADS, DH), f32)
    for k in range(PAGES_DEV):
        inputs[("k", k)].wait()
        inputs[("v", k)].wait()
        total = state_page(k, total)

    pl.semaphore_wait(barrier, SEQ - 1 + TP - 1 + 1)
    pair_state[...] = states[PAGES_DEV, :, other_rows, :].astype(bf16)
    pair_weight[0:8] = total
    for s in range(2):
        w = jnp.zeros((HEADS, DH), f32)
        for k in range(PAGES_DEV):
            pick = jnp.where(slot_page[s] == k, slot_valid[s], 0.0).astype(f32)
            w = w + pick * weights[k]
        pair_weight[8 + 8 * s : 16 + 8 * s] = w
    pair_copy(P_STATE, pair_state, pair_state_in).start()
    pair_copy(P_WEIGHT, pair_weight, pair_weight_in).start()
    for s in range(2):
        pair_slots[s] = (states[slot_page[s] + 1][:, 0:HALF, :] * slot_valid[s]).astype(bf16)
        pair_slots[2 + s] = (states[slot_page[s] + 1][:, HALF:, :] * slot_valid[s]).astype(bf16)
    pair_other = pair_slots.at[pl.ds((1 - rep) * 2, 2)]
    pair_copy(P_SLOTS, pair_other, pair_slots_in).start()
    pair_copy(P_KEYS, ck_in, other_k).start()
    pair_copy(P_VALUES, cv_in, other_v).start()

    causal = rows_i >= cols_i

    def inside_page(k):
        rows = pl.ds(pl.multiple_of(k * PAGE, PAGE), PAGE)
        c = ccol[rows, :]
        r = crow[k]
        for h in range(HEADS):
            scores = mm(q_ref[rows, head_cols(h)], k_ref[rows, head_cols(h)], NT)
            grid = jnp.exp2(c[:, h : h + 1] - r[h : h + 1, :])
            block = jnp.where(causal, scores * grid, 0.0).astype(bf16)
            mixed[rows, head_cols(h)] = mm(block, v_ref[rows, head_cols(h)], NN)

    def inside_loop(first, last):
        def one(k, _):
            inside_page(k)
            return 0

        lax.fori_loop(first, last, one, 0)

    inputs["q"].wait()
    inside_loop(0, 1)

    def half(x):
        return lax.select(first_core, x[0:4], x[4:8])

    pair_copy(P_STATE, pair_state, pair_state_in).wait_recv()
    pair_copy(P_WEIGHT, pair_weight, pair_weight_in).wait_recv()
    own_state = states[PAGES_DEV, :, own_rows, :]
    got_state = pair_state_in[...].astype(f32)
    state0 = lax.select(first_core, own_state, got_state)
    state1 = lax.select(first_core, got_state, own_state)
    own_w = [half(pair_weight[8 * n : 8 * n + 8]) for n in range(3)]
    got_w = [half(pair_weight_in[8 * n : 8 * n + 8]) for n in range(3)]
    w0 = [lax.select(first_core, a, b) for a, b in zip(own_w, got_w)]
    w1 = [lax.select(first_core, b, a) for a, b in zip(own_w, got_w)]
    chip_state = expand(w1[0])[None] * state0 + state1
    chip_w = jnp.concatenate([w1[0] * w0[0], w0[1] + w1[1] * w0[0]], axis=0)
    chip_hi = chip_w.astype(bf16).astype(f32)
    chip_rows = jnp.concatenate([chip_hi, chip_w - chip_hi], axis=0).astype(bf16)
    send_state[:, 0:HALF, :] = chip_state.astype(bf16)
    send_state[:, HALF:, :] = jnp.broadcast_to(chip_rows[None], (SEQ, 16, DH))
    seq_start(S_STATE, src_state, recv_state)
    recv_state[me] = send_state[me]

    pair_copy(P_SLOTS, pair_other, pair_slots_in).wait_recv()
    for s in range(2):
        own_slot = states[slot_page[s] + 1][:, 0:HALF, :]
        own_slot = lax.select(first_core, own_slot, states[slot_page[s] + 1][:, HALF:, :])
        slot = own_slot * slot_valid[s] + pair_slots_in[s].astype(f32)
        slot = slot + expand(w1[1 + s])[None] * state0
        send_slots[:, s] = slot.astype(bf16)
    seq_start(S_SLOTS, src_slots, recv_slots)
    recv_slots[me] = send_slots[me]

    for n in range(len(small)):
        inputs[("small", n)].wait()
    inputs["ck"].wait()
    inputs["cv"].wait()
    for p in range(DOCS):
        part = slice(4 * p, 4 * p + 4)
        stq[part, :] = stq_ref[p].astype(f32)
        stk[part, :] = stk_ref[p].astype(f32)
        stv[part, :] = stv_ref[p].astype(f32)
        std[part, :] = std_ref[p]
        sfk[p] = sfk_ref[p].astype(f32)
        sfv[p] = sfv_ref[p].astype(f32)
        for h in range(HEADS):
            sfq[pl.ds(p * 32 + h, 4, stride=8), :] = sfq_ref[p, :, head_cols(h)].astype(f32)

    scale = DH**-0.5 * LOG2E
    pair_copy(P_KEYS, ck_in, other_k).wait_recv()
    pair_copy(P_VALUES, cv_in, other_v).wait_recv()
    queries = sfq[...].astype(bf16)
    query_doc = lax.broadcasted_iota(jnp.int32, (DH, ROWS), 0) // 32
    key_page = lax.broadcasted_iota(jnp.int32, (1, ROWS), 1) // PAGE
    score, here = [], []
    for base, key_block in ((dev_page, ck_ref), (chip_page + (1 - rep) * PAGES_DEV, other_k)):
        score.append(mm(queries, key_block[...], NT) * scale)
        here.append(query_doc == jnp.broadcast_to(doc_of(key_page + base), (DH, ROWS)))
    peak = jnp.maximum(
        *[
            jnp.max(jnp.where(m, s, mask_low), axis=1, keepdims=True)
            for m, s in zip(here, score)
        ]
    )
    chance = [jnp.where(m, jnp.exp2(s - peak), 0.0) for m, s in zip(here, score)]
    amount = sum(jnp.sum(x, axis=1, keepdims=True) for x in chance)
    numer = mm(chance[0].astype(bf16), cv_ref[...], NN) + mm(
        chance[1].astype(bf16), other_v[...], NN
    )
    lane = lax.broadcasted_iota(jnp.int32, (DH, DH), 1)
    both = jnp.where(lane < 64, jnp.broadcast_to(peak, (DH, DH)), jnp.broadcast_to(amount, (DH, DH)))
    send_soft[:, 0:8, :] = numer.reshape(SEQ, 8, DH)
    send_soft[:, 8:16, :] = both.reshape(SEQ, 8, DH)
    seq_start(S_SOFT, src_soft, recv_soft)
    recv_soft[me] = send_soft[me]

    seq_wait(S_STATE, src_state, recv_state)
    running = jnp.zeros((HALF, DH), f32)
    for j in range(SEQ):
        carry[j] = running
        send_back[j] = running.astype(bf16)
        rows = recv_state[j, HALF:, :].astype(f32)
        running = expand(rows[0:4] + rows[8:12]) * running + recv_state[j, 0:HALF, :].astype(f32)
    carry[SEQ] = running
    seq_start(S_BACK, src_back, recv_back)
    recv_back[me] = send_back[me]

    inside_loop(1, 3)

    seq_wait(S_SLOTS, src_slots, recv_slots)
    for p in range(DOCS):
        last_page = jnp.clip(ends[p] - 1, 0, 2 * PAGES_DEV * SEQ - 1)
        chip = lax.shift_right_logical(last_page, 3)
        chip_last = jnp.bitwise_and(last_page, 7) == 7
        rank = sum(
            [flag(lax.shift_right_logical(ends[o] - 1, 3) == chip) for o in range(p)],
            jnp.int32(0),
        )
        rows = recv_state[chip][HALF:, :].astype(f32)
        w = expand(rows[4:8] + rows[12:16]) * jnp.where(rank == 0, 1.0, 0.0).astype(f32)
        ended = recv_slots[chip, jnp.minimum(rank, 1)].astype(f32) + w * carry[chip]
        final = lax.select(chip_last, carry[chip + 1], ended)
        final_all[p, own_rows, :] = final
        pair_final[p] = final.astype(bf16)
    pair_copy(P_FINAL, pair_final, pair_final_in).start()

    inside_loop(3, 4)

    seq_wait(S_BACK, src_back, recv_back)
    carry0 = recv_back[...].astype(f32)
    carry1 = expand(w0[0])[None] * carry0 + state0
    carry_all[:, own_rows, :] = lax.select(first_core, carry0, carry1)
    pair_carry[...] = lax.select(first_core, carry1, carry0).astype(bf16)
    pair_copy(P_CARRY, pair_carry, pair_carry_in).start()

    seq_wait(S_SOFT, src_soft, recv_soft)
    doc = me // STEPS
    step = lax.rem(me, STEPS)
    own_q = sfq[pl.ds(pl.multiple_of(me * 8, 8), 8), :]
    own_k = sfk[doc]
    own_v = sfv[doc]
    peaks = [recv_soft[s, 8:16, 0:1] for s in range(SEQ)]
    amounts = [recv_soft[s, 8:16, 64:65] for s in range(SEQ)]
    numers = [recv_soft[s, 0:8, :] for s in range(SEQ)]
    top = peaks[0]
    for x in peaks[1:]:
        top = jnp.maximum(top, x)
    own = []
    for i in range(STEPS):
        s = jnp.sum(own_q * own_k[i : i + 1, :], axis=1, keepdims=True) * scale
        own.append(lax.select(step >= i, s, jnp.full((8, 1), mask_low, f32)))
        top = jnp.maximum(top, own[-1])
    numer = jnp.zeros((8, DH), f32)
    amount = jnp.zeros((8, 1), f32)
    for s in range(SEQ):
        shrink = jnp.exp2(peaks[s] - top)
        numer = numer + numers[s] * shrink
        amount = amount + amounts[s] * shrink
    for i in range(STEPS):
        e = lax.select(step >= i, jnp.exp2(own[i] - top), jnp.zeros((8, 1), f32))
        numer = numer + e.astype(bf16).astype(f32) * own_v[i : i + 1, :]
        amount = amount + e
    send_gather[0:8, :] = numer / amount

    pair_copy(P_FINAL, pair_final, pair_final_in).wait_recv()
    final_all[:, other_rows, :] = pair_final_in[...].astype(f32)
    t16 = lax.broadcasted_iota(jnp.int32, (16, 16), 0)
    s16 = lax.broadcasted_iota(jnp.int32, (16, 16), 1)
    chain = jnp.logical_and(t16 // STEPS == s16 // STEPS, t16 >= s16)
    chain_t = jnp.logical_and(t16 // STEPS == s16 // STEPS, t16 <= s16)
    fall = std[...] * LOG2E
    fall_col = mm(chain.astype(f32), fall, NN, highest)
    fall_row = mm(fall, chain_t.astype(f32), TN, highest)
    f128 = lax.broadcasted_iota(jnp.int32, (DH, 8), 0)
    c128 = lax.broadcasted_iota(jnp.int32, (DH, 8), 1)
    pick = (f128 == c128 + me * 8).astype(f32)
    r32 = lax.broadcasted_iota(jnp.int32, (32, 8), 0)
    c32 = lax.broadcasted_iota(jnp.int32, (32, 8), 1)
    fold = (jnp.bitwise_and(r32, 7) == c32).astype(f32)
    t32 = lax.broadcasted_iota(jnp.int32, (16, 32), 0)
    p32 = lax.broadcasted_iota(jnp.int32, (16, 32), 1)
    same = t32 // STEPS == p32 // 8
    squares = jnp.zeros((16, 8), f32)
    for h in range(HEADS):
        q = stq[:, head_cols(h)]
        k = stk[:, head_cols(h)]
        v = mm(stv[:, head_cols(h)], pick, NN, highest)
        spread = jnp.exp2(fall_col[:, h : h + 1] - fall_row[h : h + 1, :])
        grid = jnp.where(chain, mm(q, k, NT, highest) * spread, 0.0)
        final = final_all[:, h * 8 : h * 8 + 8, :].reshape(32, DH)
        read = jnp.where(same, mm(q, final, NT, highest), 0.0)
        value = mm(read, fold, NN, highest) * jnp.exp2(fall_col[:, h : h + 1])
        value = value + mm(grid, v, NN, highest)
        dec_own[h] = value
        squares = squares + value * value
    send_gather[8:24, :] = mm(squares, jnp.ones((8, DH), f32), NN, highest)
    seq_start(S_GATHER, src_gather, recv_gather)
    recv_gather[me] = send_gather[...]

    pair_copy(P_CARRY, pair_carry, pair_carry_in).wait_recv()
    carry_all[:, other_rows, :] = pair_carry_in[...].astype(f32)

    lines = []
    for k in range(PAGES_DEV):
        rows = slice(k * PAGE, (k + 1) * PAGE)
        rise = jnp.exp2(ccol[rows, :])
        cont = goes_on(dev_page + k)
        w = before[k]
        squares = jnp.zeros((PAGE, DH), f32)
        for h in range(HEADS):
            part = slice(h * 8, h * 8 + 8)
            state = states[k, :, part, :] * cont + carry_all[:, part, :] * w[h : h + 1, :][None]
            qd = (q_ref[rows, head_cols(h)].astype(f32) * rise[:, h : h + 1]).astype(bf16)
            value = mixed[rows, head_cols(h)] + mm(qd, state.reshape(DH, DH).astype(bf16), NT)
            mixed[rows, head_cols(h)] = value
            squares = squares + value * value
        lines.append(mm(jnp.ones((8, DH), f32), squares, NT, highest))

    seq_wait(S_GATHER, src_gather, recv_gather)
    seq_sent(S_GATHER, src_gather, recv_gather)
    decode_squares = jnp.zeros((16, DH), f32)
    for s in range(SEQ):
        soft_ref[s] = recv_gather[s, 0:8, :]
        decode_squares = decode_squares + recv_gather[s, 8:24, :]
    for k in range(PAGES_DEV):
        for n in range(PAGE // DH):
            send_gather[2 * k + n : 2 * k + n + 1, :] = lines[k][0:1, head_cols(n)]
    send_gather[8:24, :] = decode_squares

    def tp_start(hop, _):
        tp_copy(hop).start()
        return 0

    lax.fori_loop(1, TP, tp_start, 0)
    recv_tp[tp] = send_gather[...]

    def tp_wait(hop, _):
        source = lax.rem(tp + TP - hop, TP)
        pltpu.make_async_remote_copy(
            src_ref=send_gather, dst_ref=recv_tp.at[source],
            send_sem=tp_send.at[hop], recv_sem=tp_recv.at[hop],
            device_id=(me, source, rep), device_id_type=MESH,
        ).wait_recv()
        return 0

    lax.fori_loop(1, TP, tp_wait, 0)

    features = TP * HEADS * DH
    inputs["gain"].wait()
    gain = gain_ref[...]
    total_squares = recv_tp[0, 8:24, :]
    for t in range(1, TP):
        total_squares = total_squares + recv_tp[t, 8:24, :]
    factor = lax.rsqrt(total_squares / features + norm_eps)[:, 0:8]
    gain_cols = mm(gain, pick, NN, highest)
    for h in range(HEADS):
        dec_ref[h] = dec_own[h] * factor * gain_cols[h : h + 1, :]
    ones = jnp.ones((TP, DH), f32)
    for b in range(ROWS // DH):
        total = mm(recv_tp[:, b, :], ones, TN, highest)
        factor = lax.rsqrt(total / features + norm_eps)
        rows = slice(b * DH, (b + 1) * DH)
        for h in range(HEADS):
            out_ref[rows, head_cols(h)] = (
                mixed[rows, head_cols(h)] * factor * gain[h : h + 1, :]
            ).astype(bf16)

    for which, src, dst in (
        (P_KEYS, ck_in, other_k),
        (P_VALUES, cv_in, other_v),
        (P_STATE, pair_state, pair_state_in),
        (P_WEIGHT, pair_weight, pair_weight_in),
        (P_SLOTS, pair_other, pair_slots_in),
        (P_CARRY, pair_carry, pair_carry_in),
        (P_FINAL, pair_final, pair_final_in),
    ):
        pair_copy(which, src, dst).wait_send()
    seq_sent(S_STATE, src_state, recv_state)
    seq_sent(S_SLOTS, src_slots, recv_slots)
    seq_sent(S_SOFT, src_soft, recv_soft)
    seq_sent(S_BACK, src_back, recv_back)

    def tp_sent(hop, _):
        tp_copy(hop).wait_send()
        return 0

    lax.fori_loop(1, TP, tp_sent, 0)


def per_device(
    light_query, light_key, light_value, log_decay, prompt_pages, norm_gain, cache_keys,
    cache_values, step_query, step_key, step_value, step_decay, soft_query, soft_key, soft_value,
):
    vm = pl.BlockSpec(memory_space=pltpu.VMEM)
    V = pltpu.VMEM
    D = pltpu.SemaphoreType.DMA
    out, dec, soft = pl.pallas_call(
        kernel,
        out_shape=(
            jax.ShapeDtypeStruct((ROWS, HEADS * DH), bf16),
            jax.ShapeDtypeStruct((HEADS, 16, 8), f32),
            jax.ShapeDtypeStruct((SEQ, 8, DH), f32),
        ),
        in_specs=[pl.BlockSpec(memory_space=pltpu.HBM)] * 15,
        out_specs=(vm, vm, vm),
        scratch_shapes=[
            pltpu.SMEM((DOCS,), jnp.int32),
            V((ROWS, HEADS * DH), bf16),
            V((ROWS, HEADS * DH), bf16),
            V((ROWS, HEADS * DH), bf16),
            V((HEADS, ROWS), f32),
            V((HEADS, DH), f32),
            V((ROWS, DH), bf16),
            V((ROWS, DH), bf16),
            V((DOCS, STEPS, HEADS * DH), bf16),
            V((DOCS, STEPS, HEADS * DH), bf16),
            V((DOCS, STEPS, HEADS * DH), bf16),
            V((DOCS, STEPS, HEADS), f32),
            V((DOCS, STEPS, HEADS * DH), bf16),
            V((DOCS, STEPS, DH), bf16),
            V((DOCS, STEPS, DH), bf16),
            V((ROWS, HEADS * DH), f32),
            V((ROWS, HEADS), f32),
            V((PAGES_DEV, HEADS, PAGE), f32),
            V((PAGES_DEV + 1, SEQ, 2 * HALF, DH), f32),
            V((PAGES_DEV, HEADS, DH), f32),
            V((PAGES_DEV, HEADS, DH), f32),
            V((16, HEADS * DH), f32),
            V((16, HEADS * DH), f32),
            V((16, HEADS * DH), f32),
            V((16, HEADS), f32),
            V((DH, DH), f32),
            V((DOCS, STEPS, DH), f32),
            V((DOCS, STEPS, DH), f32),
            V((ROWS, DH), bf16),
            V((ROWS, DH), bf16),
            V((SEQ, HALF, DH), bf16),
            V((SEQ, HALF, DH), bf16),
            V((24, DH), f32),
            V((24, DH), f32),
            V((4, SEQ, HALF, DH), bf16),
            V((2, SEQ, HALF, DH), bf16),
            V((SEQ, HALF + 16, DH), bf16),
            V((SEQ, HALF + 16, DH), bf16),
            V((SEQ, 2, HALF, DH), bf16),
            V((SEQ, 2, HALF, DH), bf16),
            V((SEQ, 16, DH), f32),
            V((SEQ, 16, DH), f32),
            V((SEQ + 1, HALF, DH), f32),
            V((SEQ, HALF, DH), bf16),
            V((SEQ, HALF, DH), bf16),
            V((SEQ, HALF, DH), bf16),
            V((SEQ, HALF, DH), bf16),
            V((SEQ, 2 * HALF, DH), f32),
            V((DOCS, HALF, DH), bf16),
            V((DOCS, HALF, DH), bf16),
            V((DOCS, 2 * HALF, DH), f32),
            V((HEADS, 16, 8), f32),
            V((24, DH), f32),
            V((SEQ, 24, DH), f32),
            V((TP, 24, DH), f32),
            D((7,)),
            D((7,)),
            D((5, SEQ)),
            D((5, SEQ)),
            D((TP,)),
            D((TP,)),
            D((21,)),
        ],
        compiler_params=pltpu.CompilerParams(
            collective_id=0, has_side_effects=True, vmem_limit_bytes=48 * 1024 * 1024
        ),
        name="attention_block",
    )(*[pltpu.with_memory_space_constraint(x, pltpu.HBM) for x in (
        prompt_pages, light_query, light_key, light_value, log_decay.T,
        norm_gain.reshape(HEADS, DH), cache_keys, cache_values,
        step_query, step_key, step_value, step_decay, soft_query, soft_key, soft_value,
    )])
    light_decode = dec.reshape(HEADS, DOCS, STEPS, 8).transpose(1, 2, 0, 3).astype(bf16)[None]
    soft_decode = soft.reshape(1, DOCS, STEPS, HEADS * DH).astype(bf16)
    return out, light_decode, soft_decode


def solution(mesh):
    prompt = P(("seq", "rep"), "tp")
    sample = P("rep", None, None, "tp")
    return jax.shard_map(
        per_device,
        mesh=mesh,
        in_specs=(prompt,) * 4 + (P(), P("tp")) + (prompt,) * 2 + (sample,) * 7,
        out_specs=(prompt, P("rep", None, None, "tp", "seq"), sample),
        check_vma=False,
    )
```

```python
import math

import jax
import jax.numpy as jnp
from jax import lax
from jax.experimental import pallas as pl
from jax.experimental.pallas import tpu as pltpu
from jax.sharding import PartitionSpec as P

DH = 128
PAGE = 256
DOCS = 4
STEPS = 4
HEADS = 8
SEQ = 16
TP = 8
ROWS = 1024
PAGES_DEV = ROWS // PAGE
HALF = HEADS // 2 * 8

norm_eps = 1e-06
mask_low = -1e30
LOG2E = math.log2(math.e)
highest = lax.Precision.HIGHEST
f32 = jnp.float32
bf16 = jnp.bfloat16
MESH = pl.DeviceIdType.MESH

NN = (((1,), (0,)), ((), ()))
NT = (((1,), (1,)), ((), ()))
TN = (((0,), (0,)), ((), ()))

P_KEYS, P_VALUES, P_STATE, P_WEIGHT, P_SLOTS, P_CARRY, P_FINAL = range(7)
S_STATE, S_SLOTS, S_SOFT, S_BACK, S_RESULT, S_DECODE = range(6)


def mm(a, b, dims, precision=None):
    return lax.dot_general(a, b, dims, precision=precision, preferred_element_type=f32)


def head_cols(h):
    return slice(h * DH, (h + 1) * DH)


def expand(rows):
    return jnp.concatenate(
        [jnp.broadcast_to(rows[i : i + 1], (8, DH)) for i in range(HEADS // 2)], axis=0
    )


def kernel(
    pages_in, q_in, k_in, v_in, g_in, gain_in, ck_in, cv_in,
    stq_in, stk_in, stv_in, std_in, sfq_in, sfk_in, sfv_in,
    mixed, sums_ref, dec_own, soft_ref, gain_ref,
    pages_ref, q_ref, k_ref, v_ref, g_ref, ck_ref, cv_ref,
    stq_ref, stk_ref, stv_ref, std_ref, sfq_ref, sfk_ref, sfv_ref,
    ccol, crow, states, before, weights, stq, stk, stv, std, sfq, sfk, sfv,
    other_k, other_v,
    pair_state, pair_state_in, pair_weight, pair_weight_in, pair_slots, pair_slots_in,
    send_state, recv_state, send_slots, recv_slots, send_soft, recv_soft,
    carry, send_back, recv_back, pair_carry, pair_carry_in, carry_all,
    pair_final, pair_final_in, final_all, send_result, recv_result, send_decode, recv_decode, send_tp,
    pair_send, pair_recv, seq_send, seq_recv, tp_send, tp_recv, in_sem,
):
    me = lax.axis_index("seq")
    tp = lax.axis_index("tp")
    rep = lax.axis_index("rep")
    first_core = rep == 0
    own_rows = pl.ds(pl.multiple_of(rep * HALF, HALF), HALF)
    other_rows = pl.ds(pl.multiple_of((1 - rep) * HALF, HALF), HALF)

    def page_rows(k):
        return pl.ds(k * PAGE, PAGE)

    inputs = {}

    def fetch(name, src, dst):
        inputs[name] = pltpu.make_async_copy(src, dst, in_sem.at[len(inputs)])
        inputs[name].start()

    fetch("pages", pages_in, pages_ref)
    fetch("g", g_in, g_ref)
    for k in range(PAGES_DEV):
        fetch(("k", k), k_in.at[page_rows(k)], k_ref.at[page_rows(k)])
        fetch(("v", k), v_in.at[page_rows(k)], v_ref.at[page_rows(k)])
    fetch("q", q_in, q_ref)
    fetch("ck", ck_in, ck_ref)
    fetch("cv", cv_in, cv_ref)
    small = (
        (stq_in, stq_ref), (stk_in, stk_ref), (stv_in, stv_ref), (std_in, std_ref),
        (sfq_in, sfq_ref), (sfk_in, sfk_ref), (sfv_in, sfv_ref),
    )
    for n, (src, dst) in enumerate(small):
        fetch(("small", n), src.at[0], dst)
    fetch("gain", gain_in, gain_ref)

    def pair_copy(which, src, dst):
        return pltpu.make_async_remote_copy(
            src_ref=src, dst_ref=dst, send_sem=pair_send.at[which], recv_sem=pair_recv.at[which],
            device_id=(me, tp, 1 - rep), device_id_type=MESH,
        )

    def seq_copy(phase, src, dst, hop):
        target = lax.rem(me + hop, SEQ)
        return pltpu.make_async_remote_copy(
            src_ref=src(target), dst_ref=dst.at[me],
            send_sem=seq_send.at[phase, hop], recv_sem=seq_recv.at[phase, hop],
            device_id=(target, tp, rep), device_id_type=MESH,
        )

    def seq_start(phase, src, dst):
        for hop in range(1, SEQ):
            seq_copy(phase, src, dst, hop).start()

    def seq_wait(phase, src, dst):
        for hop in range(1, SEQ):
            source = lax.rem(me + SEQ - hop, SEQ)
            pltpu.make_async_remote_copy(
                src_ref=src(source), dst_ref=dst.at[source],
                send_sem=seq_send.at[phase, hop], recv_sem=seq_recv.at[phase, hop],
                device_id=(source, tp, rep), device_id_type=MESH,
            ).wait_recv()

    def seq_sent(phase, src, dst):
        for hop in range(1, SEQ):
            seq_copy(phase, src, dst, hop).wait_send()

    src_state = lambda t: send_state.at[t]
    src_slots = lambda t: send_slots.at[t]
    src_soft = lambda t: send_soft.at[t]
    src_back = lambda t: send_back.at[t]
    src_result = lambda t: send_result
    src_decode = lambda t: send_decode

    def tp_copy(hop):
        return pltpu.make_async_remote_copy(
            src_ref=send_tp, dst_ref=sums_ref.at[tp],
            send_sem=tp_send.at[hop], recv_sem=tp_recv.at[hop],
            device_id=(me, lax.rem(tp + hop, TP), rep), device_id_type=MESH,
        )

    barrier = pltpu.get_barrier_semaphore()

    for hop in range(1, SEQ):
        pl.semaphore_signal(
            barrier, inc=1, device_id=(lax.rem(me + hop, SEQ), tp, rep), device_id_type=MESH
        )
    for hop in range(1, TP):
        pl.semaphore_signal(
            barrier, inc=1, device_id=(me, lax.rem(tp + hop, TP), rep), device_id_type=MESH
        )
    pl.semaphore_signal(barrier, inc=1, device_id=(me, tp, 1 - rep), device_id_type=MESH)

    inputs["pages"].wait()
    ends = []
    for p in range(DOCS):
        ends.append(pages_ref[p] + (ends[-1] if ends else 0))
    chip_page = me * (2 * PAGES_DEV)
    dev_page = chip_page + rep * PAGES_DEV

    def flag(cond):
        return jnp.where(cond, 1, 0).astype(jnp.int32)

    def goes_on(page):
        hits = sum(flag(e == page) for e in ends)
        return jnp.where(hits == 0, 1.0, 0.0).astype(f32)

    def doc_of(page):
        return sum((e <= page).astype(jnp.int32) for e in ends)

    slot_page, slot_valid = [], []
    inside = [flag(jnp.logical_and(e > chip_page, e < chip_page + 2 * PAGES_DEV)) for e in ends]
    for s in range(2):
        place = 0
        for p in range(DOCS):
            rank = sum(inside[:p]) if p else 0
            place = place + inside[p] * flag(rank == s) * (ends[p] - chip_page)
        local = place - 1 - rep * PAGES_DEV
        ok = jnp.logical_and(
            place > 0, jnp.logical_and(local >= 0, local < PAGES_DEV)
        )
        slot_page.append(jnp.clip(local, 0, PAGES_DEV - 1))
        slot_valid.append(jnp.where(ok, 1.0, 0.0).astype(f32))

    rows_i = lax.broadcasted_iota(jnp.int32, (PAGE, PAGE), 0)
    cols_i = lax.broadcasted_iota(jnp.int32, (PAGE, PAGE), 1)
    states[0] = jnp.zeros((SEQ, 2 * HALF, DH), f32)

    inputs["g"].wait()
    g = g_ref[...] * LOG2E
    g_high = g.astype(bf16)
    g_rest = g - g_high.astype(f32)
    g_mid = g_rest.astype(bf16)
    g_low = (g_rest - g_mid.astype(f32)).astype(bf16)
    upper = (rows_i <= cols_i).astype(f32).astype(bf16)
    parts = [
        x[:, k * PAGE : (k + 1) * PAGE].astype(f32)
        for x in (g_high, g_mid, g_low)
        for k in range(PAGES_DEV)
    ]
    summed = mm(jnp.concatenate(parts, axis=0).astype(bf16), upper, NN)
    wide = PAGES_DEV * HEADS
    summed = summed[0:wide] + summed[wide : 2 * wide] + summed[2 * wide :]
    turned = jnp.transpose(summed)

    def state_page(k, carried):
        rows = page_rows(k)
        c = turned[:, k * HEADS : (k + 1) * HEADS]
        ccol[rows, :] = c
        line = summed[k * HEADS : (k + 1) * HEADS]
        crow[k] = line
        decay = jnp.exp2(jnp.broadcast_to(line[:, PAGE - 1 : PAGE], (HEADS, DH)))
        cont = goes_on(dev_page + k)
        before[k] = carried * cont
        keep = decay * cont
        after = carried * keep
        weights[k] = after
        fade = jnp.exp2(c[PAGE - 1 : PAGE, :] - c)
        for h in range(HEADS):
            kd = (k_ref[rows, head_cols(h)].astype(f32) * fade[:, h : h + 1]).astype(bf16)
            add = mm(v_ref[rows, head_cols(h)], kd, TN)
            old = states[k, :, h * 8 : h * 8 + 8, :]
            states[k + 1, :, h * 8 : h * 8 + 8, :] = old * keep[h : h + 1, :][None] + add.reshape(
                SEQ, 8, DH
            )
        return after

    total = jnp.ones((HEADS, DH), f32)
    for k in range(PAGES_DEV):
        inputs[("k", k)].wait()
        inputs[("v", k)].wait()
        total = state_page(k, total)

    pl.semaphore_wait(barrier, SEQ - 1 + TP - 1 + 1)
    pair_state[...] = states[PAGES_DEV, :, other_rows, :].astype(bf16)
    pair_weight[0:8] = total
    for s in range(2):
        w = jnp.zeros((HEADS, DH), f32)
        for k in range(PAGES_DEV):
            pick = jnp.where(slot_page[s] == k, slot_valid[s], 0.0).astype(f32)
            w = w + pick * weights[k]
        pair_weight[8 + 8 * s : 16 + 8 * s] = w
    pair_copy(P_STATE, pair_state, pair_state_in).start()
    pair_copy(P_WEIGHT, pair_weight, pair_weight_in).start()
    for s in range(2):
        pair_slots[s] = (states[slot_page[s] + 1][:, 0:HALF, :] * slot_valid[s]).astype(bf16)
        pair_slots[2 + s] = (states[slot_page[s] + 1][:, HALF:, :] * slot_valid[s]).astype(bf16)
    pair_other = pair_slots.at[pl.ds((1 - rep) * 2, 2)]
    pair_copy(P_SLOTS, pair_other, pair_slots_in).start()
    pair_copy(P_KEYS, ck_in, other_k).start()
    pair_copy(P_VALUES, cv_in, other_v).start()

    causal = rows_i >= cols_i

    def inside_page(k):
        rows = pl.ds(pl.multiple_of(k * PAGE, PAGE), PAGE)
        c = ccol[rows, :]
        r = crow[k]
        for h in range(HEADS):
            scores = mm(q_ref[rows, head_cols(h)], k_ref[rows, head_cols(h)], NT)
            grid = jnp.exp2(c[:, h : h + 1] - r[h : h + 1, :])
            block = jnp.where(causal, scores * grid, 0.0).astype(bf16)
            mixed[rows, head_cols(h)] = mm(block, v_ref[rows, head_cols(h)], NN)

    def inside_loop(first, last):
        def one(k, _):
            inside_page(k)
            return 0

        lax.fori_loop(first, last, one, 0)

    inputs["q"].wait()
    inside_loop(0, 1)

    def half(x):
        return lax.select(first_core, x[0:4], x[4:8])

    pair_copy(P_STATE, pair_state, pair_state_in).wait_recv()
    pair_copy(P_WEIGHT, pair_weight, pair_weight_in).wait_recv()
    own_state = states[PAGES_DEV, :, own_rows, :]
    got_state = pair_state_in[...].astype(f32)
    state0 = lax.select(first_core, own_state, got_state)
    state1 = lax.select(first_core, got_state, own_state)
    own_w = [half(pair_weight[8 * n : 8 * n + 8]) for n in range(3)]
    got_w = [half(pair_weight_in[8 * n : 8 * n + 8]) for n in range(3)]
    w0 = [lax.select(first_core, a, b) for a, b in zip(own_w, got_w)]
    w1 = [lax.select(first_core, b, a) for a, b in zip(own_w, got_w)]
    chip_state = expand(w1[0])[None] * state0 + state1
    chip_w = jnp.concatenate([w1[0] * w0[0], w0[1] + w1[1] * w0[0]], axis=0)
    chip_hi = chip_w.astype(bf16).astype(f32)
    chip_rows = jnp.concatenate([chip_hi, chip_w - chip_hi], axis=0).astype(bf16)
    send_state[:, 0:HALF, :] = chip_state.astype(bf16)
    send_state[:, HALF:, :] = jnp.broadcast_to(chip_rows[None], (SEQ, 16, DH))
    seq_start(S_STATE, src_state, recv_state)
    recv_state[me] = send_state[me]

    pair_copy(P_SLOTS, pair_other, pair_slots_in).wait_recv()
    for s in range(2):
        own_slot = states[slot_page[s] + 1][:, 0:HALF, :]
        own_slot = lax.select(first_core, own_slot, states[slot_page[s] + 1][:, HALF:, :])
        slot = own_slot * slot_valid[s] + pair_slots_in[s].astype(f32)
        slot = slot + expand(w1[1 + s])[None] * state0
        send_slots[:, s] = slot.astype(bf16)
    seq_start(S_SLOTS, src_slots, recv_slots)
    recv_slots[me] = send_slots[me]

    for n in range(len(small)):
        inputs[("small", n)].wait()
    inputs["ck"].wait()
    inputs["cv"].wait()
    for p in range(DOCS):
        part = slice(4 * p, 4 * p + 4)
        stq[part, :] = stq_ref[p].astype(f32)
        stk[part, :] = stk_ref[p].astype(f32)
        stv[part, :] = stv_ref[p].astype(f32)
        std[part, :] = std_ref[p]
        sfk[p] = sfk_ref[p].astype(f32)
        sfv[p] = sfv_ref[p].astype(f32)
        for h in range(HEADS):
            sfq[pl.ds(p * 32 + h, 4, stride=8), :] = sfq_ref[p, :, head_cols(h)].astype(f32)

    scale = DH**-0.5 * LOG2E
    pair_copy(P_KEYS, ck_in, other_k).wait_recv()
    pair_copy(P_VALUES, cv_in, other_v).wait_recv()
    queries = sfq[...].astype(bf16)
    query_doc = lax.broadcasted_iota(jnp.int32, (DH, ROWS), 0) // 32
    key_page = lax.broadcasted_iota(jnp.int32, (1, ROWS), 1) // PAGE
    score, here = [], []
    for base, key_block in ((dev_page, ck_ref), (chip_page + (1 - rep) * PAGES_DEV, other_k)):
        score.append(mm(queries, key_block[...], NT) * scale)
        here.append(query_doc == jnp.broadcast_to(doc_of(key_page + base), (DH, ROWS)))
    peak = jnp.maximum(
        *[
            jnp.max(jnp.where(m, s, mask_low), axis=1, keepdims=True)
            for m, s in zip(here, score)
        ]
    )
    chance = [jnp.where(m, jnp.exp2(s - peak), 0.0) for m, s in zip(here, score)]
    amount = sum(jnp.sum(x, axis=1, keepdims=True) for x in chance)
    numer = mm(chance[0].astype(bf16), cv_ref[...], NN) + mm(
        chance[1].astype(bf16), other_v[...], NN
    )
    lane = lax.broadcasted_iota(jnp.int32, (DH, DH), 1)
    both = jnp.where(lane < 64, jnp.broadcast_to(peak, (DH, DH)), jnp.broadcast_to(amount, (DH, DH)))
    send_soft[:, 0:8, :] = numer.reshape(SEQ, 8, DH)
    send_soft[:, 8:16, :] = both.reshape(SEQ, 8, DH)
    seq_start(S_SOFT, src_soft, recv_soft)
    recv_soft[me] = send_soft[me]

    seq_wait(S_STATE, src_state, recv_state)
    running = jnp.zeros((HALF, DH), f32)
    for j in range(SEQ):
        carry[j] = running
        send_back[j] = running.astype(bf16)
        rows = recv_state[j, HALF:, :].astype(f32)
        running = expand(rows[0:4] + rows[8:12]) * running + recv_state[j, 0:HALF, :].astype(f32)
    carry[SEQ] = running
    seq_start(S_BACK, src_back, recv_back)
    recv_back[me] = send_back[me]

    seq_wait(S_SLOTS, src_slots, recv_slots)
    for p in range(DOCS):
        last_page = jnp.clip(ends[p] - 1, 0, 2 * PAGES_DEV * SEQ - 1)
        chip = lax.shift_right_logical(last_page, 3)
        chip_last = jnp.bitwise_and(last_page, 7) == 7
        rank = sum(
            [flag(lax.shift_right_logical(ends[o] - 1, 3) == chip) for o in range(p)],
            jnp.int32(0),
        )
        rows = recv_state[chip][HALF:, :].astype(f32)
        w = expand(rows[4:8] + rows[12:16]) * jnp.where(rank == 0, 1.0, 0.0).astype(f32)
        ended = recv_slots[chip, jnp.minimum(rank, 1)].astype(f32) + w * carry[chip]
        final = lax.select(chip_last, carry[chip + 1], ended)
        final_all[p, own_rows, :] = final
        pair_final[p] = final.astype(bf16)
    pair_copy(P_FINAL, pair_final, pair_final_in).start()

    def iota(shape, dim):
        return lax.broadcasted_iota(jnp.int32, shape, dim)

    chain = jnp.logical_and(
        iota((16, 16), 0) // STEPS == iota((16, 16), 1) // STEPS, iota((16, 16), 0) >= iota((16, 16), 1)
    )
    fall = mm(chain.astype(f32), std[...] * LOG2E, NN, highest)
    spread_heads = (iota((HEADS, DH), 1) // 16 == iota((HEADS, DH), 0)).astype(f32)
    fall_from = mm(fall, spread_heads, NN, highest)
    lane_step = jnp.bitwise_and(iota((16, DH), 1), 15)
    diagonal = jnp.where(lane_step == iota((16, DH), 0), fall_from, 0.0)
    fall_to = mm(jnp.ones((16, 16), f32), diagonal, NN, highest)
    linked = jnp.logical_and(
        iota((16, DH), 0) // STEPS == lane_step // STEPS, iota((16, DH), 0) >= lane_step
    )
    met = jnp.concatenate(
        [
            mm(stq[:, head_cols(h)].astype(bf16), stk[:, head_cols(h)].astype(bf16), NT)
            for h in range(HEADS)
        ],
        axis=1,
    )
    met = jnp.where(linked, met * jnp.exp2(fall_from - fall_to), 0.0)
    cols = HEADS * 8
    pick = (iota((DH, cols), 0) == jnp.bitwise_and(iota((DH, cols), 1), 7) + me * 8).astype(f32)
    values = jnp.concatenate([stv[:, head_cols(h)] for h in range(HEADS)], axis=0)
    values = mm(values.astype(bf16), pick.astype(bf16), NN)
    values = jnp.where(iota((DH, cols), 0) // 16 == iota((DH, cols), 1) // 8, values, 0.0)
    decoded = mm(met, values, NN, highest)
    spread_cols = (iota((HEADS, cols), 1) // 8 == iota((HEADS, cols), 0)).astype(f32)
    shrunk = jnp.exp2(mm(fall, spread_cols, NN, highest))
    wide = HEADS * HALF
    fold = jnp.logical_and(
        iota((wide, cols), 0) // HALF == iota((wide, cols), 1) // 8,
        jnp.bitwise_and(iota((wide, cols), 0), 7) == jnp.bitwise_and(iota((wide, cols), 1), 7),
    ).astype(f32).astype(bf16)
    same = jnp.bitwise_and(iota((16, wide), 1), HALF - 1) // 8 == iota((16, wide), 0) // STEPS

    inside_loop(1, 2)

    pair_copy(P_FINAL, pair_final, pair_final_in).wait_recv()
    final_all[:, other_rows, :] = pair_final_in[...].astype(f32)
    read = jnp.concatenate(
        [
            mm(
                stq[:, head_cols(h)].astype(bf16),
                final_all[:, h * 8 : h * 8 + 8, :].reshape(DOCS * 8, DH).astype(bf16),
                NT,
            )
            for h in range(HEADS)
        ],
        axis=1,
    )
    read = jnp.where(same, read, 0.0)
    read_high = read.astype(bf16)
    read_low = (read - read_high.astype(f32)).astype(bf16)
    read = mm(read_high, fold, NN) + mm(read_low, fold, NN)
    decoded = decoded + read * shrunk
    dec_own[...] = decoded
    squares = mm(jnp.ones((8, cols), f32), decoded * decoded, NT, highest)
    send_decode[...] = jnp.zeros((1, DH), f32)
    send_decode[:, 0:16] = squares[0:1, :]
    seq_start(S_DECODE, src_decode, recv_decode)
    recv_decode[me] = send_decode[...]

    seq_wait(S_SOFT, src_soft, recv_soft)
    doc = me // STEPS
    step = lax.rem(me, STEPS)
    own_q = sfq[pl.ds(pl.multiple_of(me * 8, 8), 8), :]
    own_k = sfk[doc]
    own_v = sfv[doc]
    peaks = [recv_soft[s, 8:16, 0:1] for s in range(SEQ)]
    amounts = [recv_soft[s, 8:16, 64:65] for s in range(SEQ)]
    numers = [recv_soft[s, 0:8, :] for s in range(SEQ)]
    top = peaks[0]
    for x in peaks[1:]:
        top = jnp.maximum(top, x)
    own = []
    for i in range(STEPS):
        s = jnp.sum(own_q * own_k[i : i + 1, :], axis=1, keepdims=True) * scale
        own.append(lax.select(step >= i, s, jnp.full((8, 1), mask_low, f32)))
        top = jnp.maximum(top, own[-1])
    numer = jnp.zeros((8, DH), f32)
    amount = jnp.zeros((8, 1), f32)
    for s in range(SEQ):
        shrink = jnp.exp2(peaks[s] - top)
        numer = numer + numers[s] * shrink
        amount = amount + amounts[s] * shrink
    for i in range(STEPS):
        e = lax.select(step >= i, jnp.exp2(own[i] - top), jnp.zeros((8, 1), f32))
        numer = numer + e.astype(bf16).astype(f32) * own_v[i : i + 1, :]
        amount = amount + e
    send_result[...] = numer / amount
    seq_start(S_RESULT, src_result, recv_result)
    recv_result[me] = send_result[...]

    inside_loop(2, 3)

    seq_wait(S_BACK, src_back, recv_back)
    carry0 = recv_back[...].astype(f32)
    carry1 = expand(w0[0])[None] * carry0 + state0
    carry_all[:, own_rows, :] = lax.select(first_core, carry0, carry1)
    pair_carry[...] = lax.select(first_core, carry1, carry0).astype(bf16)
    pair_copy(P_CARRY, pair_carry, pair_carry_in).start()

    inside_loop(3, 4)

    pair_copy(P_CARRY, pair_carry, pair_carry_in).wait_recv()
    carry_all[:, other_rows, :] = pair_carry_in[...].astype(f32)

    lines = []
    for k in range(PAGES_DEV):
        rows = slice(k * PAGE, (k + 1) * PAGE)
        rise = jnp.exp2(ccol[rows, :])
        cont = goes_on(dev_page + k)
        w = before[k]
        squares = jnp.zeros((PAGE, DH), f32)
        for h in range(HEADS):
            part = slice(h * 8, h * 8 + 8)
            state = states[k, :, part, :] * cont + carry_all[:, part, :] * w[h : h + 1, :][None]
            qd = (q_ref[rows, head_cols(h)].astype(f32) * rise[:, h : h + 1]).astype(bf16)
            value = mixed[rows, head_cols(h)] + mm(qd, state.reshape(DH, DH).astype(bf16), NT)
            mixed[rows, head_cols(h)] = value
            squares = squares + value * value
        lines.append(mm(jnp.ones((8, DH), f32), squares, NT, highest))

    seq_wait(S_RESULT, src_result, recv_result)
    soft_ref[...] = recv_result[...]
    seq_wait(S_DECODE, src_decode, recv_decode)
    decode_squares = recv_decode[0]
    for s in range(1, SEQ):
        decode_squares = decode_squares + recv_decode[s]
    for k in range(PAGES_DEV):
        for n in range(PAGE // DH):
            send_tp[2 * k + n : 2 * k + n + 1, :] = lines[k][0:1, head_cols(n)]
    send_tp[8:16, :] = jnp.broadcast_to(decode_squares, (8, DH))

    for hop in range(1, TP):
        tp_copy(hop).start()
    sums_ref[tp] = send_tp[...]
    inputs["gain"].wait()
    for hop in range(1, TP):
        source = lax.rem(tp + TP - hop, TP)
        pltpu.make_async_remote_copy(
            src_ref=send_tp, dst_ref=sums_ref.at[source],
            send_sem=tp_send.at[hop], recv_sem=tp_recv.at[hop],
            device_id=(me, source, rep), device_id_type=MESH,
        ).wait_recv()

    for which, src, dst in (
        (P_KEYS, ck_in, other_k),
        (P_VALUES, cv_in, other_v),
        (P_STATE, pair_state, pair_state_in),
        (P_WEIGHT, pair_weight, pair_weight_in),
        (P_SLOTS, pair_other, pair_slots_in),
        (P_CARRY, pair_carry, pair_carry_in),
        (P_FINAL, pair_final, pair_final_in),
    ):
        pair_copy(which, src, dst).wait_send()
    seq_sent(S_STATE, src_state, recv_state)
    seq_sent(S_SLOTS, src_slots, recv_slots)
    seq_sent(S_SOFT, src_soft, recv_soft)
    seq_sent(S_BACK, src_back, recv_back)

    seq_sent(S_RESULT, src_result, recv_result)
    seq_sent(S_DECODE, src_decode, recv_decode)
    for hop in range(1, TP):
        tp_copy(hop).wait_send()


def norm_kernel(
    mixed, sums, decoded, soft, gain_ref, out_hbm, dec_hbm, soft_hbm, block, dec_lines, dec_block, soft_block, sem
):
    me = lax.axis_index("seq")
    features = TP * HEADS * DH
    copies = []

    def send(src, dst):
        copy = pltpu.make_async_copy(src, dst, sem.at[len(copies)])
        copy.start()
        copies.append(copy)

    gain = gain_ref[...]
    ones = jnp.ones((TP, DH), f32)
    for b in range(ROWS // DH):
        total = mm(sums[:, b, :], ones, TN, highest)
        factor = lax.rsqrt(total / features + norm_eps)
        rows = slice(b * DH, (b + 1) * DH)
        for h in range(HEADS):
            block[rows, head_cols(h)] = (
                mixed[rows, head_cols(h)] * factor * gain[h : h + 1, :]
            ).astype(bf16)
        send(block.at[rows], out_hbm.at[rows])

    def iota(shape, dim):
        return lax.broadcasted_iota(jnp.int32, shape, dim)

    cols = HEADS * 8
    pick = (iota((DH, cols), 0) == jnp.bitwise_and(iota((DH, cols), 1), 7) + me * 8).astype(f32)
    gain_cols = mm(gain, pick, NN, highest)
    gain_cols = jnp.where(iota((HEADS, cols), 1) // 8 == iota((HEADS, cols), 0), gain_cols, 0.0)
    gain_cols = jnp.sum(gain_cols, axis=0, keepdims=True)
    total = mm(sums[:, 8, :], jnp.ones((TP, cols), f32), TN, highest)[0:16]
    value = decoded[...] * lax.rsqrt(total / features + norm_eps) * gain_cols
    for h in range(HEADS):
        dec_lines[pl.ds(h, 16, stride=8), :] = value[:, h * 8 : h * 8 + 8]
    dec_block[...] = dec_lines[...].reshape(DOCS, STEPS, HEADS, 8).astype(bf16)
    send(dec_block, dec_hbm.at[0])
    for p in range(DOCS):
        for h in range(HEADS):
            soft_block[p, :, head_cols(h)] = soft[pl.ds(p * 32 + h, 4, stride=8), :].astype(bf16)
    send(soft_block, soft_hbm.at[0])
    for copy in copies:
        copy.wait()


def per_device(
    light_query, light_key, light_value, log_decay, prompt_pages, norm_gain, cache_keys,
    cache_values, step_query, step_key, step_value, step_decay, soft_query, soft_key, soft_value,
):
    vm = pl.BlockSpec(memory_space=pltpu.VMEM)
    V = pltpu.VMEM
    D = pltpu.SemaphoreType.DMA
    mixed, sums, dec, soft, gain = pl.pallas_call(
        kernel,
        out_shape=(
            jax.ShapeDtypeStruct((ROWS, HEADS * DH), f32),
            jax.ShapeDtypeStruct((TP, 16, DH), f32),
            jax.ShapeDtypeStruct((16, HEADS * 8), f32),
            jax.ShapeDtypeStruct((SEQ, 8, DH), f32),
            jax.ShapeDtypeStruct((HEADS, DH), f32),
        ),
        in_specs=[pl.BlockSpec(memory_space=pltpu.HBM)] * 15,
        out_specs=(vm,) * 5,
        scratch_shapes=[
            pltpu.SMEM((DOCS,), jnp.int32),
            V((ROWS, HEADS * DH), bf16),
            V((ROWS, HEADS * DH), bf16),
            V((ROWS, HEADS * DH), bf16),
            V((HEADS, ROWS), f32),
            V((ROWS, DH), bf16),
            V((ROWS, DH), bf16),
            V((DOCS, STEPS, HEADS * DH), bf16),
            V((DOCS, STEPS, HEADS * DH), bf16),
            V((DOCS, STEPS, HEADS * DH), bf16),
            V((DOCS, STEPS, HEADS), f32),
            V((DOCS, STEPS, HEADS * DH), bf16),
            V((DOCS, STEPS, DH), bf16),
            V((DOCS, STEPS, DH), bf16),
            V((ROWS, HEADS), f32),
            V((PAGES_DEV, HEADS, PAGE), f32),
            V((PAGES_DEV + 1, SEQ, 2 * HALF, DH), f32),
            V((PAGES_DEV, HEADS, DH), f32),
            V((PAGES_DEV, HEADS, DH), f32),
            V((16, HEADS * DH), f32),
            V((16, HEADS * DH), f32),
            V((16, HEADS * DH), f32),
            V((16, HEADS), f32),
            V((DH, DH), f32),
            V((DOCS, STEPS, DH), f32),
            V((DOCS, STEPS, DH), f32),
            V((ROWS, DH), bf16),
            V((ROWS, DH), bf16),
            V((SEQ, HALF, DH), bf16),
            V((SEQ, HALF, DH), bf16),
            V((24, DH), f32),
            V((24, DH), f32),
            V((4, SEQ, HALF, DH), bf16),
            V((2, SEQ, HALF, DH), bf16),
            V((SEQ, HALF + 16, DH), bf16),
            V((SEQ, HALF + 16, DH), bf16),
            V((SEQ, 2, HALF, DH), bf16),
            V((SEQ, 2, HALF, DH), bf16),
            V((SEQ, 16, DH), f32),
            V((SEQ, 16, DH), f32),
            V((SEQ + 1, HALF, DH), f32),
            V((SEQ, HALF, DH), bf16),
            V((SEQ, HALF, DH), bf16),
            V((SEQ, HALF, DH), bf16),
            V((SEQ, HALF, DH), bf16),
            V((SEQ, 2 * HALF, DH), f32),
            V((DOCS, HALF, DH), bf16),
            V((DOCS, HALF, DH), bf16),
            V((DOCS, 2 * HALF, DH), f32),
            V((8, DH), f32),
            V((SEQ, 8, DH), f32),
            V((1, DH), f32),
            V((SEQ, 1, DH), f32),
            V((16, DH), f32),
            D((7,)),
            D((7,)),
            D((6, SEQ)),
            D((6, SEQ)),
            D((TP,)),
            D((TP,)),
            D((21,)),
        ],
        compiler_params=pltpu.CompilerParams(
            collective_id=0, has_side_effects=True, vmem_limit_bytes=48 * 1024 * 1024
        ),
        name="attention_block",
    )(*[pltpu.with_memory_space_constraint(x, pltpu.HBM) for x in (
        prompt_pages, light_query, light_key, light_value, log_decay.T,
        norm_gain.reshape(HEADS, DH), cache_keys, cache_values,
        step_query, step_key, step_value, step_decay, soft_query, soft_key, soft_value,
    )])
    hbm = pl.BlockSpec(memory_space=pl.ANY)
    return pl.pallas_call(
        norm_kernel,
        out_shape=(
            jax.ShapeDtypeStruct((ROWS, HEADS * DH), bf16),
            jax.ShapeDtypeStruct((1, DOCS, STEPS, HEADS, 8), bf16),
            jax.ShapeDtypeStruct((1, DOCS, STEPS, HEADS * DH), bf16),
        ),
        in_specs=[vm] * 5,
        out_specs=(hbm,) * 3,
        scratch_shapes=[
            V((ROWS, HEADS * DH), bf16),
            V((16 * HEADS, 8), f32),
            V((DOCS, STEPS, HEADS, 8), bf16),
            V((DOCS, STEPS, HEADS * DH), bf16),
            D((10,)),
        ],
        compiler_params=pltpu.CompilerParams(vmem_limit_bytes=16 * 1024 * 1024),
        name="norms",
    )(mixed, sums, dec, soft.reshape(SEQ * 8, DH), gain)


def solution(mesh):
    prompt = P(("seq", "rep"), "tp")
    sample = P("rep", None, None, "tp")
    return jax.shard_map(
        per_device,
        mesh=mesh,
        in_specs=(prompt,) * 4 + (P(), P("tp")) + (prompt,) * 2 + (sample,) * 7,
        out_specs=(prompt, P("rep", None, None, "tp", "seq"), sample),
        check_vma=False,
    )
```

```python
import math

import jax
import jax.numpy as jnp
from jax import lax
from jax.experimental import pallas as pl
from jax.experimental.pallas import tpu as pltpu
from jax.sharding import PartitionSpec as P

DH = 128
PAGE = 256
DOCS = 4
STEPS = 4
HEADS = 8
SEQ = 16
TP = 8
ROWS = 1024
PAGES_DEV = ROWS // PAGE
HALF = HEADS // 2 * 8

norm_eps = 1e-06
mask_low = -1e30
LOG2E = math.log2(math.e)
highest = lax.Precision.HIGHEST
f32 = jnp.float32
bf16 = jnp.bfloat16
MESH = pl.DeviceIdType.MESH

NN = (((1,), (0,)), ((), ()))
NT = (((1,), (1,)), ((), ()))
TN = (((0,), (0,)), ((), ()))

P_KEYS, P_VALUES, P_STATE, P_WEIGHT, P_SLOTS, P_CARRY, P_FINAL, P_QUERY = range(8)
SEQ_HOPS = (10, 6, 9, 11, 14, 2, 8, 5, 7, 13, 15, 1, 3, 4, 12)
TP_HOPS = (4, 3, 5, 2, 6, 1, 7)
S_STATE, S_SLOTS, S_SOFT, S_BACK, S_RESULT, S_DECODE = range(6)


def mm(a, b, dims, precision=None):
    return lax.dot_general(a, b, dims, precision=precision, preferred_element_type=f32)


def head_cols(h):
    return slice(h * DH, (h + 1) * DH)


def expand(rows):
    return jnp.concatenate(
        [jnp.broadcast_to(rows[i : i + 1], (8, DH)) for i in range(HEADS // 2)], axis=0
    )


def kernel(
    pages_in, q_in, k_in, v_in, g_in, gain_in, ck_in, cv_in,
    stq_in, stk_in, stv_in, std_in, sfq_in, sfk_in, sfv_in,
    mixed, sums_ref, dec_own, soft_ref, gain_ref,
    pages_ref, q_ref, k_ref, v_ref, g_ref, ck_ref, cv_ref,
    stq_ref, stk_ref, stv_ref, std_ref, sfq_ref, sfk_ref, sfv_ref,
    ccol, crow, states, before, weights, stq, stk, stv, std, sfq, sfk, sfv,
    other_k, other_v, other_q, query_all, read_rows,
    pair_state, pair_state_in, pair_weight, pair_weight_in, pair_slots, pair_slots_in,
    send_state, recv_state, send_slots, recv_slots, send_soft, recv_soft,
    carry, send_back, recv_back, pair_carry, pair_carry_in, carry_all,
    pair_final, pair_final_in, final_all, square_sums, send_result, recv_result, send_decode, recv_decode, send_tp,
    pair_send, pair_recv, seq_send, seq_recv, tp_send, tp_recv, in_sem,
):
    me = lax.axis_index("seq")
    tp = lax.axis_index("tp")
    rep = lax.axis_index("rep")
    first_core = rep == 0
    own_rows = pl.ds(pl.multiple_of(rep * HALF, HALF), HALF)
    other_rows = pl.ds(pl.multiple_of((1 - rep) * HALF, HALF), HALF)

    def page_rows(k):
        return pl.ds(k * PAGE, PAGE)

    inputs = {}

    def fetch(name, src, dst):
        inputs[name] = pltpu.make_async_copy(src, dst, in_sem.at[len(inputs)])
        inputs[name].start()

    fetch("pages", pages_in, pages_ref)
    fetch("g", g_in, g_ref)
    for k in range(PAGES_DEV):
        fetch(("k", k), k_in.at[page_rows(k)], k_ref.at[page_rows(k)])
        fetch(("v", k), v_in.at[page_rows(k)], v_ref.at[page_rows(k)])
    fetch("q", q_in, q_ref)
    fetch("ck", ck_in, ck_ref)
    fetch("cv", cv_in, cv_ref)
    small = (
        (stq_in, stq_ref), (stk_in, stk_ref), (stv_in, stv_ref), (std_in, std_ref),
        (sfq_in, sfq_ref), (sfk_in, sfk_ref), (sfv_in, sfv_ref),
    )
    for n, (src, dst) in enumerate(small):
        fetch(("small", n), src.at[0], dst)
    fetch("gain", gain_in, gain_ref)

    me_x, me_y = me // 4, lax.rem(me, 4)

    def seq_ahead(hop):
        return lax.rem(me_x + hop // 4, 4) * 4 + lax.rem(me_y + hop % 4, 4)

    def seq_behind(hop):
        return lax.rem(me_x + 4 - hop // 4, 4) * 4 + lax.rem(me_y + 4 - hop % 4, 4)

    def pair_copy(which, src, dst):
        return pltpu.make_async_remote_copy(
            src_ref=src, dst_ref=dst, send_sem=pair_send.at[which], recv_sem=pair_recv.at[which],
            device_id=(me, tp, 1 - rep), device_id_type=MESH,
        )

    def seq_copy(phase, src, dst, hop):
        target = seq_ahead(hop)
        return pltpu.make_async_remote_copy(
            src_ref=src(target), dst_ref=dst.at[me],
            send_sem=seq_send.at[phase, hop], recv_sem=seq_recv.at[phase, hop],
            device_id=(target, tp, rep), device_id_type=MESH,
        )

    def seq_start(phase, src, dst):
        for hop in SEQ_HOPS:
            seq_copy(phase, src, dst, hop).start()

    def seq_wait(phase, src, dst):
        for hop in SEQ_HOPS:
            source = seq_behind(hop)
            pltpu.make_async_remote_copy(
                src_ref=src(source), dst_ref=dst.at[source],
                send_sem=seq_send.at[phase, hop], recv_sem=seq_recv.at[phase, hop],
                device_id=(source, tp, rep), device_id_type=MESH,
            ).wait_recv()

    def seq_sent(phase, src, dst):
        for hop in SEQ_HOPS:
            seq_copy(phase, src, dst, hop).wait_send()

    src_state = lambda t: send_state.at[t]
    src_slots = lambda t: send_slots.at[t]
    src_soft = lambda t: send_soft.at[t]
    src_back = lambda t: send_back.at[t]
    src_result = lambda t: send_result
    src_decode = lambda t: send_decode

    def tp_copy(hop):
        return pltpu.make_async_remote_copy(
            src_ref=send_tp, dst_ref=sums_ref.at[tp],
            send_sem=tp_send.at[hop], recv_sem=tp_recv.at[hop],
            device_id=(me, lax.rem(tp + hop, TP), rep), device_id_type=MESH,
        )

    barrier = pltpu.get_barrier_semaphore()

    for hop in SEQ_HOPS:
        pl.semaphore_signal(
            barrier, inc=1, device_id=(seq_ahead(hop), tp, rep), device_id_type=MESH
        )
    for hop in TP_HOPS:
        pl.semaphore_signal(
            barrier, inc=1, device_id=(me, lax.rem(tp + hop, TP), rep), device_id_type=MESH
        )
    pl.semaphore_signal(barrier, inc=1, device_id=(me, tp, 1 - rep), device_id_type=MESH)

    inputs["pages"].wait()
    ends = []
    for p in range(DOCS):
        ends.append(pages_ref[p] + (ends[-1] if ends else 0))
    chip_page = me * (2 * PAGES_DEV)
    dev_page = chip_page + rep * PAGES_DEV

    def flag(cond):
        return jnp.where(cond, 1, 0).astype(jnp.int32)

    def goes_on(page):
        hits = sum(flag(e == page) for e in ends)
        return jnp.where(hits == 0, 1.0, 0.0).astype(f32)

    def doc_of(page):
        return sum((e <= page).astype(jnp.int32) for e in ends)

    slot_page, slot_valid, slot_doc = [], [], []
    inside = [flag(jnp.logical_and(e > chip_page, e < chip_page + 2 * PAGES_DEV)) for e in ends]
    for s in range(2):
        place, owner = 0, 0
        for p in range(DOCS):
            rank = sum(inside[:p]) if p else 0
            place = place + inside[p] * flag(rank == s) * (ends[p] - chip_page)
            owner = owner + inside[p] * flag(rank == s) * p
        local = place - 1 - rep * PAGES_DEV
        ok = jnp.logical_and(
            place > 0, jnp.logical_and(local >= 0, local < PAGES_DEV)
        )
        slot_doc.append(owner)
        slot_page.append(jnp.clip(local, 0, PAGES_DEV - 1))
        slot_valid.append(jnp.where(ok, 1.0, 0.0).astype(f32))

    rows_i = lax.broadcasted_iota(jnp.int32, (PAGE, PAGE), 0)
    cols_i = lax.broadcasted_iota(jnp.int32, (PAGE, PAGE), 1)
    states[0] = jnp.zeros((SEQ, 2 * HALF, DH), f32)

    inputs["g"].wait()
    g = g_ref[...] * LOG2E
    g_high = g.astype(bf16)
    g_rest = g - g_high.astype(f32)
    g_mid = g_rest.astype(bf16)
    g_low = (g_rest - g_mid.astype(f32)).astype(bf16)
    upper = (rows_i <= cols_i).astype(f32).astype(bf16)
    parts = [
        x[:, k * PAGE : (k + 1) * PAGE].astype(f32)
        for x in (g_high, g_mid, g_low)
        for k in range(PAGES_DEV)
    ]
    summed = mm(jnp.concatenate(parts, axis=0).astype(bf16), upper, NN)
    wide = PAGES_DEV * HEADS
    summed = summed[0:wide] + summed[wide : 2 * wide] + summed[2 * wide :]
    turned = jnp.transpose(summed)

    def state_page(k, carried):
        rows = page_rows(k)
        c = turned[:, k * HEADS : (k + 1) * HEADS]
        ccol[rows, :] = c
        line = summed[k * HEADS : (k + 1) * HEADS]
        crow[k] = line
        decay = jnp.exp2(jnp.broadcast_to(line[:, PAGE - 1 : PAGE], (HEADS, DH)))
        cont = goes_on(dev_page + k)
        before[k] = carried * cont
        keep = decay * cont
        after = carried * keep
        weights[k] = after
        fade = jnp.exp2(c[PAGE - 1 : PAGE, :] - c)
        for h in range(HEADS):
            kd = (k_ref[rows, head_cols(h)].astype(f32) * fade[:, h : h + 1]).astype(bf16)
            add = mm(v_ref[rows, head_cols(h)], kd, TN)
            old = states[k, :, h * 8 : h * 8 + 8, :]
            states[k + 1, :, h * 8 : h * 8 + 8, :] = old * keep[h : h + 1, :][None] + add.reshape(
                SEQ, 8, DH
            )
        return after

    total = jnp.ones((HEADS, DH), f32)
    for k in range(PAGES_DEV):
        inputs[("k", k)].wait()
        inputs[("v", k)].wait()
        total = state_page(k, total)

    pair_state[...] = states[PAGES_DEV, :, other_rows, :].astype(bf16)
    pair_weight[0:8] = total
    for s in range(2):
        w = jnp.zeros((HEADS, DH), f32)
        for k in range(PAGES_DEV):
            pick = jnp.where(slot_page[s] == k, slot_valid[s], 0.0).astype(f32)
            w = w + pick * weights[k]
        pair_weight[8 + 8 * s : 16 + 8 * s] = w
    pl.semaphore_wait(barrier, SEQ - 1 + TP - 1 + 1)
    pair_copy(P_STATE, pair_state, pair_state_in).start()
    pair_copy(P_WEIGHT, pair_weight, pair_weight_in).start()
    for s in range(2):
        pair_slots[s] = (states[slot_page[s] + 1][:, 0:HALF, :] * slot_valid[s]).astype(bf16)
        pair_slots[2 + s] = (states[slot_page[s] + 1][:, HALF:, :] * slot_valid[s]).astype(bf16)
    pair_other = pair_slots.at[pl.ds((1 - rep) * 2, 2)]
    pair_copy(P_SLOTS, pair_other, pair_slots_in).start()
    pair_copy(P_QUERY, stq_in.at[0], other_q).start()
    pair_copy(P_KEYS, ck_in, other_k).start()
    pair_copy(P_VALUES, cv_in, other_v).start()

    causal = rows_i >= cols_i

    def inside_page(k):
        rows = pl.ds(pl.multiple_of(k * PAGE, PAGE), PAGE)
        c = ccol[rows, :]
        r = crow[k]
        for h in range(HEADS):
            scores = mm(q_ref[rows, head_cols(h)], k_ref[rows, head_cols(h)], NT)
            grid = jnp.exp2(c[:, h : h + 1] - r[h : h + 1, :])
            block = jnp.where(causal, scores * grid, 0.0).astype(bf16)
            mixed[rows, head_cols(h)] = mm(block, v_ref[rows, head_cols(h)], NN)

    def inside_loop(first, last):
        def one(k, _):
            inside_page(k)
            return 0

        lax.fori_loop(first, last, one, 0)


    def half(x):
        return lax.select(first_core, x[0:4], x[4:8])

    pair_copy(P_STATE, pair_state, pair_state_in).wait_recv()
    pair_copy(P_WEIGHT, pair_weight, pair_weight_in).wait_recv()
    own_state = states[PAGES_DEV, :, own_rows, :]
    got_state = pair_state_in[...].astype(f32)
    state0 = lax.select(first_core, own_state, got_state)
    state1 = lax.select(first_core, got_state, own_state)
    own_w = [half(pair_weight[8 * n : 8 * n + 8]) for n in range(3)]
    got_w = [half(pair_weight_in[8 * n : 8 * n + 8]) for n in range(3)]
    w0 = [lax.select(first_core, a, b) for a, b in zip(own_w, got_w)]
    w1 = [lax.select(first_core, b, a) for a, b in zip(own_w, got_w)]
    chip_state = expand(w1[0])[None] * state0 + state1
    chip_w = jnp.concatenate([w1[0] * w0[0], w0[1] + w1[1] * w0[0]], axis=0)
    chip_hi = chip_w.astype(bf16).astype(f32)
    chip_rows = jnp.concatenate([chip_hi, chip_w - chip_hi], axis=0).astype(bf16)
    send_state[:, 0:HALF, :] = chip_state.astype(bf16)
    send_state[:, HALF:, :] = jnp.broadcast_to(chip_rows[None], (SEQ, 16, DH))
    seq_start(S_STATE, src_state, recv_state)
    recv_state[me] = send_state[me]

    for n in range(len(small)):
        inputs[("small", n)].wait()
    for p in range(DOCS):
        part = slice(4 * p, 4 * p + 4)
        stq[part, :] = stq_ref[p].astype(f32)
        stk[part, :] = stk_ref[p].astype(f32)
        stv[part, :] = stv_ref[p].astype(f32)
        std[part, :] = std_ref[p]
        sfk[p] = sfk_ref[p].astype(f32)
        sfv[p] = sfv_ref[p].astype(f32)
        for h in range(HEADS):
            sfq[pl.ds(p * 32 + h, 4, stride=8), :] = sfq_ref[p, :, head_cols(h)].astype(f32)

    pair_copy(P_QUERY, stq_in.at[0], other_q).wait_recv()
    other_lines = jnp.concatenate([other_q[p].astype(f32) for p in range(DOCS)], axis=0)
    query_all[pl.ds(pl.multiple_of(rep * 16, 16), 16), :] = stq[...].astype(bf16)
    query_all[pl.ds(pl.multiple_of((1 - rep) * 16, 16), 16), :] = other_lines.astype(bf16)

    def half_query(n):
        return query_all[:, pl.ds(pl.multiple_of((rep * (HEADS // 2) + n) * DH, DH), DH)]

    def iota(shape, dim):
        return lax.broadcasted_iota(jnp.int32, shape, dim)

    pair_copy(P_SLOTS, pair_other, pair_slots_in).wait_recv()
    slots = []
    for s in range(2):
        own_slot = states[slot_page[s] + 1][:, 0:HALF, :]
        own_slot = lax.select(first_core, own_slot, states[slot_page[s] + 1][:, HALF:, :])
        slot = own_slot * slot_valid[s] + pair_slots_in[s].astype(f32)
        slots.append(slot + expand(w1[1 + s])[None] * state0)
    lane_doc = jnp.bitwise_and(iota((DH, 32), 1), 15) // STEPS
    reads = []
    for n in range(HEADS // 2):
        read = jnp.zeros((DH, 32), f32)
        for s in range(2):
            state = slots[s][:, n * 8 : n * 8 + 8, :].reshape(DH, DH).astype(bf16)
            read = read + jnp.where(lane_doc == slot_doc[s], mm(state, half_query(n), NT), 0.0)
        reads.append(read)
    send_slots[...] = jnp.concatenate(reads, axis=1).reshape(SEQ, 8, DH)
    seq_start(S_SLOTS, src_slots, recv_slots)
    recv_slots[me] = send_slots[me]

    chain = jnp.logical_and(
        iota((16, 16), 0) // STEPS == iota((16, 16), 1) // STEPS, iota((16, 16), 0) >= iota((16, 16), 1)
    )
    fall = mm(chain.astype(f32), std[...] * LOG2E, NN, highest)
    spread_heads = (iota((HEADS, DH), 1) // 16 == iota((HEADS, DH), 0)).astype(f32)
    fall_from = mm(fall, spread_heads, NN, highest)
    lane_step = jnp.bitwise_and(iota((16, DH), 1), 15)
    diagonal = jnp.where(lane_step == iota((16, DH), 0), fall_from, 0.0)
    fall_to = mm(jnp.ones((16, 16), f32), diagonal, NN, highest)
    linked = jnp.logical_and(
        iota((16, DH), 0) // STEPS == lane_step // STEPS, iota((16, DH), 0) >= lane_step
    )
    met = jnp.concatenate(
        [
            mm(stq[:, head_cols(h)].astype(bf16), stk[:, head_cols(h)].astype(bf16), NT)
            for h in range(HEADS)
        ],
        axis=1,
    )
    met = jnp.where(linked, met * jnp.exp2(fall_from - fall_to), 0.0)
    cols = HEADS * 8
    pick = (iota((DH, cols), 0) == jnp.bitwise_and(iota((DH, cols), 1), 7) + me * 8).astype(f32)
    values = jnp.concatenate([stv[:, head_cols(h)] for h in range(HEADS)], axis=0)
    values = mm(values.astype(bf16), pick.astype(bf16), NN)
    values = jnp.where(iota((DH, cols), 0) // 16 == iota((DH, cols), 1) // 8, values, 0.0)
    decoded = mm(met, values, NN, highest)
    spread_cols = (iota((HEADS, cols), 1) // 8 == iota((HEADS, cols), 0)).astype(f32)
    shrunk = jnp.exp2(mm(fall, spread_cols, NN, highest))

    inputs["ck"].wait()
    inputs["cv"].wait()
    scale = DH**-0.5 * LOG2E
    pair_copy(P_KEYS, ck_in, other_k).wait_recv()
    pair_copy(P_VALUES, cv_in, other_v).wait_recv()
    queries = sfq[...].astype(bf16)
    query_doc = lax.broadcasted_iota(jnp.int32, (DH, ROWS), 0) // 32
    key_page = lax.broadcasted_iota(jnp.int32, (1, ROWS), 1) // PAGE
    score, here = [], []
    for base, key_block in ((dev_page, ck_ref), (chip_page + (1 - rep) * PAGES_DEV, other_k)):
        score.append(mm(queries, key_block[...], NT) * scale)
        here.append(query_doc == jnp.broadcast_to(doc_of(key_page + base), (DH, ROWS)))
    peak = jnp.maximum(
        *[
            jnp.max(jnp.where(m, s, mask_low), axis=1, keepdims=True)
            for m, s in zip(here, score)
        ]
    )
    chance = [jnp.where(m, jnp.exp2(s - peak), 0.0) for m, s in zip(here, score)]
    amount = sum(jnp.sum(x, axis=1, keepdims=True) for x in chance)
    numer = mm(chance[0].astype(bf16), cv_ref[...], NN) + mm(
        chance[1].astype(bf16), other_v[...], NN
    )
    lane = lax.broadcasted_iota(jnp.int32, (DH, DH), 1)
    both = jnp.where(lane < 64, jnp.broadcast_to(peak, (DH, DH)), jnp.broadcast_to(amount, (DH, DH)))
    send_soft[:, 0:8, :] = numer.reshape(SEQ, 8, DH)
    send_soft[:, 8:16, :] = both.reshape(SEQ, 8, DH)
    seq_start(S_SOFT, src_soft, recv_soft)
    recv_soft[me] = send_soft[me]

    seq_wait(S_STATE, src_state, recv_state)
    running = jnp.zeros((HALF, DH), f32)
    for j in range(SEQ):
        carry[j] = running
        send_back[j] = running.astype(bf16)
        rows = recv_state[j, HALF:, :].astype(f32)
        running = expand(rows[0:4] + rows[8:12]) * running + recv_state[j, 0:HALF, :].astype(f32)
    carry[SEQ] = running
    seq_start(S_BACK, src_back, recv_back)
    recv_back[me] = send_back[me]

    seq_wait(S_SLOTS, src_slots, recv_slots)
    for p in range(DOCS):
        last_page = jnp.clip(ends[p] - 1, 0, 2 * PAGES_DEV * SEQ - 1)
        chip = lax.shift_right_logical(last_page, 3)
        chip_last = jnp.bitwise_and(last_page, 7) == 7
        rank = sum(
            [flag(lax.shift_right_logical(ends[o] - 1, 3) == chip) for o in range(p)],
            jnp.int32(0),
        )
        rows = recv_state[chip][HALF:, :].astype(f32)
        w = expand(rows[4:8] + rows[12:16]) * jnp.where(rank == 0, 1.0, 0.0).astype(f32)
        final_all[p] = lax.select(chip_last, carry[chip + 1], w * carry[chip])
    tile = recv_slots[0]
    for j in range(1, SEQ):
        tile = tile + recv_slots[j]
    reads = []
    for n in range(HEADS // 2):
        state = final_all[:, n * 8 : n * 8 + 8, :].reshape(DOCS * 8, DH).astype(bf16)
        read = mm(state, half_query(n), NT)
        read = jnp.where(iota((32, 32), 0) // 8 == lane_doc[0:32], read, 0.0)
        reads.append(read[0:8] + read[8:16] + read[16:24] + read[24:32])
    pair_final[...] = tile + jnp.concatenate(reads, axis=1)
    pair_copy(P_FINAL, pair_final, pair_final_in).start()

    inputs["q"].wait()
    inside_loop(0, 1)

    pair_copy(P_FINAL, pair_final, pair_final_in).wait_recv()
    own_tile, got_tile = pair_final[...], pair_final_in[...]
    tiles = [lax.select(first_core, own_tile, got_tile), lax.select(first_core, got_tile, own_tile)]
    read_rows[...] = jnp.transpose(jnp.concatenate(tiles, axis=0))
    lines_of = [
        read_rows[pl.ds(pl.multiple_of(n * 32 + rep * 16, 16), 16), :] for n in range(HEADS // 2)
    ]
    read = jnp.concatenate([x[:, 8 * n : 8 * n + 8] for n in range(2) for x in lines_of], axis=1)
    decoded = decoded + read * shrunk
    dec_own[...] = decoded
    squares = mm(jnp.ones((8, cols), f32), decoded * decoded, NT, highest)
    send_decode[...] = jnp.zeros((1, DH), f32)
    send_decode[:, 0:16] = squares[0:1, :]
    seq_start(S_DECODE, src_decode, recv_decode)
    recv_decode[me] = send_decode[...]

    inside_loop(1, 4)

    seq_wait(S_BACK, src_back, recv_back)
    carry0 = recv_back[...].astype(f32)
    carry1 = expand(w0[0])[None] * carry0 + state0
    carry_all[:, own_rows, :] = lax.select(first_core, carry0, carry1)
    pair_carry[...] = lax.select(first_core, carry1, carry0).astype(bf16)
    pair_copy(P_CARRY, pair_carry, pair_carry_in).start()


    seq_wait(S_SOFT, src_soft, recv_soft)
    doc = me // STEPS
    step = lax.rem(me, STEPS)
    own_q = sfq[pl.ds(pl.multiple_of(me * 8, 8), 8), :]
    own_k = sfk[doc]
    own_v = sfv[doc]
    peaks = [recv_soft[s, 8:16, 0:1] for s in range(SEQ)]
    amounts = [recv_soft[s, 8:16, 64:65] for s in range(SEQ)]
    numers = [recv_soft[s, 0:8, :] for s in range(SEQ)]
    top = peaks[0]
    for x in peaks[1:]:
        top = jnp.maximum(top, x)
    own = []
    for i in range(STEPS):
        s = jnp.sum(own_q * own_k[i : i + 1, :], axis=1, keepdims=True) * scale
        own.append(lax.select(step >= i, s, jnp.full((8, 1), mask_low, f32)))
        top = jnp.maximum(top, own[-1])
    numer = jnp.zeros((8, DH), f32)
    amount = jnp.zeros((8, 1), f32)
    for s in range(SEQ):
        shrink = jnp.exp2(peaks[s] - top)
        numer = numer + numers[s] * shrink
        amount = amount + amounts[s] * shrink
    for i in range(STEPS):
        e = lax.select(step >= i, jnp.exp2(own[i] - top), jnp.zeros((8, 1), f32))
        numer = numer + e.astype(bf16).astype(f32) * own_v[i : i + 1, :]
        amount = amount + e
    send_result[...] = numer / amount
    seq_start(S_RESULT, src_result, recv_result)
    recv_result[me] = send_result[...]

    pair_copy(P_CARRY, pair_carry, pair_carry_in).wait_recv()
    carry_all[:, other_rows, :] = pair_carry_in[...].astype(f32)
    for k in range(PAGES_DEV):
        rows = page_rows(k)
        rise = jnp.exp2(ccol[rows, :])
        cont = goes_on(dev_page + k)
        w = before[k]
        squares = jnp.zeros((PAGE, DH), f32)
        for h in range(HEADS):
            part = slice(h * 8, h * 8 + 8)
            state = states[k, :, part, :] * cont + carry_all[:, part, :] * w[h : h + 1, :][None]
            qd = (q_ref[rows, head_cols(h)].astype(f32) * rise[:, h : h + 1]).astype(bf16)
            value = mixed[rows, head_cols(h)] + mm(qd, state.reshape(DH, DH).astype(bf16), NT)
            mixed[rows, head_cols(h)] = value
            squares = squares + value * value
        high = squares.astype(bf16)
        rest = (squares - high.astype(f32)).astype(bf16)
        ones = jnp.ones((16, DH), bf16)
        line = mm(ones, high, NT) + mm(ones, rest, NT)
        for n in range(PAGE // DH):
            send_tp[2 * k + n : 2 * k + n + 1, :] = line[0:1, head_cols(n)]


    seq_wait(S_DECODE, src_decode, recv_decode)
    decode_squares = recv_decode[0]
    for s in range(1, SEQ):
        decode_squares = decode_squares + recv_decode[s]
    send_tp[8:16, :] = jnp.broadcast_to(decode_squares, (8, DH))

    for hop in TP_HOPS:
        tp_copy(hop).start()
    sums_ref[tp] = send_tp[...]
    seq_wait(S_RESULT, src_result, recv_result)
    soft_ref[...] = recv_result[...]
    inputs["gain"].wait()
    for hop in TP_HOPS:
        source = lax.rem(tp + TP - hop, TP)
        pltpu.make_async_remote_copy(
            src_ref=send_tp, dst_ref=sums_ref.at[source],
            send_sem=tp_send.at[hop], recv_sem=tp_recv.at[hop],
            device_id=(me, source, rep), device_id_type=MESH,
        ).wait_recv()

    for which, src, dst in (
        (P_QUERY, stq_in.at[0], other_q),
        (P_KEYS, ck_in, other_k),
        (P_VALUES, cv_in, other_v),
        (P_STATE, pair_state, pair_state_in),
        (P_WEIGHT, pair_weight, pair_weight_in),
        (P_SLOTS, pair_other, pair_slots_in),
        (P_CARRY, pair_carry, pair_carry_in),
        (P_FINAL, pair_final, pair_final_in),
    ):
        pair_copy(which, src, dst).wait_send()
    seq_sent(S_STATE, src_state, recv_state)
    seq_sent(S_SLOTS, src_slots, recv_slots)
    seq_sent(S_SOFT, src_soft, recv_soft)
    seq_sent(S_BACK, src_back, recv_back)

    seq_sent(S_RESULT, src_result, recv_result)
    seq_sent(S_DECODE, src_decode, recv_decode)
    for hop in TP_HOPS:
        tp_copy(hop).wait_send()


def norm_kernel(
    mixed, sums, decoded, soft, gain_ref, out_hbm, dec_hbm, soft_hbm, block, dec_lines, dec_block, soft_block, sem
):
    me = lax.axis_index("seq")
    features = TP * HEADS * DH
    copies = []

    def send(src, dst):
        copy = pltpu.make_async_copy(src, dst, sem.at[len(copies)])
        copy.start()
        copies.append(copy)

    gain = gain_ref[...]
    lines = jnp.concatenate([sums[:, b, :] for b in range(ROWS // DH)], axis=1)
    total = mm(lines, jnp.ones((TP, DH), f32), TN, highest)
    factors = lax.rsqrt(total / features + norm_eps)
    for b in range(ROWS // DH):
        rows = slice(b * DH, (b + 1) * DH)
        factor = factors[rows]
        for h in range(HEADS):
            block[rows, head_cols(h)] = (
                mixed[rows, head_cols(h)] * factor * gain[h : h + 1, :]
            ).astype(bf16)
        send(block.at[rows], out_hbm.at[rows])

    def iota(shape, dim):
        return lax.broadcasted_iota(jnp.int32, shape, dim)

    cols = HEADS * 8
    pick = (iota((DH, cols), 0) == jnp.bitwise_and(iota((DH, cols), 1), 7) + me * 8).astype(f32)
    gain_cols = mm(gain, pick, NN, highest)
    gain_cols = jnp.where(iota((HEADS, cols), 1) // 8 == iota((HEADS, cols), 0), gain_cols, 0.0)
    gain_cols = jnp.sum(gain_cols, axis=0, keepdims=True)
    total = mm(sums[:, 8, :], jnp.ones((TP, cols), f32), TN, highest)[0:16]
    value = decoded[...] * lax.rsqrt(total / features + norm_eps) * gain_cols
    for h in range(HEADS):
        dec_lines[pl.ds(h, 16, stride=8), :] = value[:, h * 8 : h * 8 + 8]
    dec_block[...] = dec_lines[...].reshape(DOCS, STEPS, HEADS, 8).astype(bf16)
    send(dec_block, dec_hbm.at[0])
    for p in range(DOCS):
        for h in range(HEADS):
            soft_block[p, :, head_cols(h)] = soft[pl.ds(p * 32 + h, 4, stride=8), :].astype(bf16)
    send(soft_block, soft_hbm.at[0])
    for copy in copies:
        copy.wait()


def per_device(
    light_query, light_key, light_value, log_decay, prompt_pages, norm_gain, cache_keys,
    cache_values, step_query, step_key, step_value, step_decay, soft_query, soft_key, soft_value,
):
    vm = pl.BlockSpec(memory_space=pltpu.VMEM)
    V = pltpu.VMEM
    D = pltpu.SemaphoreType.DMA
    mixed, sums, dec, soft, gain = pl.pallas_call(
        kernel,
        out_shape=(
            jax.ShapeDtypeStruct((ROWS, HEADS * DH), f32),
            jax.ShapeDtypeStruct((TP, 16, DH), f32),
            jax.ShapeDtypeStruct((16, HEADS * 8), f32),
            jax.ShapeDtypeStruct((SEQ, 8, DH), f32),
            jax.ShapeDtypeStruct((HEADS, DH), f32),
        ),
        in_specs=[pl.BlockSpec(memory_space=pltpu.HBM)] * 15,
        out_specs=(vm,) * 5,
        scratch_shapes=[
            pltpu.SMEM((DOCS,), jnp.int32),
            V((ROWS, HEADS * DH), bf16),
            V((ROWS, HEADS * DH), bf16),
            V((ROWS, HEADS * DH), bf16),
            V((HEADS, ROWS), f32),
            V((ROWS, DH), bf16),
            V((ROWS, DH), bf16),
            V((DOCS, STEPS, HEADS * DH), bf16),
            V((DOCS, STEPS, HEADS * DH), bf16),
            V((DOCS, STEPS, HEADS * DH), bf16),
            V((DOCS, STEPS, HEADS), f32),
            V((DOCS, STEPS, HEADS * DH), bf16),
            V((DOCS, STEPS, DH), bf16),
            V((DOCS, STEPS, DH), bf16),
            V((ROWS, HEADS), f32),
            V((PAGES_DEV, HEADS, PAGE), f32),
            V((PAGES_DEV + 1, SEQ, 2 * HALF, DH), f32),
            V((PAGES_DEV, HEADS, DH), f32),
            V((PAGES_DEV, HEADS, DH), f32),
            V((16, HEADS * DH), f32),
            V((16, HEADS * DH), f32),
            V((16, HEADS * DH), f32),
            V((16, HEADS), f32),
            V((DH, DH), f32),
            V((DOCS, STEPS, DH), f32),
            V((DOCS, STEPS, DH), f32),
            V((ROWS, DH), bf16),
            V((ROWS, DH), bf16),
            V((DOCS, STEPS, HEADS * DH), bf16),
            V((32, HEADS * DH), bf16),
            V((DH, 16), f32),
            V((SEQ, HALF, DH), bf16),
            V((SEQ, HALF, DH), bf16),
            V((24, DH), f32),
            V((24, DH), f32),
            V((4, SEQ, HALF, DH), bf16),
            V((2, SEQ, HALF, DH), bf16),
            V((SEQ, HALF + 16, DH), bf16),
            V((SEQ, HALF + 16, DH), bf16),
            V((SEQ, 8, DH), f32),
            V((SEQ, 8, DH), f32),
            V((SEQ, 16, DH), f32),
            V((SEQ, 16, DH), f32),
            V((SEQ + 1, HALF, DH), f32),
            V((SEQ, HALF, DH), bf16),
            V((SEQ, HALF, DH), bf16),
            V((SEQ, HALF, DH), bf16),
            V((SEQ, HALF, DH), bf16),
            V((SEQ, 2 * HALF, DH), f32),
            V((8, DH), f32),
            V((8, DH), f32),
            V((DOCS, HALF, DH), f32),
            V((ROWS, DH), f32),
            V((8, DH), f32),
            V((SEQ, 8, DH), f32),
            V((1, DH), f32),
            V((SEQ, 1, DH), f32),
            V((16, DH), f32),
            D((8,)),
            D((8,)),
            D((6, SEQ)),
            D((6, SEQ)),
            D((TP,)),
            D((TP,)),
            D((21,)),
        ],
        compiler_params=pltpu.CompilerParams(
            collective_id=0, has_side_effects=True, vmem_limit_bytes=48 * 1024 * 1024
        ),
        name="attention_block",
    )(*[pltpu.with_memory_space_constraint(x, pltpu.HBM) for x in (
        prompt_pages, light_query, light_key, light_value, log_decay.T,
        norm_gain.reshape(HEADS, DH), cache_keys, cache_values,
        step_query, step_key, step_value, step_decay, soft_query, soft_key, soft_value,
    )])
    hbm = pl.BlockSpec(memory_space=pl.ANY)
    return pl.pallas_call(
        norm_kernel,
        out_shape=(
            jax.ShapeDtypeStruct((ROWS, HEADS * DH), bf16),
            jax.ShapeDtypeStruct((1, DOCS, STEPS, HEADS, 8), bf16),
            jax.ShapeDtypeStruct((1, DOCS, STEPS, HEADS * DH), bf16),
        ),
        in_specs=[vm] * 5,
        out_specs=(hbm,) * 3,
        scratch_shapes=[
            V((ROWS, HEADS * DH), bf16),
            V((16 * HEADS, 8), f32),
            V((DOCS, STEPS, HEADS, 8), bf16),
            V((DOCS, STEPS, HEADS * DH), bf16),
            D((10,)),
        ],
        compiler_params=pltpu.CompilerParams(vmem_limit_bytes=16 * 1024 * 1024),
        name="norms",
    )(mixed, sums, dec, soft.reshape(SEQ * 8, DH), gain)


def solution(mesh):
    prompt = P(("seq", "rep"), "tp")
    sample = P("rep", None, None, "tp")
    return jax.shard_map(
        per_device,
        mesh=mesh,
        in_specs=(prompt,) * 4 + (P(), P("tp")) + (prompt,) * 2 + (sample,) * 7,
        out_specs=(prompt, P("rep", None, None, "tp", "seq"), sample),
        check_vma=False,
    )
```

```python
import math

import jax
import jax.numpy as jnp
from jax import lax
from jax.experimental import pallas as pl
from jax.experimental.pallas import tpu as pltpu
from jax.sharding import PartitionSpec as P

DH = 128
PAGE = 256
DOCS = 4
STEPS = 4
HEADS = 8
SEQ = 16
TP = 8
ROWS = 1024
PAGES_DEV = ROWS // PAGE
HALF = HEADS // 2 * 8

norm_eps = 1e-06
mask_low = -1e30
LOG2E = math.log2(math.e)
highest = lax.Precision.HIGHEST
f32 = jnp.float32
bf16 = jnp.bfloat16
MESH = pl.DeviceIdType.MESH

NN = (((1,), (0,)), ((), ()))
NT = (((1,), (1,)), ((), ()))
TN = (((0,), (0,)), ((), ()))

P_KEYS, P_VALUES, P_STATE, P_WEIGHT, P_SLOTS, P_CARRY, P_FINAL, P_QUERY = range(8)
SEQ_HOPS = (10, 6, 9, 11, 14, 2, 8, 5, 7, 13, 15, 1, 3, 4, 12)
TP_HOPS = (4, 3, 5, 2, 6, 1, 7)
S_STATE, S_SLOTS, S_SOFT, S_BACK, S_RESULT, S_DECODE = range(6)


def mm(a, b, dims, precision=None):
    return lax.dot_general(a, b, dims, precision=precision, preferred_element_type=f32)


def head_cols(h):
    return slice(h * DH, (h + 1) * DH)


def expand(rows):
    return jnp.concatenate(
        [jnp.broadcast_to(rows[i : i + 1], (8, DH)) for i in range(HEADS // 2)], axis=0
    )


def kernel(
    pages_in, q_in, k_in, v_in, g_in, gain_in, ck_in, cv_in,
    stq_in, stk_in, stv_in, std_in, sfq_in, sfk_in, sfv_in,
    mixed, sums_ref, dec_own, soft_ref, gain_ref,
    pages_ref, q_ref, k_ref, v_ref, g_ref, ck_ref, cv_ref,
    stq_ref, stk_ref, stv_ref, std_ref, sfq_ref, sfk_ref, sfv_ref,
    ccol, crow, states, before, weights, stq, stk, stv, std, sfq, sfk, sfv,
    other_k, other_v, other_q, query_all, read_rows,
    pair_state, pair_state_in, pair_weight, pair_weight_in, pair_slots, pair_slots_in,
    send_state, recv_state, send_slots, recv_slots, send_soft, recv_soft,
    carry, send_back, recv_back, pair_carry, pair_carry_in, carry_all,
    pair_final, pair_final_in, final_all, square_sums, send_result, recv_result, send_decode, recv_decode, send_tp,
    pair_send, pair_recv, seq_send, seq_recv, tp_send, tp_recv, in_sem,
):
    me = lax.axis_index("seq")
    tp = lax.axis_index("tp")
    rep = lax.axis_index("rep")
    first_core = rep == 0
    own_rows = pl.ds(pl.multiple_of(rep * HALF, HALF), HALF)
    other_rows = pl.ds(pl.multiple_of((1 - rep) * HALF, HALF), HALF)

    def page_rows(k):
        return pl.ds(k * PAGE, PAGE)

    inputs = {}

    def fetch(name, src, dst):
        inputs[name] = pltpu.make_async_copy(src, dst, in_sem.at[len(inputs)])
        inputs[name].start()

    fetch("pages", pages_in, pages_ref)
    fetch("g", g_in, g_ref)
    for k in range(PAGES_DEV):
        fetch(("k", k), k_in.at[page_rows(k)], k_ref.at[page_rows(k)])
        fetch(("v", k), v_in.at[page_rows(k)], v_ref.at[page_rows(k)])
    fetch("q", q_in, q_ref)
    fetch("ck", ck_in, ck_ref)
    fetch("cv", cv_in, cv_ref)
    small = (
        (stq_in, stq_ref), (stk_in, stk_ref), (stv_in, stv_ref), (std_in, std_ref),
        (sfq_in, sfq_ref), (sfk_in, sfk_ref), (sfv_in, sfv_ref),
    )
    for n, (src, dst) in enumerate(small):
        fetch(("small", n), src.at[0], dst)
    fetch("gain", gain_in, gain_ref)

    me_x, me_y = me // 4, lax.rem(me, 4)

    def seq_ahead(hop):
        return lax.rem(me_x + hop // 4, 4) * 4 + lax.rem(me_y + hop % 4, 4)

    def seq_behind(hop):
        return lax.rem(me_x + 4 - hop // 4, 4) * 4 + lax.rem(me_y + 4 - hop % 4, 4)

    def pair_copy(which, src, dst):
        return pltpu.make_async_remote_copy(
            src_ref=src, dst_ref=dst, send_sem=pair_send.at[which], recv_sem=pair_recv.at[which],
            device_id=(me, tp, 1 - rep), device_id_type=MESH,
        )

    def seq_copy(phase, src, dst, hop):
        target = seq_ahead(hop)
        return pltpu.make_async_remote_copy(
            src_ref=src(target), dst_ref=dst.at[me],
            send_sem=seq_send.at[phase, hop], recv_sem=seq_recv.at[phase, hop],
            device_id=(target, tp, rep), device_id_type=MESH,
        )

    def seq_start(phase, src, dst):
        for hop in SEQ_HOPS:
            seq_copy(phase, src, dst, hop).start()

    def seq_wait(phase, src, dst):
        for hop in SEQ_HOPS:
            source = seq_behind(hop)
            pltpu.make_async_remote_copy(
                src_ref=src(source), dst_ref=dst.at[source],
                send_sem=seq_send.at[phase, hop], recv_sem=seq_recv.at[phase, hop],
                device_id=(source, tp, rep), device_id_type=MESH,
            ).wait_recv()

    def seq_sent(phase, src, dst):
        for hop in SEQ_HOPS:
            seq_copy(phase, src, dst, hop).wait_send()

    src_state = lambda t: send_state.at[t]
    src_slots = lambda t: send_slots.at[t]
    src_soft = lambda t: send_soft.at[t]
    src_back = lambda t: send_back.at[t]
    src_result = lambda t: send_result
    src_decode = lambda t: send_decode

    def tp_copy(hop):
        return pltpu.make_async_remote_copy(
            src_ref=send_tp, dst_ref=sums_ref.at[tp],
            send_sem=tp_send.at[hop], recv_sem=tp_recv.at[hop],
            device_id=(me, lax.rem(tp + hop, TP), rep), device_id_type=MESH,
        )

    barrier = pltpu.get_barrier_semaphore()

    for hop in SEQ_HOPS:
        pl.semaphore_signal(
            barrier, inc=1, device_id=(seq_ahead(hop), tp, rep), device_id_type=MESH
        )
    for hop in TP_HOPS:
        pl.semaphore_signal(
            barrier, inc=1, device_id=(me, lax.rem(tp + hop, TP), rep), device_id_type=MESH
        )
    pl.semaphore_signal(barrier, inc=1, device_id=(me, tp, 1 - rep), device_id_type=MESH)

    inputs["pages"].wait()
    ends = []
    for p in range(DOCS):
        ends.append(pages_ref[p] + (ends[-1] if ends else 0))
    chip_page = me * (2 * PAGES_DEV)
    dev_page = chip_page + rep * PAGES_DEV

    def flag(cond):
        return jnp.where(cond, 1, 0).astype(jnp.int32)

    def goes_on(page):
        hits = sum(flag(e == page) for e in ends)
        return jnp.where(hits == 0, 1.0, 0.0).astype(f32)

    def doc_of(page):
        return sum((e <= page).astype(jnp.int32) for e in ends)

    slot_page, slot_valid, slot_doc = [], [], []
    inside = [flag(jnp.logical_and(e > chip_page, e < chip_page + 2 * PAGES_DEV)) for e in ends]
    for s in range(2):
        place, owner = 0, 0
        for p in range(DOCS):
            rank = sum(inside[:p]) if p else 0
            place = place + inside[p] * flag(rank == s) * (ends[p] - chip_page)
            owner = owner + inside[p] * flag(rank == s) * p
        local = place - 1 - rep * PAGES_DEV
        ok = jnp.logical_and(
            place > 0, jnp.logical_and(local >= 0, local < PAGES_DEV)
        )
        slot_doc.append(owner)
        slot_page.append(jnp.clip(local, 0, PAGES_DEV - 1))
        slot_valid.append(jnp.where(ok, 1.0, 0.0).astype(f32))

    rows_i = lax.broadcasted_iota(jnp.int32, (PAGE, PAGE), 0)
    cols_i = lax.broadcasted_iota(jnp.int32, (PAGE, PAGE), 1)
    states[0] = jnp.zeros((SEQ, 2 * HALF, DH), f32)

    inputs["g"].wait()
    g = g_ref[...] * LOG2E
    g_high = g.astype(bf16)
    g_rest = g - g_high.astype(f32)
    g_mid = g_rest.astype(bf16)
    g_low = (g_rest - g_mid.astype(f32)).astype(bf16)
    upper = (rows_i <= cols_i).astype(f32).astype(bf16)
    parts = [
        x[:, k * PAGE : (k + 1) * PAGE].astype(f32)
        for x in (g_high, g_mid, g_low)
        for k in range(PAGES_DEV)
    ]
    summed = mm(jnp.concatenate(parts, axis=0).astype(bf16), upper, NN)
    wide = PAGES_DEV * HEADS
    summed = summed[0:wide] + summed[wide : 2 * wide] + summed[2 * wide :]
    turned = jnp.transpose(summed)

    def state_page(k, carried):
        rows = page_rows(k)
        c = turned[:, k * HEADS : (k + 1) * HEADS]
        ccol[rows, :] = c
        line = summed[k * HEADS : (k + 1) * HEADS]
        crow[k] = line
        decay = jnp.exp2(jnp.broadcast_to(line[:, PAGE - 1 : PAGE], (HEADS, DH)))
        cont = goes_on(dev_page + k)
        before[k] = carried * cont
        keep = decay * cont
        after = carried * keep
        weights[k] = after
        fade = jnp.exp2(c[PAGE - 1 : PAGE, :] - c)
        for h in range(HEADS):
            kd = (k_ref[rows, head_cols(h)].astype(f32) * fade[:, h : h + 1]).astype(bf16)
            add = mm(v_ref[rows, head_cols(h)], kd, TN)
            old = states[k, :, h * 8 : h * 8 + 8, :]
            states[k + 1, :, h * 8 : h * 8 + 8, :] = old * keep[h : h + 1, :][None] + add.reshape(
                SEQ, 8, DH
            )
        return after

    total = jnp.ones((HEADS, DH), f32)
    for k in range(PAGES_DEV):
        inputs[("k", k)].wait()
        inputs[("v", k)].wait()
        total = state_page(k, total)

    pair_state[...] = states[PAGES_DEV, :, other_rows, :].astype(bf16)
    pair_weight[0:8] = total
    for s in range(2):
        w = jnp.zeros((HEADS, DH), f32)
        for k in range(PAGES_DEV):
            pick = jnp.where(slot_page[s] == k, slot_valid[s], 0.0).astype(f32)
            w = w + pick * weights[k]
        pair_weight[8 + 8 * s : 16 + 8 * s] = w
    pl.semaphore_wait(barrier, SEQ - 1 + TP - 1 + 1)
    pair_copy(P_STATE, pair_state, pair_state_in).start()
    pair_copy(P_WEIGHT, pair_weight, pair_weight_in).start()
    for s in range(2):
        pair_slots[s] = (states[slot_page[s] + 1][:, 0:HALF, :] * slot_valid[s]).astype(bf16)
        pair_slots[2 + s] = (states[slot_page[s] + 1][:, HALF:, :] * slot_valid[s]).astype(bf16)
    pair_other = pair_slots.at[pl.ds((1 - rep) * 2, 2)]
    pair_copy(P_SLOTS, pair_other, pair_slots_in).start()
    pair_copy(P_QUERY, stq_in.at[0], other_q).start()
    pair_copy(P_KEYS, ck_in, other_k).start()
    pair_copy(P_VALUES, cv_in, other_v).start()

    causal = rows_i >= cols_i

    def inside_page(k):
        rows = pl.ds(pl.multiple_of(k * PAGE, PAGE), PAGE)
        c = ccol[rows, :]
        r = crow[k]
        rise = jnp.exp2(c)
        for h in range(HEADS):
            scores = mm(q_ref[rows, head_cols(h)], k_ref[rows, head_cols(h)], NT)
            grid = jnp.exp2(c[:, h : h + 1] - r[h : h + 1, :])
            block = jnp.where(causal, scores * grid, 0.0).astype(bf16)
            mixed[rows, head_cols(h)] = mm(block, v_ref[rows, head_cols(h)], NN)
            q_ref[rows, head_cols(h)] = (
                q_ref[rows, head_cols(h)].astype(f32) * rise[:, h : h + 1]
            ).astype(bf16)

    def inside_loop(first, last):
        def one(k, _):
            inside_page(k)
            return 0

        lax.fori_loop(first, last, one, 0)


    def half(x):
        return lax.select(first_core, x[0:4], x[4:8])

    pair_copy(P_STATE, pair_state, pair_state_in).wait_recv()
    pair_copy(P_WEIGHT, pair_weight, pair_weight_in).wait_recv()
    own_state = states[PAGES_DEV, :, own_rows, :]
    got_state = pair_state_in[...].astype(f32)
    state0 = lax.select(first_core, own_state, got_state)
    state1 = lax.select(first_core, got_state, own_state)
    own_w = [half(pair_weight[8 * n : 8 * n + 8]) for n in range(3)]
    got_w = [half(pair_weight_in[8 * n : 8 * n + 8]) for n in range(3)]
    w0 = [lax.select(first_core, a, b) for a, b in zip(own_w, got_w)]
    w1 = [lax.select(first_core, b, a) for a, b in zip(own_w, got_w)]
    chip_state = expand(w1[0])[None] * state0 + state1
    chip_w = jnp.concatenate([w1[0] * w0[0], w0[1] + w1[1] * w0[0]], axis=0)
    chip_hi = chip_w.astype(bf16).astype(f32)
    chip_rows = jnp.concatenate([chip_hi, chip_w - chip_hi], axis=0).astype(bf16)
    send_state[:, 0:HALF, :] = chip_state.astype(bf16)
    send_state[:, HALF:, :] = jnp.broadcast_to(chip_rows[None], (SEQ, 16, DH))
    seq_start(S_STATE, src_state, recv_state)
    recv_state[me] = send_state[me]

    for n in range(len(small)):
        inputs[("small", n)].wait()
    for p in range(DOCS):
        part = slice(4 * p, 4 * p + 4)
        stq[part, :] = stq_ref[p].astype(f32)
        stk[part, :] = stk_ref[p].astype(f32)
        stv[part, :] = stv_ref[p].astype(f32)
        std[part, :] = std_ref[p]
        sfk[p] = sfk_ref[p].astype(f32)
        sfv[p] = sfv_ref[p].astype(f32)
        for h in range(HEADS):
            sfq[pl.ds(p * 32 + h, 4, stride=8), :] = sfq_ref[p, :, head_cols(h)].astype(f32)

    pair_copy(P_QUERY, stq_in.at[0], other_q).wait_recv()
    other_lines = jnp.concatenate([other_q[p].astype(f32) for p in range(DOCS)], axis=0)
    query_all[pl.ds(pl.multiple_of(rep * 16, 16), 16), :] = stq[...].astype(bf16)
    query_all[pl.ds(pl.multiple_of((1 - rep) * 16, 16), 16), :] = other_lines.astype(bf16)

    def half_query(n):
        return query_all[:, pl.ds(pl.multiple_of((rep * (HEADS // 2) + n) * DH, DH), DH)]

    def iota(shape, dim):
        return lax.broadcasted_iota(jnp.int32, shape, dim)

    pair_copy(P_SLOTS, pair_other, pair_slots_in).wait_recv()
    slots = []
    for s in range(2):
        own_slot = states[slot_page[s] + 1][:, 0:HALF, :]
        own_slot = lax.select(first_core, own_slot, states[slot_page[s] + 1][:, HALF:, :])
        slot = own_slot * slot_valid[s] + pair_slots_in[s].astype(f32)
        slots.append(slot + expand(w1[1 + s])[None] * state0)
    lane_doc = jnp.bitwise_and(iota((DH, 32), 1), 15) // STEPS
    reads = []
    for n in range(HEADS // 2):
        read = jnp.zeros((DH, 32), f32)
        for s in range(2):
            state = slots[s][:, n * 8 : n * 8 + 8, :].reshape(DH, DH).astype(bf16)
            read = read + jnp.where(lane_doc == slot_doc[s], mm(state, half_query(n), NT), 0.0)
        reads.append(read)
    send_slots[...] = jnp.concatenate(reads, axis=1).reshape(SEQ, 8, DH)
    seq_start(S_SLOTS, src_slots, recv_slots)
    recv_slots[me] = send_slots[me]

    chain = jnp.logical_and(
        iota((16, 16), 0) // STEPS == iota((16, 16), 1) // STEPS, iota((16, 16), 0) >= iota((16, 16), 1)
    )
    fall = mm(chain.astype(f32), std[...] * LOG2E, NN, highest)
    spread_heads = (iota((HEADS, DH), 1) // 16 == iota((HEADS, DH), 0)).astype(f32)
    fall_from = mm(fall, spread_heads, NN, highest)
    lane_step = jnp.bitwise_and(iota((16, DH), 1), 15)
    diagonal = jnp.where(lane_step == iota((16, DH), 0), fall_from, 0.0)
    fall_to = mm(jnp.ones((16, 16), f32), diagonal, NN, highest)
    linked = jnp.logical_and(
        iota((16, DH), 0) // STEPS == lane_step // STEPS, iota((16, DH), 0) >= lane_step
    )
    met = jnp.concatenate(
        [
            mm(stq[:, head_cols(h)].astype(bf16), stk[:, head_cols(h)].astype(bf16), NT)
            for h in range(HEADS)
        ],
        axis=1,
    )
    met = jnp.where(linked, met * jnp.exp2(fall_from - fall_to), 0.0)
    cols = HEADS * 8
    pick = (iota((DH, cols), 0) == jnp.bitwise_and(iota((DH, cols), 1), 7) + me * 8).astype(f32)
    values = jnp.concatenate([stv[:, head_cols(h)] for h in range(HEADS)], axis=0)
    values = mm(values.astype(bf16), pick.astype(bf16), NN)
    values = jnp.where(iota((DH, cols), 0) // 16 == iota((DH, cols), 1) // 8, values, 0.0)
    decoded = mm(met, values, NN, highest)
    spread_cols = (iota((HEADS, cols), 1) // 8 == iota((HEADS, cols), 0)).astype(f32)
    shrunk = jnp.exp2(mm(fall, spread_cols, NN, highest))

    inputs["ck"].wait()
    inputs["cv"].wait()
    scale = DH**-0.5 * LOG2E
    pair_copy(P_KEYS, ck_in, other_k).wait_recv()
    pair_copy(P_VALUES, cv_in, other_v).wait_recv()
    queries = sfq[...].astype(bf16)
    query_doc = lax.broadcasted_iota(jnp.int32, (DH, ROWS), 0) // 32
    key_page = lax.broadcasted_iota(jnp.int32, (1, ROWS), 1) // PAGE
    score, here = [], []
    for base, key_block in ((dev_page, ck_ref), (chip_page + (1 - rep) * PAGES_DEV, other_k)):
        score.append(mm(queries, key_block[...], NT) * scale)
        here.append(query_doc == jnp.broadcast_to(doc_of(key_page + base), (DH, ROWS)))
    peak = jnp.maximum(
        *[
            jnp.max(jnp.where(m, s, mask_low), axis=1, keepdims=True)
            for m, s in zip(here, score)
        ]
    )
    chance = [jnp.where(m, jnp.exp2(s - peak), 0.0) for m, s in zip(here, score)]
    amount = sum(jnp.sum(x, axis=1, keepdims=True) for x in chance)
    numer = mm(chance[0].astype(bf16), cv_ref[...], NN) + mm(
        chance[1].astype(bf16), other_v[...], NN
    )
    lane = lax.broadcasted_iota(jnp.int32, (DH, DH), 1)
    both = jnp.where(lane < 64, jnp.broadcast_to(peak, (DH, DH)), jnp.broadcast_to(amount, (DH, DH)))
    send_soft[:, 0:8, :] = numer.reshape(SEQ, 8, DH)
    send_soft[:, 8:16, :] = both.reshape(SEQ, 8, DH)
    seq_start(S_SOFT, src_soft, recv_soft)
    recv_soft[me] = send_soft[me]

    seq_wait(S_STATE, src_state, recv_state)
    running = jnp.zeros((HALF, DH), f32)
    for j in range(SEQ):
        carry[j] = running
        send_back[j] = running.astype(bf16)
        rows = recv_state[j, HALF:, :].astype(f32)
        running = expand(rows[0:4] + rows[8:12]) * running + recv_state[j, 0:HALF, :].astype(f32)
    carry[SEQ] = running
    seq_start(S_BACK, src_back, recv_back)
    recv_back[me] = send_back[me]

    seq_wait(S_SLOTS, src_slots, recv_slots)
    for p in range(DOCS):
        last_page = jnp.clip(ends[p] - 1, 0, 2 * PAGES_DEV * SEQ - 1)
        chip = lax.shift_right_logical(last_page, 3)
        chip_last = jnp.bitwise_and(last_page, 7) == 7
        rank = sum(
            [flag(lax.shift_right_logical(ends[o] - 1, 3) == chip) for o in range(p)],
            jnp.int32(0),
        )
        rows = recv_state[chip][HALF:, :].astype(f32)
        w = expand(rows[4:8] + rows[12:16]) * jnp.where(rank == 0, 1.0, 0.0).astype(f32)
        final_all[p] = lax.select(chip_last, carry[chip + 1], w * carry[chip])
    tile = recv_slots[0]
    for j in range(1, SEQ):
        tile = tile + recv_slots[j]
    reads = []
    for n in range(HEADS // 2):
        state = final_all[:, n * 8 : n * 8 + 8, :].reshape(DOCS * 8, DH).astype(bf16)
        read = mm(state, half_query(n), NT)
        read = jnp.where(iota((32, 32), 0) // 8 == lane_doc[0:32], read, 0.0)
        reads.append(read[0:8] + read[8:16] + read[16:24] + read[24:32])
    pair_final[...] = tile + jnp.concatenate(reads, axis=1)
    pair_copy(P_FINAL, pair_final, pair_final_in).start()

    inputs["q"].wait()
    inside_loop(0, 1)

    pair_copy(P_FINAL, pair_final, pair_final_in).wait_recv()
    own_tile, got_tile = pair_final[...], pair_final_in[...]
    tiles = [lax.select(first_core, own_tile, got_tile), lax.select(first_core, got_tile, own_tile)]
    read_rows[...] = jnp.transpose(jnp.concatenate(tiles, axis=0))
    lines_of = [
        read_rows[pl.ds(pl.multiple_of(n * 32 + rep * 16, 16), 16), :] for n in range(HEADS // 2)
    ]
    read = jnp.concatenate([x[:, 8 * n : 8 * n + 8] for n in range(2) for x in lines_of], axis=1)
    decoded = decoded + read * shrunk
    dec_own[...] = decoded
    squares = mm(jnp.ones((8, cols), f32), decoded * decoded, NT, highest)
    send_decode[...] = jnp.zeros((1, DH), f32)
    send_decode[:, 0:16] = squares[0:1, :]
    seq_start(S_DECODE, src_decode, recv_decode)
    recv_decode[me] = send_decode[...]

    inside_loop(1, 4)

    seq_wait(S_BACK, src_back, recv_back)
    carry0 = recv_back[...].astype(f32)
    carry1 = expand(w0[0])[None] * carry0 + state0
    carry_all[:, own_rows, :] = lax.select(first_core, carry0, carry1)
    pair_carry[...] = lax.select(first_core, carry1, carry0).astype(bf16)
    pair_copy(P_CARRY, pair_carry, pair_carry_in).start()


    seq_wait(S_SOFT, src_soft, recv_soft)
    doc = me // STEPS
    step = lax.rem(me, STEPS)
    own_q = sfq[pl.ds(pl.multiple_of(me * 8, 8), 8), :]
    own_k = sfk[doc]
    own_v = sfv[doc]
    peaks = [recv_soft[s, 8:16, 0:1] for s in range(SEQ)]
    amounts = [recv_soft[s, 8:16, 64:65] for s in range(SEQ)]
    numers = [recv_soft[s, 0:8, :] for s in range(SEQ)]
    top = peaks[0]
    for x in peaks[1:]:
        top = jnp.maximum(top, x)
    own = []
    for i in range(STEPS):
        s = jnp.sum(own_q * own_k[i : i + 1, :], axis=1, keepdims=True) * scale
        own.append(lax.select(step >= i, s, jnp.full((8, 1), mask_low, f32)))
        top = jnp.maximum(top, own[-1])
    numer = jnp.zeros((8, DH), f32)
    amount = jnp.zeros((8, 1), f32)
    for s in range(SEQ):
        shrink = jnp.exp2(peaks[s] - top)
        numer = numer + numers[s] * shrink
        amount = amount + amounts[s] * shrink
    for i in range(STEPS):
        e = lax.select(step >= i, jnp.exp2(own[i] - top), jnp.zeros((8, 1), f32))
        numer = numer + e.astype(bf16).astype(f32) * own_v[i : i + 1, :]
        amount = amount + e
    send_result[...] = numer / amount
    seq_start(S_RESULT, src_result, recv_result)
    recv_result[me] = send_result[...]

    pair_copy(P_CARRY, pair_carry, pair_carry_in).wait_recv()
    carry_all[:, other_rows, :] = pair_carry_in[...].astype(f32)
    for k in range(PAGES_DEV):
        rows = page_rows(k)
        cont = goes_on(dev_page + k)
        w = before[k]
        squares = jnp.zeros((PAGE, DH), f32)
        for h in range(HEADS):
            part = slice(h * 8, h * 8 + 8)
            state = states[k, :, part, :] * cont + carry_all[:, part, :] * w[h : h + 1, :][None]
            qd = q_ref[rows, head_cols(h)]
            value = mixed[rows, head_cols(h)] + mm(qd, state.reshape(DH, DH).astype(bf16), NT)
            mixed[rows, head_cols(h)] = value
            squares = squares + value * value
        high = squares.astype(bf16)
        rest = (squares - high.astype(f32)).astype(bf16)
        ones = jnp.ones((16, DH), bf16)
        line = mm(ones, high, NT) + mm(ones, rest, NT)
        for n in range(PAGE // DH):
            send_tp[2 * k + n : 2 * k + n + 1, :] = line[0:1, head_cols(n)]


    seq_wait(S_DECODE, src_decode, recv_decode)
    decode_squares = recv_decode[0]
    for s in range(1, SEQ):
        decode_squares = decode_squares + recv_decode[s]
    send_tp[8:16, :] = jnp.broadcast_to(decode_squares, (8, DH))

    for hop in TP_HOPS:
        tp_copy(hop).start()
    sums_ref[tp] = send_tp[...]
    seq_wait(S_RESULT, src_result, recv_result)
    soft_ref[...] = recv_result[...]
    inputs["gain"].wait()
    for hop in TP_HOPS:
        source = lax.rem(tp + TP - hop, TP)
        pltpu.make_async_remote_copy(
            src_ref=send_tp, dst_ref=sums_ref.at[source],
            send_sem=tp_send.at[hop], recv_sem=tp_recv.at[hop],
            device_id=(me, source, rep), device_id_type=MESH,
        ).wait_recv()

    for which, src, dst in (
        (P_QUERY, stq_in.at[0], other_q),
        (P_KEYS, ck_in, other_k),
        (P_VALUES, cv_in, other_v),
        (P_STATE, pair_state, pair_state_in),
        (P_WEIGHT, pair_weight, pair_weight_in),
        (P_SLOTS, pair_other, pair_slots_in),
        (P_CARRY, pair_carry, pair_carry_in),
        (P_FINAL, pair_final, pair_final_in),
    ):
        pair_copy(which, src, dst).wait_send()
    seq_sent(S_STATE, src_state, recv_state)
    seq_sent(S_SLOTS, src_slots, recv_slots)
    seq_sent(S_SOFT, src_soft, recv_soft)
    seq_sent(S_BACK, src_back, recv_back)

    seq_sent(S_RESULT, src_result, recv_result)
    seq_sent(S_DECODE, src_decode, recv_decode)
    for hop in TP_HOPS:
        tp_copy(hop).wait_send()


def norm_kernel(
    mixed, sums, decoded, soft, gain_ref, out_hbm, dec_hbm, soft_hbm, block, dec_lines, dec_block, soft_block, sem
):
    me = lax.axis_index("seq")
    features = TP * HEADS * DH
    copies = []

    def send(src, dst):
        copy = pltpu.make_async_copy(src, dst, sem.at[len(copies)])
        copy.start()
        copies.append(copy)

    gain = gain_ref[...]
    total = sums[0, 0:8, :]
    for t in range(1, TP):
        total = total + sums[t, 0:8, :]
    factors = lax.rsqrt(total / features + norm_eps)
    for b in range(ROWS // DH):
        rows = slice(b * DH, (b + 1) * DH)
        factor = jnp.transpose(jnp.broadcast_to(factors[b : b + 1, :], (DH, DH)))
        for h in range(HEADS):
            block[rows, head_cols(h)] = (
                mixed[rows, head_cols(h)] * factor * gain[h : h + 1, :]
            ).astype(bf16)
        send(block.at[rows], out_hbm.at[rows])

    def iota(shape, dim):
        return lax.broadcasted_iota(jnp.int32, shape, dim)

    cols = HEADS * 8
    pick = (iota((DH, cols), 0) == jnp.bitwise_and(iota((DH, cols), 1), 7) + me * 8).astype(f32)
    gain_cols = mm(gain, pick, NN, highest)
    gain_cols = jnp.where(iota((HEADS, cols), 1) // 8 == iota((HEADS, cols), 0), gain_cols, 0.0)
    gain_cols = jnp.sum(gain_cols, axis=0, keepdims=True)
    total = mm(sums[:, 8, :], jnp.ones((TP, cols), f32), TN, highest)[0:16]
    value = decoded[...] * lax.rsqrt(total / features + norm_eps) * gain_cols
    for h in range(HEADS):
        dec_lines[pl.ds(h, 16, stride=8), :] = value[:, h * 8 : h * 8 + 8]
    dec_block[...] = dec_lines[...].reshape(DOCS, STEPS, HEADS, 8).astype(bf16)
    send(dec_block, dec_hbm.at[0])
    for p in range(DOCS):
        for h in range(HEADS):
            soft_block[p, :, head_cols(h)] = soft[pl.ds(p * 32 + h, 4, stride=8), :].astype(bf16)
    send(soft_block, soft_hbm.at[0])
    for copy in copies:
        copy.wait()


def per_device(
    light_query, light_key, light_value, log_decay, prompt_pages, norm_gain, cache_keys,
    cache_values, step_query, step_key, step_value, step_decay, soft_query, soft_key, soft_value,
):
    vm = pl.BlockSpec(memory_space=pltpu.VMEM)
    V = pltpu.VMEM
    D = pltpu.SemaphoreType.DMA
    mixed, sums, dec, soft, gain = pl.pallas_call(
        kernel,
        out_shape=(
            jax.ShapeDtypeStruct((ROWS, HEADS * DH), f32),
            jax.ShapeDtypeStruct((TP, 16, DH), f32),
            jax.ShapeDtypeStruct((16, HEADS * 8), f32),
            jax.ShapeDtypeStruct((SEQ, 8, DH), f32),
            jax.ShapeDtypeStruct((HEADS, DH), f32),
        ),
        in_specs=[pl.BlockSpec(memory_space=pltpu.HBM)] * 15,
        out_specs=(vm,) * 5,
        scratch_shapes=[
            pltpu.SMEM((DOCS,), jnp.int32),
            V((ROWS, HEADS * DH), bf16),
            V((ROWS, HEADS * DH), bf16),
            V((ROWS, HEADS * DH), bf16),
            V((HEADS, ROWS), f32),
            V((ROWS, DH), bf16),
            V((ROWS, DH), bf16),
            V((DOCS, STEPS, HEADS * DH), bf16),
            V((DOCS, STEPS, HEADS * DH), bf16),
            V((DOCS, STEPS, HEADS * DH), bf16),
            V((DOCS, STEPS, HEADS), f32),
            V((DOCS, STEPS, HEADS * DH), bf16),
            V((DOCS, STEPS, DH), bf16),
            V((DOCS, STEPS, DH), bf16),
            V((ROWS, HEADS), f32),
            V((PAGES_DEV, HEADS, PAGE), f32),
            V((PAGES_DEV + 1, SEQ, 2 * HALF, DH), f32),
            V((PAGES_DEV, HEADS, DH), f32),
            V((PAGES_DEV, HEADS, DH), f32),
            V((16, HEADS * DH), f32),
            V((16, HEADS * DH), f32),
            V((16, HEADS * DH), f32),
            V((16, HEADS), f32),
            V((DH, DH), f32),
            V((DOCS, STEPS, DH), f32),
            V((DOCS, STEPS, DH), f32),
            V((ROWS, DH), bf16),
            V((ROWS, DH), bf16),
            V((DOCS, STEPS, HEADS * DH), bf16),
            V((32, HEADS * DH), bf16),
            V((DH, 16), f32),
            V((SEQ, HALF, DH), bf16),
            V((SEQ, HALF, DH), bf16),
            V((24, DH), f32),
            V((24, DH), f32),
            V((4, SEQ, HALF, DH), bf16),
            V((2, SEQ, HALF, DH), bf16),
            V((SEQ, HALF + 16, DH), bf16),
            V((SEQ, HALF + 16, DH), bf16),
            V((SEQ, 8, DH), f32),
            V((SEQ, 8, DH), f32),
            V((SEQ, 16, DH), f32),
            V((SEQ, 16, DH), f32),
            V((SEQ + 1, HALF, DH), f32),
            V((SEQ, HALF, DH), bf16),
            V((SEQ, HALF, DH), bf16),
            V((SEQ, HALF, DH), bf16),
            V((SEQ, HALF, DH), bf16),
            V((SEQ, 2 * HALF, DH), f32),
            V((8, DH), f32),
            V((8, DH), f32),
            V((DOCS, HALF, DH), f32),
            V((ROWS, DH), f32),
            V((8, DH), f32),
            V((SEQ, 8, DH), f32),
            V((1, DH), f32),
            V((SEQ, 1, DH), f32),
            V((16, DH), f32),
            D((8,)),
            D((8,)),
            D((6, SEQ)),
            D((6, SEQ)),
            D((TP,)),
            D((TP,)),
            D((21,)),
        ],
        compiler_params=pltpu.CompilerParams(
            collective_id=0, has_side_effects=True, vmem_limit_bytes=48 * 1024 * 1024
        ),
        name="attention_block",
    )(*[pltpu.with_memory_space_constraint(x, pltpu.HBM) for x in (
        prompt_pages, light_query, light_key, light_value, log_decay.T,
        norm_gain.reshape(HEADS, DH), cache_keys, cache_values,
        step_query, step_key, step_value, step_decay, soft_query, soft_key, soft_value,
    )])
    hbm = pl.BlockSpec(memory_space=pl.ANY)
    return pl.pallas_call(
        norm_kernel,
        out_shape=(
            jax.ShapeDtypeStruct((ROWS, HEADS * DH), bf16),
            jax.ShapeDtypeStruct((1, DOCS, STEPS, HEADS, 8), bf16),
            jax.ShapeDtypeStruct((1, DOCS, STEPS, HEADS * DH), bf16),
        ),
        in_specs=[vm] * 5,
        out_specs=(hbm,) * 3,
        scratch_shapes=[
            V((ROWS, HEADS * DH), bf16),
            V((16 * HEADS, 8), f32),
            V((DOCS, STEPS, HEADS, 8), bf16),
            V((DOCS, STEPS, HEADS * DH), bf16),
            D((10,)),
        ],
        compiler_params=pltpu.CompilerParams(vmem_limit_bytes=16 * 1024 * 1024),
        name="norms",
    )(mixed, sums, dec, soft.reshape(SEQ * 8, DH), gain)


def solution(mesh):
    prompt = P(("seq", "rep"), "tp")
    sample = P("rep", None, None, "tp")
    return jax.shard_map(
        per_device,
        mesh=mesh,
        in_specs=(prompt,) * 4 + (P(), P("tp")) + (prompt,) * 2 + (sample,) * 7,
        out_specs=(prompt, P("rep", None, None, "tp", "seq"), sample),
        check_vma=False,
    )
```

```python
import math

import jax
import jax.numpy as jnp
from jax import lax
from jax.experimental import pallas as pl
from jax.experimental.pallas import tpu as pltpu
from jax.sharding import PartitionSpec as P

DH = 128
PAGE = 256
DOCS = 4
STEPS = 4
HEADS = 8
SEQ = 16
TP = 8
ROWS = 1024
PAGES_DEV = ROWS // PAGE
HALF = HEADS // 2 * 8

norm_eps = 1e-06
mask_low = -1e30
LOG2E = math.log2(math.e)
highest = lax.Precision.HIGHEST
f32 = jnp.float32
bf16 = jnp.bfloat16
MESH = pl.DeviceIdType.MESH

NN = (((1,), (0,)), ((), ()))
NT = (((1,), (1,)), ((), ()))
TN = (((0,), (0,)), ((), ()))

P_KEYS, P_VALUES, P_STATE, P_WEIGHT, P_SLOTS, P_CARRY, P_FINAL, P_QUERY = range(8)
SEQ_HOPS = (10, 6, 9, 11, 14, 2, 8, 5, 7, 13, 15, 1, 3, 4, 12)
TP_HOPS = (4, 3, 5, 2, 6, 1, 7)
S_STATE, S_SLOTS, S_SOFT, S_BACK, S_RESULT, S_DECODE = range(6)


def mm(a, b, dims, precision=None):
    return lax.dot_general(a, b, dims, precision=precision, preferred_element_type=f32)


def head_cols(h):
    return slice(h * DH, (h + 1) * DH)


def expand(rows):
    return jnp.concatenate(
        [jnp.broadcast_to(rows[i : i + 1], (8, DH)) for i in range(HEADS // 2)], axis=0
    )


def kernel(
    pages_in, q_in, k_in, v_in, g_in, gain_in, ck_in, cv_in,
    stq_in, stk_in, stv_in, std_in, sfq_in, sfk_in, sfv_in,
    mixed, sums_ref, dec_own, soft_ref, gain_ref,
    pages_ref, q_ref, k_ref, v_ref, g_ref, ck_ref, cv_ref,
    stq_ref, stk_ref, stv_ref, std_ref, sfq_ref, sfk_ref, sfv_ref,
    ccol, crow, states, before, weights, stq, stk, stv, std, sfq, sfk, sfv,
    other_k, other_v, other_q, query_all, read_rows,
    pair_state, pair_state_in, pair_weight, pair_weight_in, pair_slots, pair_slots_in,
    send_state, recv_state, send_slots, recv_slots, send_soft, recv_soft,
    carry, send_back, recv_back, pair_carry, pair_carry_in, carry_all,
    pair_final, pair_final_in, final_all, square_sums, send_result, recv_result, send_decode, recv_decode, send_tp,
    pair_send, pair_recv, seq_send, seq_recv, tp_send, tp_recv, in_sem,
):
    me = lax.axis_index("seq")
    tp = lax.axis_index("tp")
    rep = lax.axis_index("rep")
    first_core = rep == 0
    own_rows = pl.ds(pl.multiple_of(rep * HALF, HALF), HALF)
    other_rows = pl.ds(pl.multiple_of((1 - rep) * HALF, HALF), HALF)

    me_x, me_y = me // 4, lax.rem(me, 4)

    def seq_ahead(hop):
        return lax.rem(me_x + hop // 4, 4) * 4 + lax.rem(me_y + hop % 4, 4)

    def seq_behind(hop):
        return lax.rem(me_x + 4 - hop // 4, 4) * 4 + lax.rem(me_y + 4 - hop % 4, 4)

    def pair_copy(which, src, dst):
        return pltpu.make_async_remote_copy(
            src_ref=src, dst_ref=dst, send_sem=pair_send.at[which], recv_sem=pair_recv.at[which],
            device_id=(me, tp, 1 - rep), device_id_type=MESH,
        )

    def seq_copy(phase, src, dst, hop):
        target = seq_ahead(hop)
        return pltpu.make_async_remote_copy(
            src_ref=src(target), dst_ref=dst.at[me],
            send_sem=seq_send.at[phase, hop], recv_sem=seq_recv.at[phase, hop],
            device_id=(target, tp, rep), device_id_type=MESH,
        )

    def seq_start(phase, src, dst):
        for hop in SEQ_HOPS:
            seq_copy(phase, src, dst, hop).start()

    def seq_wait(phase, src, dst):
        for hop in SEQ_HOPS:
            source = seq_behind(hop)
            pltpu.make_async_remote_copy(
                src_ref=src(source), dst_ref=dst.at[source],
                send_sem=seq_send.at[phase, hop], recv_sem=seq_recv.at[phase, hop],
                device_id=(source, tp, rep), device_id_type=MESH,
            ).wait_recv()

    def seq_sent(phase, src, dst):
        for hop in SEQ_HOPS:
            seq_copy(phase, src, dst, hop).wait_send()

    src_state = lambda t: send_state.at[t]
    src_slots = lambda t: send_slots.at[t]
    src_soft = lambda t: send_soft.at[t]
    src_back = lambda t: send_back.at[t]
    src_result = lambda t: send_result
    src_decode = lambda t: send_decode

    def tp_copy(hop):
        return pltpu.make_async_remote_copy(
            src_ref=send_tp, dst_ref=sums_ref.at[tp],
            send_sem=tp_send.at[hop], recv_sem=tp_recv.at[hop],
            device_id=(me, lax.rem(tp + hop, TP), rep), device_id_type=MESH,
        )

    barrier = pltpu.get_barrier_semaphore()

    for hop in SEQ_HOPS:
        pl.semaphore_signal(
            barrier, inc=1, device_id=(seq_ahead(hop), tp, rep), device_id_type=MESH
        )
    for hop in TP_HOPS:
        pl.semaphore_signal(
            barrier, inc=1, device_id=(me, lax.rem(tp + hop, TP), rep), device_id_type=MESH
        )
    pl.semaphore_signal(barrier, inc=1, device_id=(me, tp, 1 - rep), device_id_type=MESH)

    def page_rows(k):
        return pl.ds(k * PAGE, PAGE)

    inputs = {}

    def fetch(name, src, dst):
        inputs[name] = pltpu.make_async_copy(src, dst, in_sem.at[len(inputs)])
        inputs[name].start()

    fetch("pages", pages_in, pages_ref)
    fetch("g", g_in, g_ref)
    for k in range(PAGES_DEV):
        fetch(("k", k), k_in.at[page_rows(k)], k_ref.at[page_rows(k)])
        fetch(("v", k), v_in.at[page_rows(k)], v_ref.at[page_rows(k)])
    fetch("q", q_in, q_ref)
    fetch("ck", ck_in, ck_ref)
    fetch("cv", cv_in, cv_ref)
    small = (
        (stq_in, stq_ref), (stk_in, stk_ref), (stv_in, stv_ref), (std_in, std_ref),
        (sfq_in, sfq_ref), (sfk_in, sfk_ref), (sfv_in, sfv_ref),
    )
    for n, (src, dst) in enumerate(small):
        fetch(("small", n), src.at[0], dst)
    fetch("gain", gain_in, gain_ref)

    inputs["pages"].wait()
    ends = []
    for p in range(DOCS):
        ends.append(pages_ref[p] + (ends[-1] if ends else 0))
    chip_page = me * (2 * PAGES_DEV)
    dev_page = chip_page + rep * PAGES_DEV

    def flag(cond):
        return jnp.where(cond, 1, 0).astype(jnp.int32)

    def goes_on(page):
        hits = sum(flag(e == page) for e in ends)
        return jnp.where(hits == 0, 1.0, 0.0).astype(f32)

    def doc_of(page):
        return sum((e <= page).astype(jnp.int32) for e in ends)

    slot_page, slot_valid, slot_doc = [], [], []
    inside = [flag(jnp.logical_and(e > chip_page, e < chip_page + 2 * PAGES_DEV)) for e in ends]
    for s in range(2):
        place, owner = 0, 0
        for p in range(DOCS):
            rank = sum(inside[:p]) if p else 0
            place = place + inside[p] * flag(rank == s) * (ends[p] - chip_page)
            owner = owner + inside[p] * flag(rank == s) * p
        local = place - 1 - rep * PAGES_DEV
        ok = jnp.logical_and(
            place > 0, jnp.logical_and(local >= 0, local < PAGES_DEV)
        )
        slot_doc.append(owner)
        slot_page.append(jnp.clip(local, 0, PAGES_DEV - 1))
        slot_valid.append(jnp.where(ok, 1.0, 0.0).astype(f32))

    rows_i = lax.broadcasted_iota(jnp.int32, (PAGE, PAGE), 0)
    cols_i = lax.broadcasted_iota(jnp.int32, (PAGE, PAGE), 1)
    states[0] = jnp.zeros((SEQ, 2 * HALF, DH), f32)

    inputs["g"].wait()
    g = g_ref[...] * LOG2E
    g_high = g.astype(bf16)
    g_rest = g - g_high.astype(f32)
    g_mid = g_rest.astype(bf16)
    g_low = (g_rest - g_mid.astype(f32)).astype(bf16)
    upper = (rows_i <= cols_i).astype(f32).astype(bf16)
    parts = [
        x[:, k * PAGE : (k + 1) * PAGE].astype(f32)
        for x in (g_high, g_mid, g_low)
        for k in range(PAGES_DEV)
    ]
    summed = mm(jnp.concatenate(parts, axis=0).astype(bf16), upper, NN)
    wide = PAGES_DEV * HEADS
    summed = summed[0:wide] + summed[wide : 2 * wide] + summed[2 * wide :]
    turned = jnp.transpose(summed)

    def state_page(k, carried):
        rows = page_rows(k)
        c = turned[:, k * HEADS : (k + 1) * HEADS]
        ccol[rows, :] = c
        line = summed[k * HEADS : (k + 1) * HEADS]
        crow[k] = line
        decay = jnp.exp2(jnp.broadcast_to(line[:, PAGE - 1 : PAGE], (HEADS, DH)))
        cont = goes_on(dev_page + k)
        before[k] = carried * cont
        keep = decay * cont
        after = carried * keep
        weights[k] = after
        fade = jnp.exp2(c[PAGE - 1 : PAGE, :] - c)
        for h in range(HEADS):
            kd = (k_ref[rows, head_cols(h)].astype(f32) * fade[:, h : h + 1]).astype(bf16)
            add = mm(v_ref[rows, head_cols(h)], kd, TN)
            old = states[k, :, h * 8 : h * 8 + 8, :]
            states[k + 1, :, h * 8 : h * 8 + 8, :] = old * keep[h : h + 1, :][None] + add.reshape(
                SEQ, 8, DH
            )
        return after

    total = jnp.ones((HEADS, DH), f32)
    for k in range(PAGES_DEV):
        inputs[("k", k)].wait()
        inputs[("v", k)].wait()
        total = state_page(k, total)

    pair_state[...] = states[PAGES_DEV, :, other_rows, :].astype(bf16)
    pair_weight[0:8] = total
    for s in range(2):
        w = jnp.zeros((HEADS, DH), f32)
        for k in range(PAGES_DEV):
            pick = jnp.where(slot_page[s] == k, slot_valid[s], 0.0).astype(f32)
            w = w + pick * weights[k]
        pair_weight[8 + 8 * s : 16 + 8 * s] = w
    pl.semaphore_wait(barrier, SEQ - 1 + TP - 1 + 1)
    pair_copy(P_STATE, pair_state, pair_state_in).start()
    pair_copy(P_WEIGHT, pair_weight, pair_weight_in).start()
    for s in range(2):
        pair_slots[s] = (states[slot_page[s] + 1][:, 0:HALF, :] * slot_valid[s]).astype(bf16)
        pair_slots[2 + s] = (states[slot_page[s] + 1][:, HALF:, :] * slot_valid[s]).astype(bf16)
    pair_other = pair_slots.at[pl.ds((1 - rep) * 2, 2)]
    pair_copy(P_SLOTS, pair_other, pair_slots_in).start()
    pair_copy(P_QUERY, stq_in.at[0], other_q).start()
    pair_copy(P_KEYS, ck_in, other_k).start()
    pair_copy(P_VALUES, cv_in, other_v).start()

    causal = rows_i >= cols_i

    def inside_page(k):
        rows = pl.ds(pl.multiple_of(k * PAGE, PAGE), PAGE)
        c = ccol[rows, :]
        r = crow[k]
        rise = jnp.exp2(c)
        for h in range(HEADS):
            scores = mm(q_ref[rows, head_cols(h)], k_ref[rows, head_cols(h)], NT)
            grid = jnp.exp2(c[:, h : h + 1] - r[h : h + 1, :])
            block = jnp.where(causal, scores * grid, 0.0).astype(bf16)
            mixed[rows, head_cols(h)] = mm(block, v_ref[rows, head_cols(h)], NN)
            q_ref[rows, head_cols(h)] = (
                q_ref[rows, head_cols(h)].astype(f32) * rise[:, h : h + 1]
            ).astype(bf16)

    def inside_loop(first, last):
        def one(k, _):
            inside_page(k)
            return 0

        lax.fori_loop(first, last, one, 0)


    def half(x):
        return lax.select(first_core, x[0:4], x[4:8])

    pair_copy(P_STATE, pair_state, pair_state_in).wait_recv()
    pair_copy(P_WEIGHT, pair_weight, pair_weight_in).wait_recv()
    own_state = states[PAGES_DEV, :, own_rows, :]
    got_state = pair_state_in[...].astype(f32)
    state0 = lax.select(first_core, own_state, got_state)
    state1 = lax.select(first_core, got_state, own_state)
    own_w = [half(pair_weight[8 * n : 8 * n + 8]) for n in range(3)]
    got_w = [half(pair_weight_in[8 * n : 8 * n + 8]) for n in range(3)]
    w0 = [lax.select(first_core, a, b) for a, b in zip(own_w, got_w)]
    w1 = [lax.select(first_core, b, a) for a, b in zip(own_w, got_w)]
    chip_state = expand(w1[0])[None] * state0 + state1
    chip_w = jnp.concatenate([w1[0] * w0[0], w0[1] + w1[1] * w0[0]], axis=0)
    chip_hi = chip_w.astype(bf16).astype(f32)
    chip_rows = jnp.concatenate([chip_hi, chip_w - chip_hi], axis=0).astype(bf16)
    send_state[:, 0:HALF, :] = chip_state.astype(bf16)
    send_state[:, HALF:, :] = jnp.broadcast_to(chip_rows[None], (SEQ, 16, DH))
    seq_start(S_STATE, src_state, recv_state)
    recv_state[me] = send_state[me]

    for n in range(len(small)):
        inputs[("small", n)].wait()
    for p in range(DOCS):
        part = slice(4 * p, 4 * p + 4)
        stq[part, :] = stq_ref[p].astype(f32)
        stk[part, :] = stk_ref[p].astype(f32)
        stv[part, :] = stv_ref[p].astype(f32)
        std[part, :] = std_ref[p]
        sfk[p] = sfk_ref[p].astype(f32)
        sfv[p] = sfv_ref[p].astype(f32)
        for h in range(HEADS):
            sfq[pl.ds(p * 32 + h, 4, stride=8), :] = sfq_ref[p, :, head_cols(h)].astype(f32)

    pair_copy(P_QUERY, stq_in.at[0], other_q).wait_recv()
    other_lines = jnp.concatenate([other_q[p].astype(f32) for p in range(DOCS)], axis=0)
    query_all[pl.ds(pl.multiple_of(rep * 16, 16), 16), :] = stq[...].astype(bf16)
    query_all[pl.ds(pl.multiple_of((1 - rep) * 16, 16), 16), :] = other_lines.astype(bf16)

    def half_query(n):
        return query_all[:, pl.ds(pl.multiple_of((rep * (HEADS // 2) + n) * DH, DH), DH)]

    def iota(shape, dim):
        return lax.broadcasted_iota(jnp.int32, shape, dim)

    pair_copy(P_SLOTS, pair_other, pair_slots_in).wait_recv()
    slots = []
    for s in range(2):
        own_slot = states[slot_page[s] + 1][:, 0:HALF, :]
        own_slot = lax.select(first_core, own_slot, states[slot_page[s] + 1][:, HALF:, :])
        slot = own_slot * slot_valid[s] + pair_slots_in[s].astype(f32)
        slots.append(slot + expand(w1[1 + s])[None] * state0)
    lane_doc = jnp.bitwise_and(iota((DH, 32), 1), 15) // STEPS
    reads = []
    for n in range(HEADS // 2):
        read = jnp.zeros((DH, 32), f32)
        for s in range(2):
            state = slots[s][:, n * 8 : n * 8 + 8, :].reshape(DH, DH).astype(bf16)
            read = read + jnp.where(lane_doc == slot_doc[s], mm(state, half_query(n), NT), 0.0)
        reads.append(read)
    send_slots[...] = jnp.concatenate(reads, axis=1).reshape(SEQ, 8, DH)
    seq_start(S_SLOTS, src_slots, recv_slots)
    recv_slots[me] = send_slots[me]

    chain = jnp.logical_and(
        iota((16, 16), 0) // STEPS == iota((16, 16), 1) // STEPS, iota((16, 16), 0) >= iota((16, 16), 1)
    )
    fall = mm(chain.astype(f32), std[...] * LOG2E, NN, highest)
    spread_heads = (iota((HEADS, DH), 1) // 16 == iota((HEADS, DH), 0)).astype(f32)
    fall_from = mm(fall, spread_heads, NN, highest)
    lane_step = jnp.bitwise_and(iota((16, DH), 1), 15)
    diagonal = jnp.where(lane_step == iota((16, DH), 0), fall_from, 0.0)
    fall_to = mm(jnp.ones((16, 16), f32), diagonal, NN, highest)
    linked = jnp.logical_and(
        iota((16, DH), 0) // STEPS == lane_step // STEPS, iota((16, DH), 0) >= lane_step
    )
    met = jnp.concatenate(
        [
            mm(stq[:, head_cols(h)].astype(bf16), stk[:, head_cols(h)].astype(bf16), NT)
            for h in range(HEADS)
        ],
        axis=1,
    )
    met = jnp.where(linked, met * jnp.exp2(fall_from - fall_to), 0.0)
    cols = HEADS * 8
    pick = (iota((DH, cols), 0) == jnp.bitwise_and(iota((DH, cols), 1), 7) + me * 8).astype(f32)
    values = jnp.concatenate([stv[:, head_cols(h)] for h in range(HEADS)], axis=0)
    values = mm(values.astype(bf16), pick.astype(bf16), NN)
    values = jnp.where(iota((DH, cols), 0) // 16 == iota((DH, cols), 1) // 8, values, 0.0)
    decoded = mm(met, values, NN, highest)
    spread_cols = (iota((HEADS, cols), 1) // 8 == iota((HEADS, cols), 0)).astype(f32)
    shrunk = jnp.exp2(mm(fall, spread_cols, NN, highest))

    inputs["ck"].wait()
    inputs["cv"].wait()
    scale = DH**-0.5 * LOG2E
    pair_copy(P_KEYS, ck_in, other_k).wait_recv()
    pair_copy(P_VALUES, cv_in, other_v).wait_recv()
    queries = sfq[...].astype(bf16)
    query_doc = lax.broadcasted_iota(jnp.int32, (DH, ROWS), 0) // 32
    key_page = lax.broadcasted_iota(jnp.int32, (1, ROWS), 1) // PAGE
    score, here = [], []
    for base, key_block in ((dev_page, ck_ref), (chip_page + (1 - rep) * PAGES_DEV, other_k)):
        score.append(mm(queries, key_block[...], NT) * scale)
        here.append(query_doc == jnp.broadcast_to(doc_of(key_page + base), (DH, ROWS)))
    peak = jnp.maximum(
        *[
            jnp.max(jnp.where(m, s, mask_low), axis=1, keepdims=True)
            for m, s in zip(here, score)
        ]
    )
    chance = [jnp.where(m, jnp.exp2(s - peak), 0.0) for m, s in zip(here, score)]
    amount = sum(jnp.sum(x, axis=1, keepdims=True) for x in chance)
    numer = mm(chance[0].astype(bf16), cv_ref[...], NN) + mm(
        chance[1].astype(bf16), other_v[...], NN
    )
    lane = lax.broadcasted_iota(jnp.int32, (DH, DH), 1)
    both = jnp.where(lane < 64, jnp.broadcast_to(peak, (DH, DH)), jnp.broadcast_to(amount, (DH, DH)))
    send_soft[:, 0:8, :] = numer.reshape(SEQ, 8, DH)
    send_soft[:, 8:16, :] = both.reshape(SEQ, 8, DH)
    seq_start(S_SOFT, src_soft, recv_soft)
    recv_soft[me] = send_soft[me]

    seq_wait(S_STATE, src_state, recv_state)
    running = jnp.zeros((HALF, DH), f32)
    for j in range(SEQ):
        carry[j] = running
        send_back[j] = running.astype(bf16)
        rows = recv_state[j, HALF:, :].astype(f32)
        running = expand(rows[0:4] + rows[8:12]) * running + recv_state[j, 0:HALF, :].astype(f32)
    carry[SEQ] = running
    seq_start(S_BACK, src_back, recv_back)
    recv_back[me] = send_back[me]

    seq_wait(S_SLOTS, src_slots, recv_slots)
    for p in range(DOCS):
        last_page = jnp.clip(ends[p] - 1, 0, 2 * PAGES_DEV * SEQ - 1)
        chip = lax.shift_right_logical(last_page, 3)
        chip_last = jnp.bitwise_and(last_page, 7) == 7
        rank = sum(
            [flag(lax.shift_right_logical(ends[o] - 1, 3) == chip) for o in range(p)],
            jnp.int32(0),
        )
        rows = recv_state[chip][HALF:, :].astype(f32)
        w = expand(rows[4:8] + rows[12:16]) * jnp.where(rank == 0, 1.0, 0.0).astype(f32)
        final_all[p] = lax.select(chip_last, carry[chip + 1], w * carry[chip])
    tile = recv_slots[0]
    for j in range(1, SEQ):
        tile = tile + recv_slots[j]
    reads = []
    for n in range(HEADS // 2):
        state = final_all[:, n * 8 : n * 8 + 8, :].reshape(DOCS * 8, DH).astype(bf16)
        read = mm(state, half_query(n), NT)
        read = jnp.where(iota((32, 32), 0) // 8 == lane_doc[0:32], read, 0.0)
        reads.append(read[0:8] + read[8:16] + read[16:24] + read[24:32])
    pair_final[...] = tile + jnp.concatenate(reads, axis=1)
    pair_copy(P_FINAL, pair_final, pair_final_in).start()

    inputs["q"].wait()
    inside_loop(0, 1)

    pair_copy(P_FINAL, pair_final, pair_final_in).wait_recv()
    own_tile, got_tile = pair_final[...], pair_final_in[...]
    tiles = [lax.select(first_core, own_tile, got_tile), lax.select(first_core, got_tile, own_tile)]
    read_rows[...] = jnp.transpose(jnp.concatenate(tiles, axis=0))
    lines_of = [
        read_rows[pl.ds(pl.multiple_of(n * 32 + rep * 16, 16), 16), :] for n in range(HEADS // 2)
    ]
    read = jnp.concatenate([x[:, 8 * n : 8 * n + 8] for n in range(2) for x in lines_of], axis=1)
    decoded = decoded + read * shrunk
    dec_own[...] = decoded
    squares = mm(jnp.ones((8, cols), f32), decoded * decoded, NT, highest)
    send_decode[...] = jnp.zeros((1, DH), f32)
    send_decode[:, 0:16] = squares[0:1, :]
    seq_start(S_DECODE, src_decode, recv_decode)
    recv_decode[me] = send_decode[...]

    inside_loop(1, 4)

    seq_wait(S_BACK, src_back, recv_back)
    carry0 = recv_back[...].astype(f32)
    carry1 = expand(w0[0])[None] * carry0 + state0
    carry_all[:, own_rows, :] = lax.select(first_core, carry0, carry1)
    pair_carry[...] = lax.select(first_core, carry1, carry0).astype(bf16)
    pair_copy(P_CARRY, pair_carry, pair_carry_in).start()


    seq_wait(S_SOFT, src_soft, recv_soft)
    doc = me // STEPS
    step = lax.rem(me, STEPS)
    own_q = sfq[pl.ds(pl.multiple_of(me * 8, 8), 8), :]
    own_k = sfk[doc]
    own_v = sfv[doc]
    peaks = [recv_soft[s, 8:16, 0:1] for s in range(SEQ)]
    amounts = [recv_soft[s, 8:16, 64:65] for s in range(SEQ)]
    numers = [recv_soft[s, 0:8, :] for s in range(SEQ)]
    top = peaks[0]
    for x in peaks[1:]:
        top = jnp.maximum(top, x)
    own = []
    for i in range(STEPS):
        s = jnp.sum(own_q * own_k[i : i + 1, :], axis=1, keepdims=True) * scale
        own.append(lax.select(step >= i, s, jnp.full((8, 1), mask_low, f32)))
        top = jnp.maximum(top, own[-1])
    numer = jnp.zeros((8, DH), f32)
    amount = jnp.zeros((8, 1), f32)
    for s in range(SEQ):
        shrink = jnp.exp2(peaks[s] - top)
        numer = numer + numers[s] * shrink
        amount = amount + amounts[s] * shrink
    for i in range(STEPS):
        e = lax.select(step >= i, jnp.exp2(own[i] - top), jnp.zeros((8, 1), f32))
        numer = numer + e.astype(bf16).astype(f32) * own_v[i : i + 1, :]
        amount = amount + e
    send_result[...] = numer / amount
    seq_start(S_RESULT, src_result, recv_result)
    recv_result[me] = send_result[...]

    pair_copy(P_CARRY, pair_carry, pair_carry_in).wait_recv()
    carry_all[:, other_rows, :] = pair_carry_in[...].astype(f32)
    for k in range(PAGES_DEV):
        rows = page_rows(k)
        cont = goes_on(dev_page + k)
        w = before[k]
        squares = jnp.zeros((PAGE, DH), f32)
        for h in range(HEADS):
            part = slice(h * 8, h * 8 + 8)
            state = states[k, :, part, :] * cont + carry_all[:, part, :] * w[h : h + 1, :][None]
            qd = q_ref[rows, head_cols(h)]
            value = mixed[rows, head_cols(h)] + mm(qd, state.reshape(DH, DH).astype(bf16), NT)
            mixed[rows, head_cols(h)] = value
            squares = squares + value * value
        high = squares.astype(bf16)
        rest = (squares - high.astype(f32)).astype(bf16)
        ones = jnp.ones((16, DH), bf16)
        line = mm(ones, high, NT) + mm(ones, rest, NT)
        for n in range(PAGE // DH):
            send_tp[2 * k + n : 2 * k + n + 1, :] = line[0:1, head_cols(n)]


    seq_wait(S_DECODE, src_decode, recv_decode)
    decode_squares = recv_decode[0]
    for s in range(1, SEQ):
        decode_squares = decode_squares + recv_decode[s]
    send_tp[8:16, :] = jnp.broadcast_to(decode_squares, (8, DH))

    for hop in TP_HOPS:
        tp_copy(hop).start()
    sums_ref[tp] = send_tp[...]
    seq_wait(S_RESULT, src_result, recv_result)
    soft_ref[...] = recv_result[...]
    inputs["gain"].wait()
    for hop in TP_HOPS:
        source = lax.rem(tp + TP - hop, TP)
        pltpu.make_async_remote_copy(
            src_ref=send_tp, dst_ref=sums_ref.at[source],
            send_sem=tp_send.at[hop], recv_sem=tp_recv.at[hop],
            device_id=(me, source, rep), device_id_type=MESH,
        ).wait_recv()

    for which, src, dst in (
        (P_QUERY, stq_in.at[0], other_q),
        (P_KEYS, ck_in, other_k),
        (P_VALUES, cv_in, other_v),
        (P_STATE, pair_state, pair_state_in),
        (P_WEIGHT, pair_weight, pair_weight_in),
        (P_SLOTS, pair_other, pair_slots_in),
        (P_CARRY, pair_carry, pair_carry_in),
        (P_FINAL, pair_final, pair_final_in),
    ):
        pair_copy(which, src, dst).wait_send()
    seq_sent(S_STATE, src_state, recv_state)
    seq_sent(S_SLOTS, src_slots, recv_slots)
    seq_sent(S_SOFT, src_soft, recv_soft)
    seq_sent(S_BACK, src_back, recv_back)

    seq_sent(S_RESULT, src_result, recv_result)
    seq_sent(S_DECODE, src_decode, recv_decode)
    for hop in TP_HOPS:
        tp_copy(hop).wait_send()


def norm_kernel(
    mixed, sums, decoded, soft, gain_ref, out_hbm, dec_hbm, soft_hbm, block, dec_lines, dec_block, soft_block, sem
):
    me = lax.axis_index("seq")
    features = TP * HEADS * DH
    copies = []

    def send(src, dst):
        copy = pltpu.make_async_copy(src, dst, sem.at[len(copies)])
        copy.start()
        copies.append(copy)

    gain = gain_ref[...]
    total = sums[0, 0:8, :]
    for t in range(1, TP):
        total = total + sums[t, 0:8, :]
    factors = lax.rsqrt(total / features + norm_eps)
    for b in range(ROWS // DH):
        rows = slice(b * DH, (b + 1) * DH)
        factor = jnp.transpose(jnp.broadcast_to(factors[b : b + 1, :], (DH, DH)))
        for h in range(HEADS):
            block[rows, head_cols(h)] = (
                mixed[rows, head_cols(h)] * factor * gain[h : h + 1, :]
            ).astype(bf16)
        send(block.at[rows], out_hbm.at[rows])

    def iota(shape, dim):
        return lax.broadcasted_iota(jnp.int32, shape, dim)

    cols = HEADS * 8
    pick = (iota((DH, cols), 0) == jnp.bitwise_and(iota((DH, cols), 1), 7) + me * 8).astype(f32)
    gain_cols = mm(gain, pick, NN, highest)
    gain_cols = jnp.where(iota((HEADS, cols), 1) // 8 == iota((HEADS, cols), 0), gain_cols, 0.0)
    gain_cols = jnp.sum(gain_cols, axis=0, keepdims=True)
    total = mm(sums[:, 8, :], jnp.ones((TP, cols), f32), TN, highest)[0:16]
    value = decoded[...] * lax.rsqrt(total / features + norm_eps) * gain_cols
    for h in range(HEADS):
        dec_lines[pl.ds(h, 16, stride=8), :] = value[:, h * 8 : h * 8 + 8]
    dec_block[...] = dec_lines[...].reshape(DOCS, STEPS, HEADS, 8).astype(bf16)
    send(dec_block, dec_hbm.at[0])
    for p in range(DOCS):
        for h in range(HEADS):
            soft_block[p, :, head_cols(h)] = soft[pl.ds(p * 32 + h, 4, stride=8), :].astype(bf16)
    send(soft_block, soft_hbm.at[0])
    for copy in copies:
        copy.wait()


def per_device(
    light_query, light_key, light_value, log_decay, prompt_pages, norm_gain, cache_keys,
    cache_values, step_query, step_key, step_value, step_decay, soft_query, soft_key, soft_value,
):
    vm = pl.BlockSpec(memory_space=pltpu.VMEM)
    V = pltpu.VMEM
    D = pltpu.SemaphoreType.DMA
    mixed, sums, dec, soft, gain = pl.pallas_call(
        kernel,
        out_shape=(
            jax.ShapeDtypeStruct((ROWS, HEADS * DH), f32),
            jax.ShapeDtypeStruct((TP, 16, DH), f32),
            jax.ShapeDtypeStruct((16, HEADS * 8), f32),
            jax.ShapeDtypeStruct((SEQ, 8, DH), f32),
            jax.ShapeDtypeStruct((HEADS, DH), f32),
        ),
        in_specs=[pl.BlockSpec(memory_space=pltpu.HBM)] * 15,
        out_specs=(vm,) * 5,
        scratch_shapes=[
            pltpu.SMEM((DOCS,), jnp.int32),
            V((ROWS, HEADS * DH), bf16),
            V((ROWS, HEADS * DH), bf16),
            V((ROWS, HEADS * DH), bf16),
            V((HEADS, ROWS), f32),
            V((ROWS, DH), bf16),
            V((ROWS, DH), bf16),
            V((DOCS, STEPS, HEADS * DH), bf16),
            V((DOCS, STEPS, HEADS * DH), bf16),
            V((DOCS, STEPS, HEADS * DH), bf16),
            V((DOCS, STEPS, HEADS), f32),
            V((DOCS, STEPS, HEADS * DH), bf16),
            V((DOCS, STEPS, DH), bf16),
            V((DOCS, STEPS, DH), bf16),
            V((ROWS, HEADS), f32),
            V((PAGES_DEV, HEADS, PAGE), f32),
            V((PAGES_DEV + 1, SEQ, 2 * HALF, DH), f32),
            V((PAGES_DEV, HEADS, DH), f32),
            V((PAGES_DEV, HEADS, DH), f32),
            V((16, HEADS * DH), f32),
            V((16, HEADS * DH), f32),
            V((16, HEADS * DH), f32),
            V((16, HEADS), f32),
            V((DH, DH), f32),
            V((DOCS, STEPS, DH), f32),
            V((DOCS, STEPS, DH), f32),
            V((ROWS, DH), bf16),
            V((ROWS, DH), bf16),
            V((DOCS, STEPS, HEADS * DH), bf16),
            V((32, HEADS * DH), bf16),
            V((DH, 16), f32),
            V((SEQ, HALF, DH), bf16),
            V((SEQ, HALF, DH), bf16),
            V((24, DH), f32),
            V((24, DH), f32),
            V((4, SEQ, HALF, DH), bf16),
            V((2, SEQ, HALF, DH), bf16),
            V((SEQ, HALF + 16, DH), bf16),
            V((SEQ, HALF + 16, DH), bf16),
            V((SEQ, 8, DH), f32),
            V((SEQ, 8, DH), f32),
            V((SEQ, 16, DH), f32),
            V((SEQ, 16, DH), f32),
            V((SEQ + 1, HALF, DH), f32),
            V((SEQ, HALF, DH), bf16),
            V((SEQ, HALF, DH), bf16),
            V((SEQ, HALF, DH), bf16),
            V((SEQ, HALF, DH), bf16),
            V((SEQ, 2 * HALF, DH), f32),
            V((8, DH), f32),
            V((8, DH), f32),
            V((DOCS, HALF, DH), f32),
            V((ROWS, DH), f32),
            V((8, DH), f32),
            V((SEQ, 8, DH), f32),
            V((1, DH), f32),
            V((SEQ, 1, DH), f32),
            V((16, DH), f32),
            D((8,)),
            D((8,)),
            D((6, SEQ)),
            D((6, SEQ)),
            D((TP,)),
            D((TP,)),
            D((21,)),
        ],
        compiler_params=pltpu.CompilerParams(
            collective_id=0, has_side_effects=True, vmem_limit_bytes=48 * 1024 * 1024
        ),
        name="attention_block",
    )(*[pltpu.with_memory_space_constraint(x, pltpu.HBM) for x in (
        prompt_pages, light_query, light_key, light_value, log_decay.T,
        norm_gain.reshape(HEADS, DH), cache_keys, cache_values,
        step_query, step_key, step_value, step_decay, soft_query, soft_key, soft_value,
    )])
    hbm = pl.BlockSpec(memory_space=pl.ANY)
    return pl.pallas_call(
        norm_kernel,
        out_shape=(
            jax.ShapeDtypeStruct((ROWS, HEADS * DH), bf16),
            jax.ShapeDtypeStruct((1, DOCS, STEPS, HEADS, 8), bf16),
            jax.ShapeDtypeStruct((1, DOCS, STEPS, HEADS * DH), bf16),
        ),
        in_specs=[vm] * 5,
        out_specs=(hbm,) * 3,
        scratch_shapes=[
            V((ROWS, HEADS * DH), bf16),
            V((16 * HEADS, 8), f32),
            V((DOCS, STEPS, HEADS, 8), bf16),
            V((DOCS, STEPS, HEADS * DH), bf16),
            D((10,)),
        ],
        compiler_params=pltpu.CompilerParams(vmem_limit_bytes=16 * 1024 * 1024),
        name="norms",
    )(mixed, sums, dec, soft.reshape(SEQ * 8, DH), gain)


def solution(mesh):
    prompt = P(("seq", "rep"), "tp")
    sample = P("rep", None, None, "tp")
    return jax.shard_map(
        per_device,
        mesh=mesh,
        in_specs=(prompt,) * 4 + (P(), P("tp")) + (prompt,) * 2 + (sample,) * 7,
        out_specs=(prompt, P("rep", None, None, "tp", "seq"), sample),
        check_vma=False,
    )
```
